32 devices in a mesh: grp: 4 (over z), enc: 8 (over y, x, core).
Axes of the slice: x: 2, y: 2, z: 4, core: 2. Of those that a mesh axis runs over, the one named last changes fastest.
Arguments:
- history: bfloat16 [384, 128, 1024], P(('grp', 'enc')), may hold values from -6 to 6
- hist_len: int32 [384], P(('grp', 'enc')), may hold values from 0 to 2, as said below
- cand: bfloat16 [16384, 1024], P(('grp', 'enc')), may hold values from -6 to 6
- cand_owner: int32 [16384, 1], P(('grp', 'enc')), may hold values from 0 to 31; in each aligned block of 512 rows (0 to 511, 512 to 1023, ...) at most 24 rows name the same one
- cand_user: int32 [16384], P(('grp', 'enc')), may hold values from 0 to 11
- norm_gain: float32 [1024], replicated, may hold values from 0.1 to 1.9
- w_proj: bfloat16 [1024, 2048], replicated, may hold values from -0.1875 to 0.1875
Outputs:
- kv_cache: bfloat16 [384, 128, 1024], P(('grp', 'enc'))
- cand_out: bfloat16 [16384, 512], P(('grp', 'enc'))
The draws below stay inside these ranges and needn't reach their ends.
Inputs may be any that keep to these rules, and one draw needn't show every extreme that they name: `hist_len`: blocks of history of each missed user; the first user slot of every device has 2. `cand_owner`: among the 512 candidates of one device no owner device is named more than 24 times.
All inputs are finite; a program needn't handle non-finite values.
Results may differ from the reference program's by a relative error of at most 0.013.
Values may be sent and summed in bfloat16 or wider, within the bound.
No kernel may reach another device: no remote copies, remote signals or barrier semaphores. Data moves between devices by JAX's collectives and lax.ppermute only.
A program may use at most 64 MiB of HBM per device.

```python
import math
import jax
import jax.numpy as jnp
import numpy as np
from jax import lax

D = 1024
HEADS = 4
HDIM = 128
PIECE = 64
MAXP = 2
USERS = 12
CAND = 512
HD = 512
CAPC = 24
N_GRP = 4
N_ENC = 8


def draw_hist_len(key, part):
    values = jax.random.randint(key, (N_GRP * N_ENC, USERS), 0, MAXP + 1)
    values = values.at[:, 0].set(MAXP)
    return values.reshape(-1).astype(jnp.int32)


def with_ends(array, stream_key, low, high):
    longest = array.shape.index(max(array.shape))
    spots = []
    for shift in (0, 1):
        where = [jax.random.randint(jax.random.fold_in(stream_key, axis), (), 0, length) for axis, length in enumerate(array.shape)]
        where[longest] = (where[longest] + shift) % array.shape[longest]
        spots.append(tuple(where))
    return array.at[spots[0]].set(low).at[spots[1]].set(high)


def level_of(key, shape, cuts, least, largest):
    level = 1.0
    for dim, parts in cuts:
        heights = jax.random.uniform(jax.random.fold_in(jax.random.fold_in(key, 6), dim), (parts,), jnp.float32, least / len(cuts), largest / len(cuts))
        level = level * jnp.repeat(jnp.exp(heights), shape[dim] // parts).reshape((-1,) + (1,) * (len(shape) - 1 - dim))
    return level


def shared_out(own_key, own, number, rows, amount, top, limit, lean):
    ranking = jax.random.permutation(own_key, amount)
    packed, common = shares(amount, rows * top, limit, lean, True), shares(amount, rows * top, limit, lean, False)
    places = jnp.arange(amount)

    def named(sizes, turn):
        used = int((sizes > 0).sum())
        fixed = max(1, used // 4)
        shifted = fixed + (places - fixed + turn * (used - fixed)) % max(1, amount - fixed)
        return jnp.zeros((amount,), jnp.int32).at[ranking[jnp.where(places < fixed, places, shifted)]].set(jnp.asarray(sizes, jnp.int32))

    sizes = jnp.where(number % 4 == 0, named(packed, number // 4), named(common, number - number // 4 - 1))
    mixed = jax.random.permutation(jax.random.fold_in(own, 3), amount)
    giver, taker = mixed[0:amount // 2 * 2:2], mixed[1:amount // 2 * 2:2]
    room = jnp.minimum(sizes[giver] - 1, limit - sizes[taker]) // 2
    room = jnp.where((giver == ranking[0]) | (taker == ranking[0]) | (sizes[taker] == 0), 0, jnp.maximum(room, 0))
    shifted = jax.random.randint(jax.random.fold_in(own, 4), (amount // 2,), 0, 1 << 20) % (room + 1)
    sizes = sizes.at[giver].add(-shifted).at[taker].add(shifted)
    members = jnp.searchsorted(jnp.cumsum(sizes), jnp.arange(rows * top), side="right").astype(jnp.int32)
    grid = members.reshape(top, rows).T
    grid = grid[jax.random.permutation(jax.random.fold_in(own, 1), rows)]
    turn = jax.random.randint(jax.random.fold_in(own, 2), (rows, 1), 0, top)
    return jnp.take_along_axis(grid, (jnp.arange(top)[None, :] + turn) % top, axis=1)


def shares(amount, total, reach, skew, full):
    weights = [(1 << 20) // math.isqrt(rank ** skew) + 1 for rank in range(1, amount + 1)]
    largest = reach if full else min(reach, max(-(-total // amount), total * weights[0] // sum(weights)))
    least = 1 if total - largest >= amount - 1 else 0
    counts, surplus = [largest] + [least] * (amount - 1), total - largest - least * (amount - 1)
    while surplus > 0:
        free = [i for i in range(1, amount) if counts[i] < largest] or [i for i in range(1, amount) if counts[i] < reach]
        mass, budget = sum([weights[i] for i in free]), surplus
        for i in free:
            more = min(reach - counts[i], max(1, budget * weights[i] // mass), surplus)
            counts[i] = counts[i] + more
            surplus = surplus - more
    return np.array(counts)


def normal_values(own_key, extent, scale, reach, pieces=(), held_as=jnp.bfloat16):
    values = jax.random.normal(own_key, extent, jnp.float32) * scale
    if len(pieces) > 0:
        values = level_of(own_key, extent, pieces, -0.22, 0.18) * values
    return jnp.clip(values, min=-reach, max=reach).astype(held_as)


def setup_inputs(seed: int = 0) -> dict:
    key_of = jax.random.split(jax.random.key(seed), 8)
    history = normal_values(key_of[0], (N_GRP * N_ENC * USERS, MAXP * PIECE, D), 1.0, 6.0, ((0, 32),))
    hist_len = draw_hist_len(jax.random.fold_in(key_of[7], 71), 0)
    cand = normal_values(key_of[2], (N_GRP * N_ENC * CAND, D), 1.0, 6.0, ((0, 32),))
    cand_owner_keys = jax.random.split(jax.random.fold_in(key_of[3], 1), (N_GRP * N_ENC * CAND) // CAND)
    cand_owner_turns = jax.random.permutation(jax.random.fold_in(key_of[3], 3), (N_GRP * N_ENC * CAND) // CAND)
    cand_owner = jax.vmap(lambda own, number: shared_out(jax.random.fold_in(key_of[3], 2), own, number, CAND, N_GRP * N_ENC, 1, CAPC, 2))(cand_owner_keys, cand_owner_turns).reshape((N_GRP * N_ENC * CAND, 1))
    cand_user = with_ends(jax.random.randint(key_of[4], (N_GRP * N_ENC * CAND,), 0, USERS), jax.random.fold_in(key_of[4], 1), 0, USERS - 1).astype(jnp.int32)
    norm_gain = jnp.clip(1.0 + 0.18 * jax.random.normal(key_of[5], (D,), jnp.float32), 0.1, 1.9)
    w_proj = normal_values(key_of[6], (D, 4 * HD), D ** -0.5, 0.1875)
    return dict(history=history, hist_len=hist_len, cand=cand, cand_owner=cand_owner, cand_user=cand_user, norm_gain=norm_gain, w_proj=w_proj)


def norm_rows(values):
    center = values - lax.optimization_barrier(jnp.mean(values, axis=-1, keepdims=True))
    spread = lax.optimization_barrier(jnp.mean(center * center, axis=-1, keepdims=True))
    return center * lax.rsqrt(spread + 1e-05)

def encode_users(block, lengths, norm_gain, w_kv):
    normed = (norm_rows(block.astype(jnp.float32)) * norm_gain).astype(jnp.bfloat16)
    mixed = jnp.einsum('urd,de->ure', normed.astype(jnp.float32), w_kv.astype(jnp.float32))
    keyval = jax.nn.silu(mixed).astype(jnp.bfloat16)
    row_ids = jnp.arange(block.shape[1], dtype=jnp.int32)
    live = row_ids[None, :] < (lengths * PIECE)[:, None]
    return jnp.where(live[:, :, None], keyval, jnp.zeros_like(keyval))

def reference(history, hist_len, cand, cand_owner, cand_user, norm_gain, w_proj):
    width = HEADS * HDIM
    w_kv = jnp.concatenate([w_proj[:, 3 * width:], w_proj[:, width:2 * width]], axis=1)
    devices = N_GRP * N_ENC
    rows = MAXP * PIECE
    hist_blocks = history.reshape(devices, USERS, rows, D)
    len_blocks = hist_len.reshape(devices, USERS)
    kv_cache = lax.map(lambda pair: encode_users(pair[0], pair[1], norm_gain, w_kv), (hist_blocks, len_blocks))
    kv_cache = kv_cache.reshape(devices * USERS, rows, 2 * width)
    total = cand.shape[0]
    owner = cand_owner[:, 0]
    user_index = (owner * USERS + cand_user).astype(jnp.int32)
    score_scale = HDIM ** (-0.5)

    def one_block(pack):
        cand_rows, users = pack
        count = cand_rows.shape[0]
        normed = (norm_rows(cand_rows.astype(jnp.float32)) * norm_gain).astype(jnp.bfloat16)
        projected = jax.nn.silu(jnp.dot(normed, w_proj, preferred_element_type=jnp.float32)).astype(jnp.bfloat16)
        gate = projected[:, :width]
        own_v = projected[:, width:2 * width].reshape(count, HEADS, HDIM).astype(jnp.float32)
        query = projected[:, 2 * width:3 * width].reshape(count, HEADS, HDIM).astype(jnp.float32)
        own_k = projected[:, 3 * width:].reshape(count, HEADS, HDIM).astype(jnp.float32)
        stored = kv_cache[users]
        hist_k = stored[:, :, :width].reshape(count, rows, HEADS, HDIM).astype(jnp.float32)
        hist_v = stored[:, :, width:].reshape(count, rows, HEADS, HDIM).astype(jnp.float32)
        scores = jnp.einsum('nhd,nrhd->nhr', query, hist_k) * score_scale
        attention_weight = jax.nn.silu(scores).astype(jnp.bfloat16)
        self_weight = jax.nn.silu(lax.optimization_barrier(jnp.sum(query * own_k, axis=-1)) * score_scale).astype(jnp.bfloat16)
        attended = jnp.einsum('nhr,nrhd->nhd', attention_weight.astype(jnp.float32), hist_v)
        attended = attended + self_weight.astype(jnp.float32)[:, :, None] * own_v
        normed_attn = norm_rows(attended.reshape(count, width)).astype(jnp.bfloat16)
        return (normed_attn.astype(jnp.float32) * gate.astype(jnp.float32)).astype(jnp.bfloat16)
    step = min(CAND, 128)
    cand_out = lax.map(one_block, (cand.reshape(total // step, step, D), user_index.reshape(total // step, step)))
    return (kv_cache, cand_out.reshape(total, width))
```

```python
import functools

import jax
import jax.numpy as jnp
from jax import lax
from jax.experimental import pallas as pl
from jax.experimental.pallas import tpu as pltpu
from jax.sharding import PartitionSpec as P

HDIM = 128
PIECE = 64
CODE = 64
F32 = jnp.float32
BF16 = jnp.bfloat16
AXES = ("grp", "enc")
NT = (((1,), (1,)), ((), ()))


def silu(x):
    half = 0.5 * x
    return half + half * jnp.tanh(half)


def norm_rows(values):
    center = values - jnp.mean(values, axis=-1, keepdims=True)
    spread = jnp.mean(center * center, axis=-1, keepdims=True)
    return center * lax.rsqrt(spread + 1e-05)


def mm(a, b):
    return jnp.dot(a, b, preferred_element_type=F32)


def one_hot(hit):
    return jnp.where(hit, 1.0, 0.0).astype(BF16)


def iota(shape, dim):
    return lax.broadcasted_iota(jnp.int32, shape, dim)


def strict_upper(n):
    return one_hot(iota((n, n), 0) < iota((n, n), 1))


def dispatch_kernel(n_dev, cap, cand_ref, gain_ref, wq_ref, owner_ref, normed_ref, q_ref, slot_ref, out_ref):
    count = cand_ref.shape[0]
    step = 128
    gain = gain_ref[...]
    for r in range(0, count, step):
        rows = slice(r, r + step)
        normed = (norm_rows(cand_ref[rows, :].astype(F32)) * gain).astype(BF16)
        normed_ref[rows, :] = normed
        q_ref[rows, :] = silu(mm(normed, wq_ref[...])).astype(BF16)
    owner = owner_ref[...]
    named = iota((n_dev, count), 0) == owner
    before = mm(one_hot(named), strict_upper(count))
    rank = jnp.sum(jnp.where(named, before, 0.0), axis=0, keepdims=True)
    slot = owner * cap + rank.astype(jnp.int32)
    slot_ref[...] = slot
    total = n_dev * cap
    pick = one_hot(iota((total, count), 0) == slot)
    out_ref[...] = mm(pick, q_ref[...]).astype(BF16)


def encode_kernel(len_ref, hist_ref, gain_ref, wv_ref, wk_ref, out_ref):
    users, rows, dim = hist_ref.shape
    width = wk_ref.shape[1]
    first = pl.program_id(0) * users
    x = hist_ref[...].reshape(users * rows, dim).astype(F32)
    normed = (norm_rows(x) * gain_ref[...]).astype(BF16)
    keys = silu(mm(normed, wk_ref[...]))
    values = silu(mm(normed, wv_ref[...]))
    row_ids = iota((rows, width), 0)
    for u in range(users):
        live = row_ids < len_ref[first + u] * PIECE
        part = slice(u * rows, (u + 1) * rows)
        out_ref[u, :, :width] = jnp.where(live, keys[part], 0.0).astype(BF16)
        out_ref[u, :, width:] = jnp.where(live, values[part], 0.0).astype(BF16)


def own_kernel(normed_ref, q_ref, slot_ref, wu_ref, wv_ref, wk_ref, u_ref, self_ref, column_ref):
    count, width = q_ref.shape
    step = 128
    for r in range(0, count, step):
        rows = slice(r, r + step)
        normed = normed_ref[rows, :]
        u_ref[rows, :] = silu(mm(normed, wu_ref[...])).astype(BF16)
        own_v = silu(mm(normed, wv_ref[...])).astype(BF16).astype(F32)
        own_k = silu(mm(normed, wk_ref[...])).astype(BF16).astype(F32)
        prod = q_ref[rows, :].astype(F32) * own_k
        for h in range(width // HDIM):
            cols = slice(h * HDIM, (h + 1) * HDIM)
            score = jnp.sum(prod[:, cols], axis=-1, keepdims=True) * HDIM ** (-0.5)
            weight = silu(score).astype(BF16).astype(F32)
            self_ref[rows, cols] = weight * own_v[:, cols]
    spread = jnp.broadcast_to(slot_ref[...].astype(F32), (128, count))
    column_ref[...] = spread.T.astype(jnp.int32)


def users_kernel(cap, me_ref, code_ref, out_ref):
    n_dev, count = code_ref.shape
    total = n_dev * cap
    user = code_ref[...] - me_ref[0] * CODE
    mine = (user >= 0) & (user < CODE)
    rank = mm(one_hot(mine), strict_upper(count)).astype(jnp.int32)
    rank = jnp.where(mine, rank, -1)
    user = user.astype(F32)
    lane = iota((n_dev, 128), 1)
    table = jnp.zeros((n_dev, 128), F32)
    for k in range(cap):
        found = jnp.sum(jnp.where(rank == k, user, 0.0), axis=1, keepdims=True)
        table = jnp.where(lane == k, found, table)
    source = iota((total, n_dev), 0) - iota((total, n_dev), 1) * cap
    spread = mm(one_hot((source >= 0) & (source < cap)), table.astype(BF16))
    place = lax.rem(iota((total, 128), 0), cap)
    own = jnp.where(place == iota((total, 128), 1), spread, 0.0)
    out_ref[...] = jnp.broadcast_to(jnp.sum(own, axis=1, keepdims=True), (total, 128))


def attend_kernel(uid_ref, q_ref, k_ref, v_ref, out_ref, mask_ref, odd_ref):
    rows = k_ref.shape[0]
    pairs = rows // 256

    @pl.when(pl.program_id(0) == 0)
    def _():
        uid = uid_ref[...]
        odd = jnp.zeros_like(uid)
        for p in range(pairs):
            low, high = uid == 2.0 * p, uid == 2.0 * p + 1.0
            mask_ref[:, p * 128:(p + 1) * 128] = one_hot(low | high)
            odd = jnp.where(high, 1.0, odd)
        odd_ref[...] = odd

    odd = odd_ref[...] > 0.5

    def spread(x):
        return jnp.concatenate([x * mask_ref[:, p * 128:(p + 1) * 128] for p in range(pairs)], axis=1)

    def chosen(x):
        return jnp.where(odd, x[:, 128:], x[:, :128])

    keys = jnp.concatenate([k_ref[p * 256:(p + 1) * 256, :] for p in range(pairs)], axis=1)
    scores = chosen(lax.dot_general(spread(q_ref[...]), keys, NT, preferred_element_type=F32))
    weight = silu(scores * HDIM ** (-0.5)).astype(BF16)
    values = jnp.concatenate(
        [
            jnp.concatenate([v_ref[p * 256:p * 256 + 128, :], v_ref[p * 256 + 128:(p + 1) * 256, :]], axis=1)
            for p in range(pairs)
        ],
        axis=0,
    )
    out_ref[...] = chosen(mm(spread(weight), values)).astype(BF16)


def answer_kernel(back_ref, column_ref, self_ref, u_ref, out_ref):
    total = back_ref.shape[0]
    count = u_ref.shape[0]
    step = 128
    for r in range(0, count, step):
        rows = slice(r, r + step)
        slot = column_ref[rows, 0:1]
        pick = one_hot(iota((step, total), 1) == slot)
        attended = mm(pick, back_ref[...]) + self_ref[rows, :]
        normed = norm_rows(attended).astype(BF16).astype(F32)
        out_ref[rows, :] = (normed * u_ref[rows, :].astype(F32)).astype(BF16)


def params(**more):
    return pltpu.CompilerParams(vmem_limit_bytes=40 * 1024 * 1024, **more)


def whole(shape):
    return pl.BlockSpec(shape, lambda *_: (0,) * len(shape))


def column(shape, index):
    return pl.BlockSpec(shape, lambda *_: (0, index))


def cost(flops, size):
    return pl.CostEstimate(flops=flops, bytes_accessed=size, transcendentals=0)


def body(history, hist_len, cand, cand_owner, cand_user, norm_gain, w_proj):
    users, rows, dim = history.shape
    width = w_proj.shape[1] // 4
    heads = width // HDIM
    count = cand.shape[0]
    n_enc = lax.axis_size("enc")
    n_dev = lax.axis_size("grp") * n_enc
    cap = max(2, 3 * count // (2 * n_dev))
    total = n_dev * cap
    gain = norm_gain.reshape(1, dim)
    owner = cand_owner.reshape(1, count)
    me = (lax.axis_index("grp") * n_enc + lax.axis_index("enc")).astype(jnp.int32).reshape(1)
    shape = jax.ShapeDtypeStruct

    codes = lax.all_gather(cand_owner[:, 0] * CODE + cand_user, AXES, axis=0, tiled=False)

    normed, q, slot, outgoing = pl.pallas_call(
        functools.partial(dispatch_kernel, n_dev, cap),
        grid=(1,),
        in_specs=[whole((count, dim)), whole((1, dim)), column((dim, width), 2), whole((1, count))],
        out_specs=[whole((count, dim)), whole((count, width)), whole((1, count)), whole((total, width))],
        out_shape=[
            shape((count, dim), BF16),
            shape((count, width), BF16),
            shape((1, count), jnp.int32),
            shape((total, width), BF16),
        ],
        compiler_params=params(),
        cost_estimate=cost(2 * count * width * (dim + total), 4 << 20),
        name="dispatch",
    )(cand, gain, w_proj, owner)

    arrived = lax.all_to_all(
        outgoing.reshape(n_dev, cap, width), AXES, split_axis=0, concat_axis=0, tiled=True
    ).reshape(total, width)

    step = 3
    kv_cache = pl.pallas_call(
        encode_kernel,
        grid=(users // step,),
        in_specs=[
            pl.BlockSpec(memory_space=pltpu.SMEM),
            pl.BlockSpec((step, rows, dim), lambda i: (i, 0, 0)),
            whole((1, dim)),
            column((dim, width), 1),
            column((dim, width), 3),
        ],
        out_specs=pl.BlockSpec((step, rows, 2 * width), lambda i: (i, 0, 0)),
        out_shape=shape((users, rows, 2 * width), BF16),
        compiler_params=params(),
        cost_estimate=cost(2 * users * rows * dim * 2 * width, 8 << 20),
        name="encode",
    )(hist_len, history, gain, w_proj, w_proj)

    gate, own, slots = pl.pallas_call(
        own_kernel,
        grid=(1,),
        in_specs=[
            whole((count, dim)),
            whole((count, width)),
            whole((1, count)),
            column((dim, width), 0),
            column((dim, width), 1),
            column((dim, width), 3),
        ],
        out_specs=[whole((count, width)), whole((count, width)), whole((count, 128))],
        out_shape=[shape((count, width), BF16), shape((count, width), F32), shape((count, 128), jnp.int32)],
        compiler_params=params(),
        cost_estimate=cost(6 * count * dim * width, 6 << 20),
        name="own",
    )(normed, q, slot, w_proj, w_proj, w_proj)

    uid = pl.pallas_call(
        functools.partial(users_kernel, cap),
        grid=(1,),
        in_specs=[pl.BlockSpec(memory_space=pltpu.SMEM), whole((n_dev, count))],
        out_specs=whole((total, 128)),
        out_shape=shape((total, 128), F32),
        compiler_params=params(),
        cost_estimate=cost(1 << 28, 1 << 19),
        name="users",
    )(me, codes)

    flat = kv_cache.reshape(users * rows, 2 * width)
    attended = pl.pallas_call(
        attend_kernel,
        grid=(heads,),
        in_specs=[
            whole((total, 128)),
            pl.BlockSpec((total, HDIM), lambda h: (0, h)),
            pl.BlockSpec((users * rows, HDIM), lambda h: (0, h)),
            pl.BlockSpec((users * rows, HDIM), lambda h: (0, heads + h)),
        ],
        out_specs=pl.BlockSpec((total, HDIM), lambda h: (0, h)),
        out_shape=shape((total, width), BF16),
        scratch_shapes=[pltpu.VMEM((total, users * 64), BF16), pltpu.VMEM((total, 128), F32)],
        compiler_params=params(),
        cost_estimate=cost(2 * total * rows * users * width * 2, 6 << 20),
        name="attend",
    )(uid, arrived, flat, flat)

    back = lax.all_to_all(
        attended.reshape(n_dev, cap, width), AXES, split_axis=0, concat_axis=0, tiled=True
    ).reshape(total, width)

    cand_out = pl.pallas_call(
        answer_kernel,
        grid=(1,),
        in_specs=[
            whole((total, width)),
            whole((count, 128)),
            whole((count, width)),
            whole((count, width)),
        ],
        out_specs=whole((count, width)),
        out_shape=shape((count, width), BF16),
        compiler_params=params(),
        cost_estimate=cost(2 * count * total * width, 4 << 20),
        name="answer",
    )(back, slots, own, gate)
    return (kv_cache, cand_out)


def solution(mesh):
    placed = (
        P(AXES, None, None),
        P(AXES),
        P(AXES, None),
        P(AXES, None),
        P(AXES),
        P(),
        P(),
    )
    return jax.shard_map(
        body,
        mesh=mesh,
        in_specs=placed,
        out_specs=(P(AXES, None, None), P(AXES, None)),
        check_vma=False,
    )
```

```python
import functools

import jax
import jax.numpy as jnp
from jax import lax
from jax.experimental import pallas as pl
from jax.experimental.pallas import tpu as pltpu
from jax.sharding import PartitionSpec as P

HDIM = 128
PIECE = 64
F32 = jnp.float32
BF16 = jnp.bfloat16
AXES = ("grp", "enc")
NT = (((1,), (1,)), ((), ()))


def silu(x):
    half = 0.5 * x
    return half + half * jnp.tanh(half)


def norm_rows(values):
    center = values - jnp.mean(values, axis=-1, keepdims=True)
    spread = jnp.mean(center * center, axis=-1, keepdims=True)
    return center * lax.rsqrt(spread + 1e-05)


def mm(a, b):
    return jnp.dot(a, b, preferred_element_type=F32)


def one_hot(hit):
    return jnp.where(hit, 1.0, 0.0).astype(BF16)


def iota(shape, dim):
    return lax.broadcasted_iota(jnp.int32, shape, dim)


def ranks(owner, n_dev):
    count = owner.shape[1]
    named = iota((n_dev, count), 0) == owner
    before = mm(one_hot(named), one_hot(iota((count, count), 0) < iota((count, count), 1)))
    return named, jnp.sum(jnp.where(named, before, 0.0), axis=0, keepdims=True).astype(jnp.int32)


def dispatch_kernel(cap, cand_ref, gain_ref, wq_ref, owner_ref, user_ref, out_ref, q_ref, pick_ref):
    n_dev = out_ref.shape[0]
    step, width = cand_ref.shape[0], wq_ref.shape[1]
    count = owner_ref.shape[1]
    heads = width // HDIM
    i = pl.program_id(0)

    @pl.when(i == 0)
    def _():
        owner = owner_ref[...]
        named, rank = ranks(owner, n_dev)
        pick_ref[...] = one_hot(iota((n_dev * cap, count), 0) == owner * cap + rank)
        users = jnp.where(named, user_ref[...].astype(F32), 0.0).astype(BF16)
        place = one_hot(iota((128, count), 0) == rank)
        table = lax.dot_general(users, place, NT, preferred_element_type=F32)
        out_ref[:, heads * cap :, :] = jnp.broadcast_to(table[:, None, :], (n_dev, 8, 128)).astype(BF16)

    normed = (norm_rows(cand_ref[...].astype(F32)) * gain_ref[...]).astype(BF16)
    q_ref[pl.ds(pl.multiple_of(i * step, step), step), :] = silu(mm(normed, wq_ref[...])).astype(BF16)

    @pl.when(i == pl.num_programs(0) - 1)
    def _():
        sent = mm(pick_ref[...], q_ref[...])
        for h in range(heads):
            part = sent[:, h * HDIM : (h + 1) * HDIM].reshape(n_dev, cap, HDIM)
            out_ref[:, h * cap : (h + 1) * cap, :] = part.astype(BF16)


def encode_kernel(len_ref, hist_ref, gain_ref, wv_ref, wk_ref, out_ref, key_ref, value_ref):
    users, rows, dim = hist_ref.shape
    width = wk_ref.shape[1]
    first = pl.program_id(0) * users
    x = hist_ref[...].reshape(users * rows, dim).astype(F32)
    normed = (norm_rows(x) * gain_ref[...]).astype(BF16)
    keys = silu(mm(normed, wk_ref[...]))
    values = silu(mm(normed, wv_ref[...]))
    row_ids = iota((rows, width), 0)
    for u in range(users):
        live = row_ids < len_ref[first + u] * PIECE
        part = slice(u * rows, (u + 1) * rows)
        side = slice((u % 2) * rows, (u % 2 + 1) * rows)
        pair = slice((u // 2) * HDIM, (u // 2 + 1) * HDIM)
        key = jnp.where(live, keys[part], 0.0)
        value = jnp.where(live, values[part], 0.0).astype(BF16)
        out_ref[u, :, :width] = key.astype(BF16)
        out_ref[u, :, width:] = value
        for h in range(width // HDIM):
            cols = slice(h * HDIM, (h + 1) * HDIM)
            key_ref[h, pair, side] = key[:, cols].T.astype(BF16)
            value_ref[h, pair, side] = value[:, cols]


def own_kernel(n_dev, cap, cand_ref, gain_ref, w_ref, owner_ref, u_ref, self_ref, column_ref):
    step, width = u_ref.shape
    i = pl.program_id(0)
    normed = (norm_rows(cand_ref[...].astype(F32)) * gain_ref[...]).astype(BF16)

    def projected(part):
        return silu(mm(normed, w_ref[:, part * width : (part + 1) * width])).astype(BF16)

    u_ref[...] = projected(0)
    own_v = projected(1).astype(F32)
    prod = projected(2).astype(F32) * projected(3).astype(F32)
    for h in range(width // HDIM):
        cols = slice(h * HDIM, (h + 1) * HDIM)
        score = jnp.sum(prod[:, cols], axis=-1, keepdims=True) * HDIM ** (-0.5)
        self_ref[:, cols] = silu(score).astype(BF16).astype(F32) * own_v[:, cols]

    @pl.when(i == 0)
    def _():
        owner = owner_ref[...]
        _, rank = ranks(owner, n_dev)
        slot = (owner * cap + rank).astype(F32)
        column_ref[...] = jnp.broadcast_to(slot, (128, slot.shape[1])).T.astype(jnp.int32)


def attend_kernel(cap, table_ref, q_ref, k_ref, v_ref, out_ref, mask_ref, odd_ref):
    n_dev = q_ref.shape[0]
    total = n_dev * cap
    pairs = k_ref.shape[1] // HDIM

    @pl.when(pl.program_id(0) == 0)
    def _():
        table = table_ref[:, 0:1, :].astype(F32)
        full = (n_dev, cap, 128)
        uid = jnp.where(iota(full, 1) == iota(full, 2), jnp.broadcast_to(table, full), 0.0)
        uid = jnp.broadcast_to(jnp.sum(uid, axis=2, keepdims=True), full).reshape(total, 128)
        pair = jnp.floor(uid * 0.5)
        odd_ref[...] = uid - 2.0 * pair
        for p in range(pairs):
            mask_ref[:, p * 128 : (p + 1) * 128] = one_hot(pair == 1.0 * p)

    odd = odd_ref[...] > 0.5

    def spread(x):
        return jnp.concatenate([x * mask_ref[:, p * 128 : (p + 1) * 128] for p in range(pairs)], axis=1)

    def chosen(x):
        return jnp.where(odd, x[:, 128:], x[:, :128])

    for h in range(k_ref.shape[0]):
        rows = slice(h * cap, (h + 1) * cap)
        query = q_ref[:, rows, :].astype(F32).reshape(total, HDIM).astype(BF16)
        scores = chosen(mm(spread(query), k_ref[h]))
        weight = silu(scores * HDIM ** (-0.5)).astype(BF16)
        attended = chosen(mm(spread(weight), v_ref[h]))
        out_ref[:, rows, :] = attended.reshape(n_dev, cap, HDIM).astype(BF16)


def answer_kernel(back_ref, column_ref, self_ref, u_ref, out_ref):
    step, width = u_ref.shape
    n_dev = back_ref.shape[0]
    heads = width // HDIM
    cap = back_ref.shape[1] // heads
    total = n_dev * cap
    pick = one_hot(iota((step, total), 1) == column_ref[:, 0:1])
    back = [
        back_ref[:, h * cap : (h + 1) * cap, :].astype(F32).reshape(total, HDIM).astype(BF16) for h in range(heads)
    ]
    attended = mm(pick, jnp.concatenate(back, axis=1)) + self_ref[...]
    normed = norm_rows(attended).astype(BF16).astype(F32)
    out_ref[...] = (normed * u_ref[...].astype(F32)).astype(BF16)


def params():
    return pltpu.CompilerParams(vmem_limit_bytes=58 * 1024 * 1024)


def whole(shape):
    return pl.BlockSpec(shape, lambda *_: (0,) * len(shape))


def column(shape, index):
    return pl.BlockSpec(shape, lambda *_: (0, index))


def cost(flops, size):
    return pl.CostEstimate(flops=flops, bytes_accessed=size, transcendentals=0)


def exchange(slots):
    return lax.all_to_all(slots, AXES, split_axis=0, concat_axis=0, tiled=True)


def body(history, hist_len, cand, cand_owner, cand_user, norm_gain, w_proj):
    users, rows, dim = history.shape
    width = w_proj.shape[1] // 4
    heads = width // HDIM
    count = cand.shape[0]
    n_dev = lax.axis_size("grp") * lax.axis_size("enc")
    cap = -(-max(2, 3 * count // (2 * n_dev)) // 8) * 8
    total = n_dev * cap
    gain = norm_gain.reshape(1, dim)
    owner = cand_owner.reshape(1, count)
    user = cand_user.reshape(1, count)
    shape = jax.ShapeDtypeStruct

    step = count // 2
    outgoing = pl.pallas_call(
        functools.partial(dispatch_kernel, cap),
        grid=(count // step,),
        in_specs=[
            pl.BlockSpec((step, dim), lambda i: (i, 0)),
            whole((1, dim)),
            column((dim, width), 2),
            whole((1, count)),
            whole((1, count)),
        ],
        out_specs=whole((n_dev, heads * cap + 8, HDIM)),
        out_shape=shape((n_dev, heads * cap + 8, HDIM), BF16),
        scratch_shapes=[pltpu.VMEM((count, width), BF16), pltpu.VMEM((total, count), BF16)],
        compiler_params=params(),
        cost_estimate=cost(2 * count * width * (dim + total), 4 << 20),
        name="dispatch",
    )(cand, gain, w_proj, owner, user)

    arrived = exchange(outgoing)

    span = 4
    kv_cache, keys, values = pl.pallas_call(
        encode_kernel,
        grid=(users // span,),
        in_specs=[
            pl.BlockSpec(memory_space=pltpu.SMEM),
            pl.BlockSpec((span, rows, dim), lambda i: (i, 0, 0)),
            whole((1, dim)),
            column((dim, width), 1),
            column((dim, width), 3),
        ],
        out_specs=[
            pl.BlockSpec((span, rows, 2 * width), lambda i: (i, 0, 0)),
            pl.BlockSpec((heads, span * HDIM // 2, 2 * rows), lambda i: (0, i, 0)),
            pl.BlockSpec((heads, span * rows // 2, 2 * HDIM), lambda i: (0, i, 0)),
        ],
        out_shape=[
            shape((users, rows, 2 * width), BF16),
            shape((heads, users * HDIM // 2, 2 * rows), BF16),
            shape((heads, users * rows // 2, 2 * HDIM), BF16),
        ],
        compiler_params=params(),
        cost_estimate=cost(2 * users * rows * dim * 2 * width, 12 << 20),
        name="encode",
    )(hist_len, history, gain, w_proj, w_proj)

    gate, own, slots = pl.pallas_call(
        functools.partial(own_kernel, n_dev, cap),
        grid=(count // step,),
        in_specs=[
            pl.BlockSpec((step, dim), lambda i: (i, 0)),
            whole((1, dim)),
            whole((dim, 4 * width)),
            whole((1, count)),
        ],
        out_specs=[
            pl.BlockSpec((step, width), lambda i: (i, 0)),
            pl.BlockSpec((step, width), lambda i: (i, 0)),
            whole((count, 128)),
        ],
        out_shape=[shape((count, width), BF16), shape((count, width), F32), shape((count, 128), jnp.int32)],
        compiler_params=params(),
        cost_estimate=cost(8 * count * dim * width, 6 << 20),
        name="own",
    )(cand, gain, w_proj, owner)

    each = 2
    attended = pl.pallas_call(
        functools.partial(attend_kernel, cap),
        grid=(heads // each,),
        in_specs=[
            pl.BlockSpec((n_dev, 8, HDIM), lambda h: (0, heads * cap // 8, 0)),
            pl.BlockSpec((n_dev, each * cap, HDIM), lambda h: (0, h, 0)),
            pl.BlockSpec((each, users * HDIM // 2, 2 * rows), lambda h: (h, 0, 0)),
            pl.BlockSpec((each, users * rows // 2, 2 * HDIM), lambda h: (h, 0, 0)),
        ],
        out_specs=pl.BlockSpec((n_dev, each * cap, HDIM), lambda h: (0, h, 0)),
        out_shape=shape((n_dev, heads * cap, HDIM), BF16),
        scratch_shapes=[pltpu.VMEM((total, users * 64), BF16), pltpu.VMEM((total, 128), F32)],
        compiler_params=params(),
        cost_estimate=cost(2 * total * rows * users * width * 2, 6 << 20),
        name="attend",
    )(arrived, arrived, keys, values)

    back = exchange(attended)

    cand_out = pl.pallas_call(
        answer_kernel,
        grid=(count // step,),
        in_specs=[
            whole((n_dev, heads * cap, HDIM)),
            pl.BlockSpec((step, 128), lambda i: (i, 0)),
            pl.BlockSpec((step, width), lambda i: (i, 0)),
            pl.BlockSpec((step, width), lambda i: (i, 0)),
        ],
        out_specs=pl.BlockSpec((step, width), lambda i: (i, 0)),
        out_shape=shape((count, width), BF16),
        compiler_params=params(),
        cost_estimate=cost(2 * count * total * width, 4 << 20),
        name="answer",
    )(back, slots, own, gate)
    return (kv_cache, cand_out)


def solution(mesh):
    placed = (
        P(AXES, None, None),
        P(AXES),
        P(AXES, None),
        P(AXES, None),
        P(AXES),
        P(),
        P(),
    )
    return jax.shard_map(
        body,
        mesh=mesh,
        in_specs=placed,
        out_specs=(P(AXES, None, None), P(AXES, None)),
        check_vma=False,
    )
```

```python
import functools

import jax
import jax.numpy as jnp
from jax import lax
from jax.experimental import pallas as pl
from jax.experimental.pallas import tpu as pltpu
from jax.sharding import PartitionSpec as P

HDIM = 128
PIECE = 64
F32 = jnp.float32
BF16 = jnp.bfloat16
AXES = ("grp", "enc")
NT = (((1,), (1,)), ((), ()))


def silu(x):
    half = 0.5 * x
    return half + half * jnp.tanh(half)


def norm_rows(values):
    center = values - jnp.mean(values, axis=-1, keepdims=True)
    spread = jnp.mean(center * center, axis=-1, keepdims=True)
    return center * lax.rsqrt(spread + 1e-05)


def mm(a, b):
    return jnp.dot(a, b, preferred_element_type=F32)


def one_hot(hit):
    return jnp.where(hit, 1.0, 0.0).astype(BF16)


def iota(shape, dim):
    return lax.broadcasted_iota(jnp.int32, shape, dim)


def ranks(place, n_dev):
    count = place.shape[1]
    named = iota((n_dev, count), 0) == place
    before = mm(one_hot(named), one_hot(iota((count, count), 0) < iota((count, count), 1)))
    return named, jnp.sum(jnp.where(named, before, 0.0), axis=0, keepdims=True).astype(jnp.int32)


def place_of(owner, n_grp, n_enc):
    return lax.rem(owner, n_enc) * n_grp + lax.div(owner, n_enc)


def dispatch_kernel(
    n_grp, n_enc, cap, cand_hbm, gain_hbm, w_hbm, owner_hbm, user_hbm, out_hbm,
    cand_ref, gain_ref, wq_ref, owner_ref, user_ref, out_ref, q_ref, pick_ref, small_sem, cand_sem, w_sem, out_sem,
):
    n_dev = out_ref.shape[0]
    count, width = q_ref.shape
    heads = width // HDIM
    parts = cand_sem.shape[0]
    step = count // parts

    def block(ref, i):
        return ref.at[pl.ds(i * step, step), :]

    small = [
        pltpu.make_async_copy(owner_hbm, owner_ref, small_sem.at[0]),
        pltpu.make_async_copy(user_hbm, user_ref, small_sem.at[1]),
        pltpu.make_async_copy(gain_hbm, gain_ref, small_sem.at[2]),
    ]
    loads = [pltpu.make_async_copy(block(cand_hbm, i), block(cand_ref, i), cand_sem.at[i]) for i in range(parts)]
    weights = pltpu.make_async_copy(w_hbm.at[:, pl.ds(2 * width, width)], wq_ref, w_sem.at[0])
    for copy in small:
        copy.start()
    loads[0].start()
    weights.start()
    for copy in loads[1:]:
        copy.start()
    for copy in small:
        copy.wait()
    place = place_of(owner_ref[...], n_grp, n_enc)
    named, rank = ranks(place, n_dev)
    pick_ref[...] = one_hot(iota((n_dev * cap, count), 0) == place * cap + rank)
    users = jnp.where(named, user_ref[...].astype(F32), 0.0).astype(BF16)
    table = lax.dot_general(users, one_hot(iota((128, count), 0) == rank), NT, preferred_element_type=F32)
    out_ref[:, heads * cap :, :] = jnp.broadcast_to(table[:, None, :], (n_dev, 8, 128)).astype(BF16)
    gain = gain_ref[...]
    for i in range(parts):
        rows = slice(i * step, (i + 1) * step)
        loads[i].wait()
        normed = (norm_rows(cand_ref[rows, :].astype(F32)) * gain).astype(BF16)
        if i == 0:
            weights.wait()
        q_ref[rows, :] = silu(mm(normed, wq_ref[...])).astype(BF16)
    stores = []
    groups = out_sem.shape[0]
    span = n_dev // groups
    for g in range(groups):
        devs = slice(g * span, (g + 1) * span)
        sent = mm(pick_ref[g * span * cap : (g + 1) * span * cap, :], q_ref[...])
        for h in range(heads):
            part = sent[:, h * HDIM : (h + 1) * HDIM].reshape(span, cap, HDIM)
            out_ref[devs, h * cap : (h + 1) * cap, :] = part.astype(BF16)
        at = pl.ds(g * span, span)
        stores.append(pltpu.make_async_copy(out_ref.at[at], out_hbm.at[at], out_sem.at[g]))
        stores[-1].start()
    for copy in stores:
        copy.wait()


def encode_kernel(len_ref, hist_ref, gain_ref, wv_ref, wk_ref, out_ref, key_ref, value_ref):
    users, rows, dim = hist_ref.shape
    width = wk_ref.shape[1]
    first = pl.program_id(0) * users
    x = hist_ref[...].reshape(users * rows, dim).astype(F32)
    normed = (norm_rows(x) * gain_ref[...]).astype(BF16)
    keys = silu(mm(normed, wk_ref[...]))
    values = silu(mm(normed, wv_ref[...]))
    row_ids = iota((rows, width), 0)
    for u in range(users):
        live = row_ids < len_ref[first + u] * PIECE
        part = slice(u * rows, (u + 1) * rows)
        side = slice((u % 2) * rows, (u % 2 + 1) * rows)
        pair = slice((u // 2) * HDIM, (u // 2 + 1) * HDIM)
        key = jnp.where(live, keys[part], 0.0)
        value = jnp.where(live, values[part], 0.0).astype(BF16)
        out_ref[u, :, :width] = key.astype(BF16)
        out_ref[u, :, width:] = value
        for h in range(width // HDIM):
            cols = slice(h * HDIM, (h + 1) * HDIM)
            key_ref[h, pair, side] = key[:, cols].T.astype(BF16)
            value_ref[h, pair, side] = value[:, cols]


def own_kernel(n_grp, n_enc, cap, cand_ref, gain_ref, w_ref, owner_ref, u_ref, v_ref, aux_ref, slot_ref):
    step, width = u_ref.shape
    heads = width // HDIM
    i = pl.program_id(0)

    @pl.when(i == 0)
    def _():
        place = place_of(owner_ref[...], n_grp, n_enc)
        _, rank = ranks(place, n_grp * n_enc)
        slot = (place * cap + rank).astype(F32)
        slot_ref[...] = jnp.broadcast_to(slot, (128, slot.shape[1])).T

    normed = (norm_rows(cand_ref[...].astype(F32)) * gain_ref[...]).astype(BF16)

    def projected(part):
        return silu(mm(normed, w_ref[:, part * width : (part + 1) * width])).astype(BF16)

    u_ref[...] = projected(0)
    v_ref[...] = projected(1)
    prod = projected(2).astype(F32) * projected(3).astype(F32)
    lane = iota((step, 128), 1)
    aux = slot_ref[pl.ds(pl.multiple_of(i * step, step), step), :]
    for h in range(heads):
        score = jnp.sum(prod[:, h * HDIM : (h + 1) * HDIM], axis=-1, keepdims=True) * HDIM ** (-0.5)
        aux = jnp.where(lane == h, silu(score).astype(BF16).astype(F32), aux)
    aux_ref[...] = aux


def attend_kernel(
    cap, arrived_ref, k_hbm, v_hbm, out_hbm, k_ref, v_ref, out_ref, mask_ref, odd_ref, k_sem, v_sem, out_sem
):
    n_dev = arrived_ref.shape[0]
    heads = k_ref.shape[0]
    total = n_dev * cap
    pairs = k_ref.shape[1] // HDIM
    keys = [pltpu.make_async_copy(k_hbm.at[h], k_ref.at[h], k_sem.at[h]) for h in range(heads)]
    values = [pltpu.make_async_copy(v_hbm.at[h], v_ref.at[h], v_sem.at[h]) for h in range(heads)]
    for h in range(heads):
        keys[h].start()
        values[h].start()

    table = arrived_ref[:, heads * cap : heads * cap + 8, :].astype(F32)[:, 0:1, :]
    full = (n_dev, cap, 128)
    uid = jnp.where(iota(full, 1) == iota(full, 2), jnp.broadcast_to(table, full), 0.0)
    uid = jnp.broadcast_to(jnp.sum(uid, axis=2, keepdims=True), full).reshape(total, 128)
    pair = jnp.floor(uid * 0.5)
    odd_ref[...] = uid - 2.0 * pair
    for p in range(pairs):
        mask_ref[:, p * 128 : (p + 1) * 128] = one_hot(pair == 1.0 * p)

    def spread(x):
        return jnp.concatenate([x * mask_ref[:, p * 128 : (p + 1) * 128] for p in range(pairs)], axis=1)

    def chosen(x):
        return jnp.where(odd_ref[...] > 0.5, x[:, 128:], x[:, :128])

    def scores(h):
        query = arrived_ref[:, h * cap : (h + 1) * cap, :].astype(F32).reshape(total, HDIM).astype(BF16)
        keys[h].wait()
        return mm(spread(query), k_ref[h])

    stores = []
    score = scores(0)
    for h in range(heads):
        later = scores(h + 1) if h + 1 < heads else None
        weight = silu(chosen(score) * HDIM ** (-0.5)).astype(BF16)
        values[h].wait()
        attended = chosen(mm(spread(weight), v_ref[h]))
        out_ref[:, h * cap : (h + 1) * cap, :] = attended.reshape(n_dev, cap, HDIM).astype(BF16)
        at = (slice(None), pl.ds(h * cap, cap), slice(None))
        stores.append(pltpu.make_async_copy(out_ref.at[at], out_hbm.at[at], out_sem.at[h]))
        stores[-1].start()
        score = later
    for copy in stores:
        copy.wait()


def answer_kernel(back_ref, u_ref, v_ref, aux_ref, out_ref):
    count, width = u_ref.shape
    n_dev = back_ref.shape[0]
    heads = width // HDIM
    cap = back_ref.shape[1] // heads
    total = n_dev * cap
    back = [
        back_ref[:, h * cap : (h + 1) * cap, :].astype(F32).reshape(total, HDIM).astype(BF16) for h in range(heads)
    ]
    back = jnp.concatenate(back, axis=1)
    step = min(count, 128)
    for r in range(0, count, step):
        rows = slice(r, r + step)
        aux = aux_ref[rows, :]
        pick = one_hot(iota((step, total), 1) == aux[:, heads : heads + 1].astype(jnp.int32))
        own_v = v_ref[rows, :].astype(F32)
        own = [own_v[:, h * HDIM : (h + 1) * HDIM] * aux[:, h : h + 1] for h in range(heads)]
        normed = norm_rows(mm(pick, back) + jnp.concatenate(own, axis=1)).astype(BF16).astype(F32)
        out_ref[rows, :] = (normed * u_ref[rows, :].astype(F32)).astype(BF16)


def params():
    return pltpu.CompilerParams(vmem_limit_bytes=36 * 1024 * 1024)


def whole(shape):
    return pl.BlockSpec(shape, lambda *_: (0,) * len(shape))


def column(shape, index):
    return pl.BlockSpec(shape, lambda *_: (0, index))


def cost(flops, size):
    return pl.CostEstimate(flops=flops, bytes_accessed=size, transcendentals=0)


def in_hbm(x):
    return pltpu.with_memory_space_constraint(x, pltpu.HBM)


def in_vmem(x):
    return pltpu.with_memory_space_constraint(x, pltpu.VMEM)


def exchange(slots):
    return lax.all_to_all(slots, ("enc", "grp"), split_axis=0, concat_axis=0, tiled=True)


def body(history, hist_len, cand, cand_owner, cand_user, norm_gain, w_proj):
    users, rows, dim = history.shape
    width = w_proj.shape[1] // 4
    heads = width // HDIM
    count = cand.shape[0]
    n_grp, n_enc = lax.axis_size("grp"), lax.axis_size("enc")
    n_dev = n_grp * n_enc
    cap = -(-max(2, 3 * count // (2 * n_dev)) // 8) * 8
    total = n_dev * cap
    parts = 4
    shape = jax.ShapeDtypeStruct
    anywhere = pl.BlockSpec(memory_space=pl.ANY)
    dma = pltpu.SemaphoreType.DMA

    history, cand, w_proj = in_hbm(history), in_hbm(cand), in_hbm(w_proj)
    gain = in_hbm(norm_gain.reshape(1, dim))
    owner = in_hbm(cand_owner.reshape(1, count))
    user = in_hbm(cand_user.reshape(1, count))

    outgoing = pl.pallas_call(
        functools.partial(dispatch_kernel, n_grp, n_enc, cap),
        in_specs=[anywhere] * 5,
        out_specs=anywhere,
        out_shape=pltpu.HBM((n_dev, heads * cap + 8, HDIM), BF16),
        scratch_shapes=[
            pltpu.VMEM((count, dim), BF16),
            pltpu.VMEM((1, dim), F32),
            pltpu.VMEM((dim, width), BF16),
            pltpu.VMEM((1, count), jnp.int32),
            pltpu.VMEM((1, count), jnp.int32),
            pltpu.VMEM((n_dev, heads * cap + 8, HDIM), BF16),
            pltpu.VMEM((count, width), BF16),
            pltpu.VMEM((total, count), BF16),
            dma((3,)),
            dma((parts,)),
            dma((1,)),
            dma((parts,)),
        ],
        compiler_params=params(),
        cost_estimate=cost(2 * count * width * (dim + total), 4 << 20),
        name="dispatch",
    )(cand, gain, w_proj, owner, user)

    arrived = exchange(outgoing)

    span = 4
    kv_cache, keys, values = pl.pallas_call(
        encode_kernel,
        grid=(users // span,),
        in_specs=[
            pl.BlockSpec(memory_space=pltpu.SMEM),
            pl.BlockSpec((span, rows, dim), lambda i: (i, 0, 0)),
            whole((1, dim)),
            column((dim, width), 1),
            column((dim, width), 3),
        ],
        out_specs=[
            pl.BlockSpec((span, rows, 2 * width), lambda i: (i, 0, 0)),
            pl.BlockSpec((heads, span * HDIM // 2, 2 * rows), lambda i: (0, i, 0)),
            pl.BlockSpec((heads, span * rows // 2, 2 * HDIM), lambda i: (0, i, 0)),
        ],
        out_shape=[
            shape((users, rows, 2 * width), BF16),
            pltpu.HBM((heads, users * HDIM // 2, 2 * rows), BF16),
            pltpu.HBM((heads, users * rows // 2, 2 * HDIM), BF16),
        ],
        compiler_params=params(),
        cost_estimate=cost(2 * users * rows * dim * 2 * width, 12 << 20),
        name="encode",
    )(in_hbm(hist_len), history, gain, w_proj, w_proj)

    step = count // 2
    gate, own_v, aux = pl.pallas_call(
        functools.partial(own_kernel, n_grp, n_enc, cap),
        grid=(count // step,),
        in_specs=[
            pl.BlockSpec((step, dim), lambda i: (i, 0)),
            whole((1, dim)),
            whole((dim, 4 * width)),
            whole((1, count)),
        ],
        out_specs=[
            pl.BlockSpec((step, width), lambda i: (i, 0)),
            pl.BlockSpec((step, width), lambda i: (i, 0)),
            pl.BlockSpec((step, 128), lambda i: (i, 0)),
        ],
        out_shape=[shape((count, width), BF16), shape((count, width), BF16), shape((count, 128), F32)],
        scratch_shapes=[pltpu.VMEM((count, 128), F32)],
        compiler_params=params(),
        cost_estimate=cost(8 * count * dim * width, 6 << 20),
        name="own",
    )(cand, gain, w_proj, owner)

    kv_shape = (heads, users * HDIM // 2, 2 * rows)
    attended = pl.pallas_call(
        functools.partial(attend_kernel, cap),
        in_specs=[pl.BlockSpec(memory_space=pltpu.VMEM), anywhere, anywhere],
        out_specs=anywhere,
        out_shape=pltpu.HBM((n_dev, heads * cap, HDIM), BF16),
        scratch_shapes=[
            pltpu.VMEM(kv_shape, BF16),
            pltpu.VMEM(kv_shape, BF16),
            pltpu.VMEM((n_dev, heads * cap, HDIM), BF16),
            pltpu.VMEM((total, users * 64), BF16),
            pltpu.VMEM((total, 128), F32),
            dma((heads,)),
            dma((heads,)),
            dma((heads,)),
        ],
        compiler_params=params(),
        cost_estimate=cost(2 * total * rows * users * width * 2, 6 << 20),
        name="attend",
    )(in_vmem(arrived), in_hbm(keys), in_hbm(values))

    back = exchange(attended)

    cand_out = pl.pallas_call(
        answer_kernel,
        in_specs=[pl.BlockSpec(memory_space=pltpu.VMEM)] * 4,
        out_specs=pl.BlockSpec(memory_space=pltpu.VMEM),
        out_shape=shape((count, width), BF16),
        compiler_params=params(),
        cost_estimate=cost(2 * count * total * width, 4 << 20),
        name="answer",
    )(in_vmem(back), gate, own_v, aux)
    return (kv_cache, cand_out)


def solution(mesh):
    placed = (
        P(AXES, None, None),
        P(AXES),
        P(AXES, None),
        P(AXES, None),
        P(AXES),
        P(),
        P(),
    )
    return jax.shard_map(
        body,
        mesh=mesh,
        in_specs=placed,
        out_specs=(P(AXES, None, None), P(AXES, None)),
        check_vma=False,
    )
```

```python
import functools

import jax
import jax.numpy as jnp
from jax import lax
from jax.experimental import pallas as pl
from jax.experimental.pallas import tpu as pltpu
from jax.sharding import PartitionSpec as P

HDIM = 128
PIECE = 64
F32 = jnp.float32
BF16 = jnp.bfloat16
AXES = ("grp", "enc")
NT = (((1,), (1,)), ((), ()))


def silu(x):
    half = 0.5 * x
    return half + half * jnp.tanh(half)


def norm_rows(values):
    center = values - jnp.mean(values, axis=-1, keepdims=True)
    spread = jnp.mean(center * center, axis=-1, keepdims=True)
    return center * lax.rsqrt(spread + 1e-05)


def mm(a, b):
    return jnp.dot(a, b, preferred_element_type=F32)


def one_hot(hit):
    return jnp.where(hit, 1.0, 0.0).astype(BF16)


def iota(shape, dim):
    return lax.broadcasted_iota(jnp.int32, shape, dim)


def ranks(place, n_dev):
    count = place.shape[1]
    named = iota((n_dev, count), 0) == place
    hot = jnp.where(named, 1.0, 0.0)
    upper = one_hot(iota((128, 128), 0) < iota((128, 128), 1))
    carry, before = jnp.zeros((n_dev, 1), F32), []
    for c in range(0, count, 128):
        block = hot[:, c : c + 128]
        before.append(mm(block.astype(BF16), upper) + carry)
        carry = carry + jnp.sum(block, axis=1, keepdims=True)
    rank = jnp.where(named, jnp.concatenate(before, axis=1), 0.0)
    return named, jnp.sum(rank, axis=0, keepdims=True).astype(jnp.int32)


def dispatch_kernel(
    cap, cand_hbm, gain_hbm, w_hbm, owner_hbm, user_hbm, out_hbm,
    cand_ref, gain_ref, wq_ref, owner_ref, user_ref, out_ref, q_ref, pick_ref, small_sem, cand_sem, w_sem, out_sem,
):
    n_dev = out_ref.shape[0]
    count, width = q_ref.shape
    heads = width // HDIM
    parts = cand_sem.shape[0]
    step = count // parts

    def block(ref, i):
        return ref.at[pl.ds(i * step, step), :]

    small = [
        pltpu.make_async_copy(owner_hbm, owner_ref, small_sem.at[0]),
        pltpu.make_async_copy(user_hbm, user_ref, small_sem.at[1]),
        pltpu.make_async_copy(gain_hbm, gain_ref, small_sem.at[2]),
    ]
    loads = [pltpu.make_async_copy(block(cand_hbm, i), block(cand_ref, i), cand_sem.at[i]) for i in range(parts)]
    weights = pltpu.make_async_copy(w_hbm.at[:, pl.ds(2 * width, width)], wq_ref, w_sem.at[0])
    for copy in small:
        copy.start()
    loads[0].start()
    weights.start()
    for copy in loads[1:]:
        copy.start()
    for copy in small:
        copy.wait()
    place = owner_ref[...]
    named, rank = ranks(place, n_dev)
    pick_ref[...] = one_hot(iota((n_dev * cap, count), 0) == place * cap + rank)
    users = jnp.where(named, user_ref[...].astype(F32), 0.0).astype(BF16)
    table = lax.dot_general(users, one_hot(iota((128, count), 0) == rank), NT, preferred_element_type=F32)
    out_ref[:, heads * cap :, :] = jnp.broadcast_to(table[:, None, :], (n_dev, 8, 128)).astype(BF16)
    for copy in loads:
        copy.wait()
    weights.wait()
    gain = gain_ref[...]
    for r in range(0, count, 256):
        rows = slice(r, r + 256)
        x = cand_ref[rows, :].astype(F32)
        center = x - jnp.mean(x, axis=-1, keepdims=True)
        scale = lax.rsqrt(jnp.mean(center * center, axis=-1, keepdims=True) + 1e-05)
        q_ref[rows, :] = silu(mm((center * gain).astype(BF16), wq_ref[...]) * scale).astype(BF16)
    stores = []
    groups = out_sem.shape[0]
    span = n_dev // groups
    for g in range(groups):
        devs = slice(g * span, (g + 1) * span)
        sent = mm(pick_ref[g * span * cap : (g + 1) * span * cap, :], q_ref[...])
        for h in range(heads):
            part = sent[:, h * HDIM : (h + 1) * HDIM].reshape(span, cap, HDIM)
            out_ref[devs, h * cap : (h + 1) * cap, :] = part.astype(BF16)
        at = pl.ds(g * span, span)
        stores.append(pltpu.make_async_copy(out_ref.at[at], out_hbm.at[at], out_sem.at[g]))
        stores[-1].start()
    for copy in stores:
        copy.wait()


def encode_kernel(len_ref, hist_ref, gain_ref, wv_ref, wk_ref, out_ref, key_ref, value_ref):
    users, rows, dim = hist_ref.shape
    width = wk_ref.shape[1]
    first = pl.program_id(0) * users
    x = hist_ref[...].reshape(users * rows, dim).astype(F32)
    normed = (norm_rows(x) * gain_ref[...]).astype(BF16)
    keys = silu(mm(normed, wk_ref[...]))
    values = silu(mm(normed, wv_ref[...]))
    row_ids = iota((rows, width), 0)
    for u in range(users):
        live = row_ids < len_ref[first + u] * PIECE
        part = slice(u * rows, (u + 1) * rows)
        side = slice((u % 2) * rows, (u % 2 + 1) * rows)
        pair = slice((u // 2) * HDIM, (u // 2 + 1) * HDIM)
        key = jnp.where(live, keys[part], 0.0)
        value = jnp.where(live, values[part], 0.0).astype(BF16)
        out_ref[u, :, :width] = key.astype(BF16)
        out_ref[u, :, width:] = value
        for h in range(width // HDIM):
            cols = slice(h * HDIM, (h + 1) * HDIM)
            key_ref[h, pair, side] = key[:, cols].T.astype(BF16)
            value_ref[h, pair, side] = value[:, cols]


def own_kernel(n_dev, cap, cand_ref, gain_ref, w_ref, owner_ref, u_ref, v_ref, aux_ref, slot_ref):
    step, width = u_ref.shape
    heads = width // HDIM
    i = pl.program_id(0)

    @pl.when(i == 0)
    def _():
        place = owner_ref[...]
        _, rank = ranks(place, n_dev)
        slot = (place * cap + rank).astype(F32)
        slot_ref[...] = jnp.broadcast_to(slot, (128, slot.shape[1])).T

    normed = (norm_rows(cand_ref[...].astype(F32)) * gain_ref[...]).astype(BF16)

    def projected(part):
        return silu(mm(normed, w_ref[:, part * width : (part + 1) * width])).astype(BF16)

    u_ref[...] = projected(0)
    v_ref[...] = projected(1)
    prod = projected(2).astype(F32) * projected(3).astype(F32)
    lane = iota((step, 128), 1)
    aux = slot_ref[pl.ds(pl.multiple_of(i * step, step), step), :]
    for h in range(heads):
        score = jnp.sum(prod[:, h * HDIM : (h + 1) * HDIM], axis=-1, keepdims=True) * HDIM ** (-0.5)
        aux = jnp.where(lane == h, silu(score).astype(BF16).astype(F32), aux)
    aux_ref[...] = aux


def attend_kernel(
    cap, arrived_ref, k_hbm, v_hbm, out_hbm, k_ref, v_ref, out_ref, mask_ref, odd_ref, k_sem, v_sem, out_sem
):
    n_dev = arrived_ref.shape[0]
    heads, depth = k_ref.shape[0], k_ref.shape[1]
    total = n_dev * cap
    pairs = depth // HDIM
    groups = k_sem.shape[0]
    each = heads // groups

    def load(hbm, ref, sem, g):
        at = pl.ds(g * each, each)
        return pltpu.make_async_copy(hbm.at[at], ref.at[at], sem.at[g])

    for g in range(groups):
        load(k_hbm, k_ref, k_sem, g).start()
        load(v_hbm, v_ref, v_sem, g).start()

    full = (n_dev, cap, 128)
    table = arrived_ref[:, heads * cap : heads * cap + 8, :].astype(F32)[:, 0:1, :]
    own = jnp.where(iota(full, 1) == iota(full, 2), jnp.broadcast_to(table, full), 0.0)
    uid = mm(own.reshape(total, 128).astype(BF16), jnp.ones((128, 128), BF16))
    pair = jnp.floor(uid * 0.5)
    odd_ref[...] = uid - 2.0 * pair
    pair = pair.astype(BF16)
    for p in range(pairs):
        hit = pair == jnp.asarray(1.0 * p, BF16)
        mask_ref[:, p * 128 : (p + 1) * 128] = jnp.where(hit, jnp.ones((), BF16), jnp.zeros((), BF16))

    def spread(x):
        return jnp.concatenate([x * mask_ref[:, p * 128 : (p + 1) * 128] for p in range(pairs)], axis=1)

    def chosen(x):
        return jnp.where(odd_ref[...] > 0.5, x[:, 128:], x[:, :128])

    @pl.loop(0, groups)
    def _(g):
        members = [g * each + t for t in range(each)]
        load(k_hbm, k_ref, k_sem, g).wait()
        load(v_hbm, v_ref, v_sem, g).wait()
        scores = []
        for h in members:
            rows = pl.ds(pl.multiple_of(h * cap, cap), cap)
            query = arrived_ref[:, rows, :].astype(F32).reshape(total, HDIM).astype(BF16)
            scores.append(mm(spread(query), k_ref[h]))
        weights = [silu(chosen(score) * HDIM ** (-0.5)).astype(BF16) for score in scores]
        for h, weight in zip(members, weights):
            cols = pl.ds(pl.multiple_of(h * HDIM, HDIM), HDIM)
            out_ref[:, cols] = chosen(mm(spread(weight), v_ref[h])).astype(BF16)

    copy = pltpu.make_async_copy(out_ref, out_hbm, out_sem.at[0])
    copy.start()
    copy.wait()


def answer_kernel(back_ref, u_ref, v_ref, aux_ref, out_ref):
    width = u_ref.shape[1]
    total = back_ref.shape[0]
    heads = width // HDIM
    aux = aux_ref[...]
    pick = one_hot(iota((aux.shape[0], total), 1) == aux[:, heads : heads + 1].astype(jnp.int32))
    own_v = v_ref[...].astype(F32)
    own = [own_v[:, h * HDIM : (h + 1) * HDIM] * aux[:, h : h + 1] for h in range(heads)]
    normed = norm_rows(mm(pick, back_ref[...]) + jnp.concatenate(own, axis=1))
    out_ref[...] = normed.astype(BF16) * u_ref[...]


def params():
    return pltpu.CompilerParams(vmem_limit_bytes=36 * 1024 * 1024)


def whole(shape):
    return pl.BlockSpec(shape, lambda *_: (0,) * len(shape))


def column(shape, index):
    return pl.BlockSpec(shape, lambda *_: (0, index))


def cost(flops, size):
    return pl.CostEstimate(flops=flops, bytes_accessed=size, transcendentals=0)


def in_hbm(x):
    return pltpu.with_memory_space_constraint(x, pltpu.HBM)


def in_vmem(x):
    return pltpu.with_memory_space_constraint(x, pltpu.VMEM)


def exchange(slots):
    return lax.all_to_all(slots, AXES, split_axis=0, concat_axis=0, tiled=True)


def body(history, hist_len, cand, cand_owner, cand_user, norm_gain, w_proj):
    users, rows, dim = history.shape
    width = w_proj.shape[1] // 4
    heads = width // HDIM
    count = cand.shape[0]
    n_dev = lax.axis_size("grp") * lax.axis_size("enc")
    cap = -(-max(2, 3 * count // (2 * n_dev)) // 8) * 8
    total = n_dev * cap
    parts = 4
    shape = jax.ShapeDtypeStruct
    anywhere = pl.BlockSpec(memory_space=pl.ANY)
    dma = pltpu.SemaphoreType.DMA

    history, cand, w_proj = in_hbm(history), in_hbm(cand), in_hbm(w_proj)
    gain = in_hbm(norm_gain.reshape(1, dim))
    owner = in_hbm(cand_owner.reshape(1, count))
    user = in_hbm(cand_user.reshape(1, count))

    outgoing = pl.pallas_call(
        functools.partial(dispatch_kernel, cap),
        in_specs=[anywhere] * 5,
        out_specs=anywhere,
        out_shape=pltpu.HBM((n_dev, heads * cap + 8, HDIM), BF16),
        scratch_shapes=[
            pltpu.VMEM((count, dim), BF16),
            pltpu.VMEM((1, dim), F32),
            pltpu.VMEM((dim, width), BF16),
            pltpu.VMEM((1, count), jnp.int32),
            pltpu.VMEM((1, count), jnp.int32),
            pltpu.VMEM((n_dev, heads * cap + 8, HDIM), BF16),
            pltpu.VMEM((count, width), BF16),
            pltpu.VMEM((total, count), BF16),
            dma((3,)),
            dma((parts,)),
            dma((1,)),
            dma((1,)),
        ],
        compiler_params=params(),
        cost_estimate=cost(2 * count * width * (dim + total), 4 << 20),
        name="dispatch",
    )(cand, gain, w_proj, owner, user)

    arrived = exchange(outgoing)

    span = 4
    kv_cache, keys, values = pl.pallas_call(
        encode_kernel,
        grid=(users // span,),
        in_specs=[
            pl.BlockSpec(memory_space=pltpu.SMEM),
            pl.BlockSpec((span, rows, dim), lambda i: (i, 0, 0)),
            whole((1, dim)),
            column((dim, width), 1),
            column((dim, width), 3),
        ],
        out_specs=[
            pl.BlockSpec((span, rows, 2 * width), lambda i: (i, 0, 0)),
            pl.BlockSpec((heads, span * HDIM // 2, 2 * rows), lambda i: (0, i, 0)),
            pl.BlockSpec((heads, span * rows // 2, 2 * HDIM), lambda i: (0, i, 0)),
        ],
        out_shape=[
            shape((users, rows, 2 * width), BF16),
            pltpu.HBM((heads, users * HDIM // 2, 2 * rows), BF16),
            pltpu.HBM((heads, users * rows // 2, 2 * HDIM), BF16),
        ],
        compiler_params=params(),
        cost_estimate=cost(2 * users * rows * dim * 2 * width, 12 << 20),
        name="encode",
    )(in_hbm(hist_len), history, gain, w_proj, w_proj)

    step = count // 2
    gate, own_v, aux = pl.pallas_call(
        functools.partial(own_kernel, n_dev, cap),
        grid=(count // step,),
        in_specs=[
            pl.BlockSpec((step, dim), lambda i: (i, 0)),
            whole((1, dim)),
            whole((dim, 4 * width)),
            whole((1, count)),
        ],
        out_specs=[
            pl.BlockSpec((step, width), lambda i: (i, 0)),
            pl.BlockSpec((step, width), lambda i: (i, 0)),
            pl.BlockSpec((step, 128), lambda i: (i, 0)),
        ],
        out_shape=[shape((count, width), BF16), shape((count, width), BF16), shape((count, 128), F32)],
        scratch_shapes=[pltpu.VMEM((count, 128), F32)],
        compiler_params=params(),
        cost_estimate=cost(8 * count * dim * width, 6 << 20),
        name="own",
    )(cand, gain, w_proj, owner)

    kv_shape = (heads, users * HDIM // 2, 2 * rows)
    attended = pl.pallas_call(
        functools.partial(attend_kernel, cap),
        in_specs=[pl.BlockSpec(memory_space=pltpu.VMEM), anywhere, anywhere],
        out_specs=anywhere,
        out_shape=pltpu.HBM((total, width), BF16),
        scratch_shapes=[
            pltpu.VMEM(kv_shape, BF16),
            pltpu.VMEM(kv_shape, BF16),
            pltpu.VMEM((total, width), BF16),
            pltpu.VMEM((total, users * 64), BF16),
            pltpu.VMEM((total, 128), F32),
            dma((heads // 2,)),
            dma((heads // 2,)),
            dma((1,)),
        ],
        compiler_params=params(),
        cost_estimate=cost(2 * total * rows * users * width * 2, 6 << 20),
        name="attend",
    )(in_vmem(arrived), in_hbm(keys), in_hbm(values))

    back = exchange(attended.reshape(n_dev, cap, width)).reshape(total, width)

    cand_out = pl.pallas_call(
        answer_kernel,
        in_specs=[pl.BlockSpec(memory_space=pltpu.VMEM)] * 4,
        out_specs=pl.BlockSpec(memory_space=pltpu.VMEM),
        out_shape=shape((count, width), BF16),
        compiler_params=params(),
        cost_estimate=cost(2 * count * total * width, 4 << 20),
        name="answer",
    )(in_vmem(back), gate, own_v, aux)
    return (kv_cache, cand_out)


def solution(mesh):
    placed = (
        P(AXES, None, None),
        P(AXES),
        P(AXES, None),
        P(AXES, None),
        P(AXES),
        P(),
        P(),
    )
    return jax.shard_map(
        body,
        mesh=mesh,
        in_specs=placed,
        out_specs=(P(AXES, None, None), P(AXES, None)),
        check_vma=False,
    )
```

```python
import functools

import jax
import jax.numpy as jnp
from jax import lax
from jax.experimental import pallas as pl
from jax.experimental.pallas import tpu as pltpu
from jax.sharding import PartitionSpec as P

HDIM = 128
PIECE = 64
F32 = jnp.float32
BF16 = jnp.bfloat16
AXES = ("grp", "enc")
NT = (((1,), (1,)), ((), ()))


def silu(x):
    half = 0.5 * x
    return half + half * jnp.tanh(half)


def norm_rows(values):
    center = values - jnp.mean(values, axis=-1, keepdims=True)
    spread = jnp.mean(center * center, axis=-1, keepdims=True)
    return center * lax.rsqrt(spread + 1e-05)


def mm(a, b):
    return jnp.dot(a, b, preferred_element_type=F32)


def one_hot(hit):
    return jnp.where(hit, 1.0, 0.0).astype(BF16)


def iota(shape, dim):
    return lax.broadcasted_iota(jnp.int32, shape, dim)


def ranks(place, n_dev):
    count = place.shape[1]
    named = iota((n_dev, count), 0) == place
    hot = jnp.where(named, 1.0, 0.0)
    upper = one_hot(iota((128, 128), 0) < iota((128, 128), 1))
    carry, before = jnp.zeros((n_dev, 1), F32), []
    for c in range(0, count, 128):
        block = hot[:, c : c + 128]
        before.append(mm(block.astype(BF16), upper) + carry)
        carry = carry + jnp.sum(block, axis=1, keepdims=True)
    rank = jnp.where(named, jnp.concatenate(before, axis=1), 0.0)
    return named, jnp.sum(rank, axis=0, keepdims=True).astype(jnp.int32)


def dispatch_kernel(
    cap, cand_hbm, gain_hbm, w_hbm, owner_hbm, user_hbm, out_hbm,
    cand_ref, gain_ref, wq_ref, owner_ref, user_ref, out_ref, q_ref, pick_ref, small_sem, cand_sem, w_sem, out_sem,
):
    n_dev = out_ref.shape[0]
    count, width = q_ref.shape
    heads = width // HDIM
    parts = cand_sem.shape[0]
    step = count // parts

    def block(ref, i):
        return ref.at[pl.ds(i * step, step), :]

    small = [
        pltpu.make_async_copy(owner_hbm, owner_ref, small_sem.at[0]),
        pltpu.make_async_copy(user_hbm, user_ref, small_sem.at[1]),
        pltpu.make_async_copy(gain_hbm, gain_ref, small_sem.at[2]),
    ]
    loads = [pltpu.make_async_copy(block(cand_hbm, i), block(cand_ref, i), cand_sem.at[i]) for i in range(parts)]
    weights = pltpu.make_async_copy(w_hbm.at[:, pl.ds(2 * width, width)], wq_ref, w_sem.at[0])
    for copy in small:
        copy.start()
    loads[0].start()
    weights.start()
    for copy in loads[1:]:
        copy.start()
    for copy in small:
        copy.wait()
    place = owner_ref[...]
    named, rank = ranks(place, n_dev)
    pick_ref[...] = one_hot(iota((n_dev * cap, count), 0) == place * cap + rank)
    users = jnp.where(named, user_ref[...].astype(F32), 0.0).astype(BF16)
    table = lax.dot_general(users, one_hot(iota((128, count), 0) == rank), NT, preferred_element_type=F32)
    out_ref[:, heads * cap :, :] = jnp.broadcast_to(table[:, None, :], (n_dev, 8, 128)).astype(BF16)
    for copy in loads:
        copy.wait()
    weights.wait()
    gain = gain_ref[...]
    for r in range(0, count, 256):
        rows = slice(r, r + 256)
        x = cand_ref[rows, :].astype(F32)
        center = x - jnp.mean(x, axis=-1, keepdims=True)
        scale = lax.rsqrt(jnp.mean(center * center, axis=-1, keepdims=True) + 1e-05)
        q_ref[rows, :] = silu(mm((center * gain).astype(BF16), wq_ref[...]) * scale).astype(BF16)
    stores = []
    groups = out_sem.shape[0]
    span = n_dev // groups
    for g in range(groups):
        devs = slice(g * span, (g + 1) * span)
        sent = mm(pick_ref[g * span * cap : (g + 1) * span * cap, :], q_ref[...])
        for h in range(heads):
            part = sent[:, h * HDIM : (h + 1) * HDIM].reshape(span, cap, HDIM)
            out_ref[devs, h * cap : (h + 1) * cap, :] = part.astype(BF16)
        at = pl.ds(g * span, span)
        stores.append(pltpu.make_async_copy(out_ref.at[at], out_hbm.at[at], out_sem.at[g]))
        stores[-1].start()
    for copy in stores:
        copy.wait()


def encode_kernel(len_ref, hist_ref, gain_ref, wv_ref, wk_ref, out_ref, key_ref, value_ref):
    users, rows, dim = hist_ref.shape
    width = wk_ref.shape[1]
    first = pl.program_id(0) * users
    x = hist_ref[...].reshape(users * rows, dim).astype(F32)
    normed = (norm_rows(x) * gain_ref[...]).astype(BF16)
    keys = silu(mm(normed, wk_ref[...]))
    values = silu(mm(normed, wv_ref[...]))
    row_ids = iota((rows, width), 0)
    for u in range(users):
        live = row_ids < len_ref[first + u] * PIECE
        part = slice(u * rows, (u + 1) * rows)
        side = slice((u % 2) * rows, (u % 2 + 1) * rows)
        pair = slice((u // 2) * HDIM, (u // 2 + 1) * HDIM)
        key = jnp.where(live, keys[part], 0.0)
        value = jnp.where(live, values[part], 0.0).astype(BF16)
        out_ref[u, :, :width] = key.astype(BF16)
        out_ref[u, :, width:] = value
        for h in range(width // HDIM):
            cols = slice(h * HDIM, (h + 1) * HDIM)
            key_ref[h, pair, side] = key[:, cols].T.astype(BF16)
            value_ref[h, pair, side] = value[:, cols]


def own_kernel(n_dev, cap, me_ref, cand_ref, gain_ref, w_ref, owner_ref, u_ref, v_ref, aux_ref, slot_ref):
    step, width = u_ref.shape
    heads = width // HDIM
    i = pl.program_id(0)

    @pl.when(i == 0)
    def _():
        place = owner_ref[...]
        _, rank = ranks(place, n_dev)
        slot = ((place ^ me_ref[0]) * cap + rank).astype(F32)
        slot_ref[...] = jnp.broadcast_to(slot, (128, slot.shape[1])).T

    normed = (norm_rows(cand_ref[...].astype(F32)) * gain_ref[...]).astype(BF16)

    def projected(part):
        return silu(mm(normed, w_ref[:, part * width : (part + 1) * width])).astype(BF16)

    u_ref[...] = projected(0)
    v_ref[...] = projected(1)
    prod = projected(2).astype(F32) * projected(3).astype(F32)
    lane = iota((step, 128), 1)
    aux = slot_ref[pl.ds(pl.multiple_of(i * step, step), step), :]
    for h in range(heads):
        score = jnp.sum(prod[:, h * HDIM : (h + 1) * HDIM], axis=-1, keepdims=True) * HDIM ** (-0.5)
        aux = jnp.where(lane == h, silu(score).astype(BF16).astype(F32), aux)
    aux_ref[...] = aux


def attend_kernel(cap, n_out, me_ref, arrived_ref, k_hbm, v_hbm, *refs):
    out_hbm, (k_ref, v_ref, out_ref, mask_ref, odd_ref, k_sem, v_sem, out_sem) = refs[:n_out], refs[n_out:]
    n_dev = arrived_ref.shape[0]
    heads, depth = k_ref.shape[0], k_ref.shape[1]
    total = n_dev * cap
    pairs = depth // HDIM
    groups = k_sem.shape[0]
    each = heads // groups

    def load(hbm, ref, sem, g):
        at = pl.ds(g * each, each)
        return pltpu.make_async_copy(hbm.at[at], ref.at[at], sem.at[g])

    for g in range(groups):
        load(k_hbm, k_ref, k_sem, g).start()
        load(v_hbm, v_ref, v_sem, g).start()

    full = (n_dev, cap, 128)
    table = arrived_ref[:, heads * cap : heads * cap + 8, :].astype(F32)[:, 0:1, :]
    own = jnp.where(iota(full, 1) == iota(full, 2), jnp.broadcast_to(table, full), 0.0)
    uid = mm(own.reshape(total, 128).astype(BF16), jnp.ones((128, 128), BF16))
    pair = jnp.floor(uid * 0.5)
    odd_ref[...] = uid - 2.0 * pair
    pair = pair.astype(BF16)
    for p in range(pairs):
        hit = pair == jnp.asarray(1.0 * p, BF16)
        mask_ref[:, p * 128 : (p + 1) * 128] = jnp.where(hit, jnp.ones((), BF16), jnp.zeros((), BF16))

    def spread(x):
        return jnp.concatenate([x * mask_ref[:, p * 128 : (p + 1) * 128] for p in range(pairs)], axis=1)

    def chosen(x):
        return jnp.where(odd_ref[...] > 0.5, x[:, 128:], x[:, :128])

    @pl.loop(0, groups)
    def _(g):
        members = [g * each + t for t in range(each)]
        load(k_hbm, k_ref, k_sem, g).wait()
        load(v_hbm, v_ref, v_sem, g).wait()
        scores = []
        for h in members:
            rows = pl.ds(pl.multiple_of(h * cap, cap), cap)
            query = arrived_ref[:, rows, :].astype(F32).reshape(total, HDIM).astype(BF16)
            scores.append(mm(spread(query), k_ref[h]))
        weights = [silu(chosen(score) * HDIM ** (-0.5)).astype(BF16) for score in scores]
        for h, weight in zip(members, weights):
            cols = pl.ds(pl.multiple_of(h * HDIM, HDIM), HDIM)
            attended = chosen(mm(spread(weight), v_ref[h]))
            out_ref[:, :, cols] = attended.reshape(n_dev, cap, HDIM).astype(BF16)

    if n_out == 1:
        stores = [pltpu.make_async_copy(out_ref, out_hbm[0], out_sem.at[0])]
    else:
        stores = [
            pltpu.make_async_copy(out_ref.at[me_ref[0] ^ k], out_hbm[k], out_sem.at[k]) for k in range(n_out)
        ]
    for copy in stores:
        copy.start()
    for copy in stores:
        copy.wait()


def answer_kernel(n_back, *refs):
    back_refs, (u_ref, v_ref, aux_ref, out_ref) = refs[:n_back], refs[n_back:]
    width = u_ref.shape[1]
    heads = width // HDIM
    back = jnp.concatenate([ref[...].astype(F32).reshape(-1, width) for ref in back_refs], axis=0).astype(BF16)
    total = back.shape[0]
    aux = aux_ref[...]
    pick = one_hot(iota((aux.shape[0], total), 1) == aux[:, heads : heads + 1].astype(jnp.int32))
    own_v = v_ref[...].astype(F32)
    own = [own_v[:, h * HDIM : (h + 1) * HDIM] * aux[:, h : h + 1] for h in range(heads)]
    normed = norm_rows(mm(pick, back) + jnp.concatenate(own, axis=1))
    out_ref[...] = normed.astype(BF16) * u_ref[...]


def params():
    return pltpu.CompilerParams(vmem_limit_bytes=36 * 1024 * 1024)


def whole(shape):
    return pl.BlockSpec(shape, lambda *_: (0,) * len(shape))


def column(shape, index):
    return pl.BlockSpec(shape, lambda *_: (0, index))


def cost(flops, size):
    return pl.CostEstimate(flops=flops, bytes_accessed=size, transcendentals=0)


def in_hbm(x):
    return pltpu.with_memory_space_constraint(x, pltpu.HBM)


def in_vmem(x):
    return pltpu.with_memory_space_constraint(x, pltpu.VMEM)


def exchange(slots):
    return lax.all_to_all(slots, AXES, split_axis=0, concat_axis=0, tiled=True)


def swap(x, k, n_dev):
    return lax.ppermute(x, AXES, [(i, i ^ k) for i in range(n_dev)])


def body(history, hist_len, cand, cand_owner, cand_user, norm_gain, w_proj):
    users, rows, dim = history.shape
    width = w_proj.shape[1] // 4
    heads = width // HDIM
    count = cand.shape[0]
    n_dev = lax.axis_size("grp") * lax.axis_size("enc")
    cap = -(-max(2, 3 * count // (2 * n_dev)) // 8) * 8
    total = n_dev * cap
    parts = 4
    direct = n_dev <= 32
    n_out = n_dev if direct else 1
    me = (lax.axis_index("grp") * lax.axis_size("enc") + lax.axis_index("enc")).astype(jnp.int32).reshape(1)
    me = me if direct else jnp.zeros_like(me)
    scalar = pl.BlockSpec(memory_space=pltpu.SMEM)
    shape = jax.ShapeDtypeStruct
    anywhere = pl.BlockSpec(memory_space=pl.ANY)
    dma = pltpu.SemaphoreType.DMA

    history, cand, w_proj = in_hbm(history), in_hbm(cand), in_hbm(w_proj)
    gain = in_hbm(norm_gain.reshape(1, dim))
    owner = in_hbm(cand_owner.reshape(1, count))
    user = in_hbm(cand_user.reshape(1, count))

    outgoing = pl.pallas_call(
        functools.partial(dispatch_kernel, cap),
        in_specs=[anywhere] * 5,
        out_specs=anywhere,
        out_shape=pltpu.HBM((n_dev, heads * cap + 8, HDIM), BF16),
        scratch_shapes=[
            pltpu.VMEM((count, dim), BF16),
            pltpu.VMEM((1, dim), F32),
            pltpu.VMEM((dim, width), BF16),
            pltpu.VMEM((1, count), jnp.int32),
            pltpu.VMEM((1, count), jnp.int32),
            pltpu.VMEM((n_dev, heads * cap + 8, HDIM), BF16),
            pltpu.VMEM((count, width), BF16),
            pltpu.VMEM((total, count), BF16),
            dma((3,)),
            dma((parts,)),
            dma((1,)),
            dma((1,)),
        ],
        compiler_params=params(),
        cost_estimate=cost(2 * count * width * (dim + total), 4 << 20),
        name="dispatch",
    )(cand, gain, w_proj, owner, user)

    arrived = exchange(outgoing)

    span = 4
    kv_cache, keys, values = pl.pallas_call(
        encode_kernel,
        grid=(users // span,),
        in_specs=[
            pl.BlockSpec(memory_space=pltpu.SMEM),
            pl.BlockSpec((span, rows, dim), lambda i: (i, 0, 0)),
            whole((1, dim)),
            column((dim, width), 1),
            column((dim, width), 3),
        ],
        out_specs=[
            pl.BlockSpec((span, rows, 2 * width), lambda i: (i, 0, 0)),
            pl.BlockSpec((heads, span * HDIM // 2, 2 * rows), lambda i: (0, i, 0)),
            pl.BlockSpec((heads, span * rows // 2, 2 * HDIM), lambda i: (0, i, 0)),
        ],
        out_shape=[
            shape((users, rows, 2 * width), BF16),
            pltpu.HBM((heads, users * HDIM // 2, 2 * rows), BF16),
            pltpu.HBM((heads, users * rows // 2, 2 * HDIM), BF16),
        ],
        compiler_params=params(),
        cost_estimate=cost(2 * users * rows * dim * 2 * width, 12 << 20),
        name="encode",
    )(in_hbm(hist_len), history, gain, w_proj, w_proj)

    step = count // 2
    gate, own_v, aux = pl.pallas_call(
        functools.partial(own_kernel, n_dev, cap),
        grid=(count // step,),
        in_specs=[
            scalar,
            pl.BlockSpec((step, dim), lambda i: (i, 0)),
            whole((1, dim)),
            whole((dim, 4 * width)),
            whole((1, count)),
        ],
        out_specs=[
            pl.BlockSpec((step, width), lambda i: (i, 0)),
            pl.BlockSpec((step, width), lambda i: (i, 0)),
            pl.BlockSpec((step, 128), lambda i: (i, 0)),
        ],
        out_shape=[shape((count, width), BF16), shape((count, width), BF16), shape((count, 128), F32)],
        scratch_shapes=[pltpu.VMEM((count, 128), F32)],
        compiler_params=params(),
        cost_estimate=cost(8 * count * dim * width, 6 << 20),
        name="own",
    )(me, cand, gain, w_proj, owner)

    kv_shape = (heads, users * HDIM // 2, 2 * rows)
    attended = pl.pallas_call(
        functools.partial(attend_kernel, cap, n_out),
        in_specs=[scalar, pl.BlockSpec(memory_space=pltpu.VMEM), anywhere, anywhere],
        out_specs=[anywhere] * n_out,
        out_shape=[pltpu.HBM((cap, width) if direct else (n_dev, cap, width), BF16)] * n_out,
        scratch_shapes=[
            pltpu.VMEM(kv_shape, BF16),
            pltpu.VMEM(kv_shape, BF16),
            pltpu.VMEM((n_dev, cap, width), BF16),
            pltpu.VMEM((total, users * 64), BF16),
            pltpu.VMEM((total, 128), F32),
            dma((heads // 2,)),
            dma((heads // 2,)),
            dma((n_out,)),
        ],
        compiler_params=params(),
        cost_estimate=cost(2 * total * rows * users * width * 2, 6 << 20),
        name="attend",
    )(me, in_vmem(arrived), in_hbm(keys), in_hbm(values))

    if direct:
        back = {k: swap(attended[k], k, n_dev) for k in range(n_dev - 1, 0, -1)}
        back = [attended[0]] + [back[k] for k in range(1, n_dev)]
    else:
        back = [exchange(attended[0])]

    cand_out = pl.pallas_call(
        functools.partial(answer_kernel, n_out),
        in_specs=[pl.BlockSpec(memory_space=pltpu.VMEM)] * (n_out + 3),
        out_specs=pl.BlockSpec(memory_space=pltpu.VMEM),
        out_shape=shape((count, width), BF16),
        compiler_params=params(),
        cost_estimate=cost(2 * count * total * width, 4 << 20),
        name="answer",
    )(*[in_vmem(x) for x in back], gate, own_v, aux)
    return (kv_cache, cand_out)


def solution(mesh):
    placed = (
        P(AXES, None, None),
        P(AXES),
        P(AXES, None),
        P(AXES, None),
        P(AXES),
        P(),
        P(),
    )
    return jax.shard_map(
        body,
        mesh=mesh,
        in_specs=placed,
        out_specs=(P(AXES, None, None), P(AXES, None)),
        check_vma=False,
    )
```

```python
import functools

import jax
import jax.numpy as jnp
from jax import lax
from jax.experimental import pallas as pl
from jax.experimental.pallas import tpu as pltpu
from jax.sharding import PartitionSpec as P

HDIM = 128
PIECE = 64
F32 = jnp.float32
BF16 = jnp.bfloat16
AXES = ("grp", "enc")
NT = (((1,), (1,)), ((), ()))


def silu(x):
    half = 0.5 * x
    return half + half * jnp.tanh(half)


def norm_rows(values):
    center = values - jnp.mean(values, axis=-1, keepdims=True)
    spread = jnp.mean(center * center, axis=-1, keepdims=True)
    return center * lax.rsqrt(spread + 1e-05)


def mm(a, b):
    return jnp.dot(a, b, preferred_element_type=F32)


def one_hot(hit):
    return jnp.where(hit, 1.0, 0.0).astype(BF16)


def iota(shape, dim):
    return lax.broadcasted_iota(jnp.int32, shape, dim)


def ranks(place, n_dev):
    count = place.shape[1]
    named = iota((n_dev, count), 0) == place
    hot = jnp.where(named, 1.0, 0.0)
    upper = one_hot(iota((128, 128), 0) < iota((128, 128), 1))
    carry, before = jnp.zeros((n_dev, 1), F32), []
    for c in range(0, count, 128):
        block = hot[:, c : c + 128]
        before.append(mm(block.astype(BF16), upper) + carry)
        carry = carry + jnp.sum(block, axis=1, keepdims=True)
    rank = jnp.where(named, jnp.concatenate(before, axis=1), 0.0)
    return named, jnp.sum(rank, axis=0, keepdims=True).astype(jnp.int32)


def dispatch_kernel(
    cap, cand_hbm, gain_hbm, w_hbm, owner_hbm, user_hbm, out_hbm,
    cand_ref, gain_ref, wq_ref, owner_ref, user_ref, out_ref, q_ref, pick_ref, small_sem, cand_sem, w_sem, out_sem,
):
    n_dev = out_ref.shape[0]
    count, width = q_ref.shape
    heads = width // HDIM
    parts = cand_sem.shape[0]
    step = count // parts

    def block(ref, i):
        return ref.at[pl.ds(i * step, step), :]

    small = [
        pltpu.make_async_copy(owner_hbm, owner_ref, small_sem.at[0]),
        pltpu.make_async_copy(user_hbm, user_ref, small_sem.at[1]),
        pltpu.make_async_copy(gain_hbm, gain_ref, small_sem.at[2]),
    ]
    loads = [pltpu.make_async_copy(block(cand_hbm, i), block(cand_ref, i), cand_sem.at[i]) for i in range(parts)]
    weights = pltpu.make_async_copy(w_hbm.at[:, pl.ds(2 * width, width)], wq_ref, w_sem.at[0])
    for copy in small:
        copy.start()
    loads[0].start()
    weights.start()
    for copy in loads[1:]:
        copy.start()
    for copy in small:
        copy.wait()
    place = owner_ref[...]
    named, rank = ranks(place, n_dev)
    pick_ref[...] = one_hot(iota((n_dev * cap, count), 0) == place * cap + rank)
    users = jnp.where(named, user_ref[...].astype(F32), 0.0).astype(BF16)
    table = lax.dot_general(users, one_hot(iota((128, count), 0) == rank), NT, preferred_element_type=F32)
    out_ref[:, heads * cap :, :] = jnp.broadcast_to(table[:, None, :], (n_dev, 8, 128)).astype(BF16)
    for copy in loads:
        copy.wait()
    weights.wait()
    gain = gain_ref[...]
    for r in range(0, count, 256):
        rows = slice(r, r + 256)
        x = cand_ref[rows, :].astype(F32)
        center = x - jnp.mean(x, axis=-1, keepdims=True)
        scale = lax.rsqrt(jnp.mean(center * center, axis=-1, keepdims=True) + 1e-05)
        q_ref[rows, :] = silu(mm((center * gain).astype(BF16), wq_ref[...]) * scale).astype(BF16)
    stores = []
    groups = out_sem.shape[0]
    span = n_dev // groups
    for g in range(groups):
        devs = slice(g * span, (g + 1) * span)
        sent = mm(pick_ref[g * span * cap : (g + 1) * span * cap, :], q_ref[...])
        for h in range(heads):
            part = sent[:, h * HDIM : (h + 1) * HDIM].reshape(span, cap, HDIM)
            out_ref[devs, h * cap : (h + 1) * cap, :] = part.astype(BF16)
        at = pl.ds(g * span, span)
        stores.append(pltpu.make_async_copy(out_ref.at[at], out_hbm.at[at], out_sem.at[g]))
        stores[-1].start()
    for copy in stores:
        copy.wait()


def encode_kernel(len_ref, hist_ref, gain_ref, wv_ref, wk_ref, out_ref, key_ref, value_ref):
    users, rows, dim = hist_ref.shape
    width = wk_ref.shape[1]
    first = pl.program_id(0) * users
    x = hist_ref[...].reshape(users * rows, dim).astype(F32)
    normed = (norm_rows(x) * gain_ref[...]).astype(BF16)
    keys = silu(mm(normed, wk_ref[...]))
    values = silu(mm(normed, wv_ref[...]))
    row_ids = iota((rows, width), 0)
    for u in range(users):
        live = row_ids < len_ref[first + u] * PIECE
        part = slice(u * rows, (u + 1) * rows)
        side = slice((u % 2) * rows, (u % 2 + 1) * rows)
        pair = slice((u // 2) * HDIM, (u // 2 + 1) * HDIM)
        key = jnp.where(live, keys[part], 0.0)
        value = jnp.where(live, values[part], 0.0).astype(BF16)
        out_ref[u, :, :width] = key.astype(BF16)
        out_ref[u, :, width:] = value
        for h in range(width // HDIM):
            cols = slice(h * HDIM, (h + 1) * HDIM)
            key_ref[h, pair, side] = key[:, cols].T.astype(BF16)
            value_ref[h, pair, side] = value[:, cols]


def own_kernel(cap, cand_ref, gain_ref, w_ref, owner_ref, u_ref, self_ref, pick_ref, slot_ref):
    step, width = u_ref.shape
    total = pick_ref.shape[1]
    i = pl.program_id(0)

    @pl.when(i == 0)
    def _():
        place = owner_ref[...]
        _, rank = ranks(place, total // cap)
        slot = (place * cap + rank).astype(F32)
        slot_ref[...] = jnp.broadcast_to(slot, (128, slot.shape[1])).T

    normed = (norm_rows(cand_ref[...].astype(F32)) * gain_ref[...]).astype(BF16)

    def projected(part):
        return silu(mm(normed, w_ref[:, part * width : (part + 1) * width])).astype(BF16)

    u_ref[...] = projected(0)
    own_v = projected(1).astype(F32)
    prod = projected(2).astype(F32) * projected(3).astype(F32)
    for h in range(width // HDIM):
        cols = slice(h * HDIM, (h + 1) * HDIM)
        score = jnp.sum(prod[:, cols], axis=-1, keepdims=True) * HDIM ** (-0.5)
        self_ref[:, cols] = (silu(score).astype(BF16).astype(F32) * own_v[:, cols]).astype(BF16)
    slot = slot_ref[pl.ds(pl.multiple_of(i * step, step), step), 0:1].astype(jnp.int32)
    pick_ref[...] = one_hot(iota((step, total), 1) == slot)


def attend_kernel(
    cap, arrived_ref, k_hbm, v_hbm, _, out_hbm, k_ref, v_ref, out_ref, mask_ref, odd_ref, k_sem, v_sem, out_sem
):
    n_dev = arrived_ref.shape[0]
    heads, depth = k_ref.shape[0], k_ref.shape[1]
    total = n_dev * cap
    pairs = depth // HDIM
    groups = k_sem.shape[0]
    each = heads // groups

    def load(hbm, ref, sem, g):
        at = pl.ds(g * each, each)
        return pltpu.make_async_copy(hbm.at[at], ref.at[at], sem.at[g])

    for g in range(groups):
        load(k_hbm, k_ref, k_sem, g).start()
        load(v_hbm, v_ref, v_sem, g).start()

    full = (n_dev, cap, 128)
    table = arrived_ref[:, heads * cap : heads * cap + 8, :].astype(F32)[:, 0:1, :]
    own = jnp.where(iota(full, 1) == iota(full, 2), jnp.broadcast_to(table, full), 0.0)
    uid = mm(own.reshape(total, 128).astype(BF16), jnp.ones((128, 128), BF16))
    pair = jnp.floor(uid * 0.5)
    odd_ref[...] = uid - 2.0 * pair
    pair = pair.astype(BF16)
    for p in range(pairs):
        hit = pair == jnp.asarray(1.0 * p, BF16)
        mask_ref[:, p * 128 : (p + 1) * 128] = jnp.where(hit, jnp.ones((), BF16), jnp.zeros((), BF16))

    def spread(x):
        return jnp.concatenate([x * mask_ref[:, p * 128 : (p + 1) * 128] for p in range(pairs)], axis=1)

    def chosen(x):
        return jnp.where(odd_ref[...] > 0.5, x[:, 128:], x[:, :128])

    @pl.loop(0, groups)
    def _(g):
        members = [g * each + t for t in range(each)]
        load(k_hbm, k_ref, k_sem, g).wait()
        scores = []
        for h in members:
            rows = pl.ds(pl.multiple_of(h * cap, cap), cap)
            query = arrived_ref[:, rows, :].astype(F32).reshape(total, HDIM).astype(BF16)
            scores.append(mm(spread(query), k_ref[h]))
        weights = [silu(chosen(score) * HDIM ** (-0.5)).astype(BF16) for score in scores]
        load(v_hbm, v_ref, v_sem, g).wait()
        for h, weight in zip(members, weights):
            cols = pl.ds(pl.multiple_of(h * HDIM, HDIM), HDIM)
            out_ref[:, cols] = chosen(mm(spread(weight), v_ref[h])).astype(BF16)

    copy = pltpu.make_async_copy(out_ref, out_hbm, out_sem.at[0])
    copy.start()
    copy.wait()


def answer_kernel(back_ref, u_ref, self_ref, pick_ref, out_ref):
    normed = norm_rows(mm(pick_ref[...], back_ref[...]) + self_ref[...].astype(F32))
    out_ref[...] = normed.astype(BF16) * u_ref[...]


def params():
    return pltpu.CompilerParams(vmem_limit_bytes=36 * 1024 * 1024)


def whole(shape):
    return pl.BlockSpec(shape, lambda *_: (0,) * len(shape))


def column(shape, index):
    return pl.BlockSpec(shape, lambda *_: (0, index))


def cost(flops, size):
    return pl.CostEstimate(flops=flops, bytes_accessed=size, transcendentals=0)


def in_hbm(x):
    return pltpu.with_memory_space_constraint(x, pltpu.HBM)


def in_vmem(x):
    return pltpu.with_memory_space_constraint(x, pltpu.VMEM)


def exchange(slots):
    return lax.all_to_all(slots, AXES, split_axis=0, concat_axis=0, tiled=True)


def body(history, hist_len, cand, cand_owner, cand_user, norm_gain, w_proj):
    users, rows, dim = history.shape
    width = w_proj.shape[1] // 4
    heads = width // HDIM
    count = cand.shape[0]
    n_dev = lax.axis_size("grp") * lax.axis_size("enc")
    cap = -(-max(2, 3 * count // (2 * n_dev)) // 8) * 8
    total = n_dev * cap
    parts = 4
    shape = jax.ShapeDtypeStruct
    anywhere = pl.BlockSpec(memory_space=pl.ANY)
    dma = pltpu.SemaphoreType.DMA

    history, cand, w_proj = in_hbm(history), in_hbm(cand), in_hbm(w_proj)
    gain = in_hbm(norm_gain.reshape(1, dim))
    owner = in_hbm(cand_owner.reshape(1, count))
    user = in_hbm(cand_user.reshape(1, count))

    outgoing = pl.pallas_call(
        functools.partial(dispatch_kernel, cap),
        in_specs=[anywhere] * 5,
        out_specs=anywhere,
        out_shape=pltpu.HBM((n_dev, heads * cap + 8, HDIM), BF16),
        scratch_shapes=[
            pltpu.VMEM((count, dim), BF16),
            pltpu.VMEM((1, dim), F32),
            pltpu.VMEM((dim, width), BF16),
            pltpu.VMEM((1, count), jnp.int32),
            pltpu.VMEM((1, count), jnp.int32),
            pltpu.VMEM((n_dev, heads * cap + 8, HDIM), BF16),
            pltpu.VMEM((count, width), BF16),
            pltpu.VMEM((total, count), BF16),
            dma((3,)),
            dma((parts,)),
            dma((1,)),
            dma((1,)),
        ],
        compiler_params=params(),
        cost_estimate=cost(2 * count * width * (dim + total), 4 << 20),
        name="dispatch",
    )(cand, gain, w_proj, owner, user)

    arrived = exchange(outgoing)

    span = 4
    kv_cache, keys, values = pl.pallas_call(
        encode_kernel,
        grid=(users // span,),
        in_specs=[
            pl.BlockSpec(memory_space=pltpu.SMEM),
            pl.BlockSpec((span, rows, dim), lambda i: (i, 0, 0)),
            whole((1, dim)),
            column((dim, width), 1),
            column((dim, width), 3),
        ],
        out_specs=[
            pl.BlockSpec((span, rows, 2 * width), lambda i: (i, 0, 0)),
            pl.BlockSpec((heads, span * HDIM // 2, 2 * rows), lambda i: (0, i, 0)),
            pl.BlockSpec((heads, span * rows // 2, 2 * HDIM), lambda i: (0, i, 0)),
        ],
        out_shape=[
            shape((users, rows, 2 * width), BF16),
            pltpu.HBM((heads, users * HDIM // 2, 2 * rows), BF16),
            pltpu.HBM((heads, users * rows // 2, 2 * HDIM), BF16),
        ],
        compiler_params=params(),
        cost_estimate=cost(2 * users * rows * dim * 2 * width, 12 << 20),
        name="encode",
    )(in_hbm(hist_len), history, gain, w_proj, w_proj)

    step = count // 2
    gate, own, pick = pl.pallas_call(
        functools.partial(own_kernel, cap),
        grid=(count // step,),
        in_specs=[
            pl.BlockSpec((step, dim), lambda i: (i, 0)),
            whole((1, dim)),
            whole((dim, 4 * width)),
            whole((1, count)),
        ],
        out_specs=[
            pl.BlockSpec((step, width), lambda i: (i, 0)),
            pl.BlockSpec((step, width), lambda i: (i, 0)),
            pl.BlockSpec((step, total), lambda i: (i, 0)),
        ],
        out_shape=[shape((count, width), BF16), shape((count, width), BF16), shape((count, total), BF16)],
        scratch_shapes=[pltpu.VMEM((count, 128), F32)],
        compiler_params=params(),
        cost_estimate=cost(8 * count * dim * width, 6 << 20),
        name="own",
    )(cand, gain, w_proj, owner)

    kv_shape = (heads, users * HDIM // 2, 2 * rows)
    attended = pl.pallas_call(
        functools.partial(attend_kernel, cap),
        in_specs=[pl.BlockSpec(memory_space=pltpu.VMEM), anywhere, anywhere, anywhere],
        out_specs=anywhere,
        out_shape=pltpu.HBM((total, width), BF16),
        scratch_shapes=[
            pltpu.VMEM(kv_shape, BF16),
            pltpu.VMEM(kv_shape, BF16),
            pltpu.VMEM((total, width), BF16),
            pltpu.VMEM((total, users * 64), BF16),
            pltpu.VMEM((total, 128), F32),
            dma((heads // 2,)),
            dma((heads // 2,)),
            dma((1,)),
        ],
        compiler_params=params(),
        cost_estimate=cost(2 * total * rows * users * width * 2, 6 << 20),
        name="attend",
    )(in_vmem(arrived), in_hbm(keys), in_hbm(values), own)

    back = exchange(attended.reshape(n_dev, cap, width)).reshape(total, width)

    cand_out = pl.pallas_call(
        answer_kernel,
        in_specs=[pl.BlockSpec(memory_space=pltpu.VMEM)] * 4,
        out_specs=pl.BlockSpec(memory_space=pltpu.VMEM),
        out_shape=shape((count, width), BF16),
        compiler_params=params(),
        cost_estimate=cost(2 * count * total * width, 4 << 20),
        name="answer",
    )(in_vmem(back), gate, own, pick)
    return (kv_cache, cand_out)


def solution(mesh):
    placed = (
        P(AXES, None, None),
        P(AXES),
        P(AXES, None),
        P(AXES, None),
        P(AXES),
        P(),
        P(),
    )
    return jax.shard_map(
        body,
        mesh=mesh,
        in_specs=placed,
        out_specs=(P(AXES, None, None), P(AXES, None)),
        check_vma=False,
    )
```

```python
import functools

import jax
import jax.numpy as jnp
from jax import lax
from jax.experimental import pallas as pl
from jax.experimental.pallas import tpu as pltpu
from jax.sharding import PartitionSpec as P

HDIM = 128
PIECE = 64
F32 = jnp.float32
BF16 = jnp.bfloat16
AXES = ("grp", "enc")
NT = (((1,), (1,)), ((), ()))


def silu(x):
    half = 0.5 * x
    return half + half * jnp.tanh(half)


def norm_rows(values):
    center = values - jnp.mean(values, axis=-1, keepdims=True)
    spread = jnp.mean(center * center, axis=-1, keepdims=True)
    return center * lax.rsqrt(spread + 1e-05)


def mm(a, b):
    return jnp.dot(a, b, preferred_element_type=F32)


def one_hot(hit):
    return jnp.where(hit, 1.0, 0.0).astype(BF16)


def iota(shape, dim):
    return lax.broadcasted_iota(jnp.int32, shape, dim)


def ranks(place, n_dev):
    count = place.shape[1]
    named = iota((n_dev, count), 0) == place
    hot = jnp.where(named, 1.0, 0.0)
    upper = one_hot(iota((128, 128), 0) < iota((128, 128), 1))
    carry, before = jnp.zeros((n_dev, 1), F32), []
    for c in range(0, count, 128):
        block = hot[:, c : c + 128]
        before.append(mm(block.astype(BF16), upper) + carry)
        carry = carry + jnp.sum(block, axis=1, keepdims=True)
    rank = jnp.where(named, jnp.concatenate(before, axis=1), 0.0)
    return named, jnp.sum(rank, axis=0, keepdims=True).astype(jnp.int32)


def dispatch_kernel(
    cap, cand_hbm, gain_hbm, w_hbm, owner_hbm, user_hbm, out_hbm,
    cand_ref, gain_ref, wq_ref, owner_ref, user_ref, out_ref, q_ref, pick_ref, small_sem, cand_sem, w_sem, out_sem,
):
    n_dev = out_ref.shape[0]
    count, width = q_ref.shape
    heads = width // HDIM
    parts = cand_sem.shape[0]
    step = count // parts

    def block(ref, i):
        return ref.at[pl.ds(i * step, step), :]

    small = [
        pltpu.make_async_copy(owner_hbm, owner_ref, small_sem.at[0]),
        pltpu.make_async_copy(user_hbm, user_ref, small_sem.at[1]),
        pltpu.make_async_copy(gain_hbm, gain_ref, small_sem.at[2]),
    ]
    loads = [pltpu.make_async_copy(block(cand_hbm, i), block(cand_ref, i), cand_sem.at[i]) for i in range(parts)]
    weights = pltpu.make_async_copy(w_hbm.at[:, pl.ds(2 * width, width)], wq_ref, w_sem.at[0])
    for copy in small:
        copy.start()
    loads[0].start()
    weights.start()
    for copy in loads[1:]:
        copy.start()
    for copy in small:
        copy.wait()
    place = owner_ref[...]
    named, rank = ranks(place, n_dev)
    pick_ref[...] = one_hot(iota((n_dev * cap, count), 0) == place * cap + rank)
    users = jnp.where(named, user_ref[...].astype(F32), 0.0).astype(BF16)
    table = lax.dot_general(users, one_hot(iota((128, count), 0) == rank), NT, preferred_element_type=F32)
    out_ref[:, heads * cap :, :] = jnp.broadcast_to(table[:, None, :], (n_dev, 8, 128)).astype(BF16)
    for copy in loads:
        copy.wait()
    weights.wait()
    gain = gain_ref[...]
    for r in range(0, count, 256):
        rows = slice(r, r + 256)
        x = cand_ref[rows, :].astype(F32)
        center = x - jnp.mean(x, axis=-1, keepdims=True)
        scale = lax.rsqrt(jnp.mean(center * center, axis=-1, keepdims=True) + 1e-05)
        q_ref[rows, :] = silu(mm((center * gain).astype(BF16), wq_ref[...]) * scale).astype(BF16)
    stores = []
    groups = out_sem.shape[0]
    span = n_dev // groups
    for g in range(groups):
        devs = slice(g * span, (g + 1) * span)
        sent = mm(pick_ref[g * span * cap : (g + 1) * span * cap, :], q_ref[...])
        for h in range(heads):
            part = sent[:, h * HDIM : (h + 1) * HDIM].reshape(span, cap, HDIM)
            out_ref[devs, h * cap : (h + 1) * cap, :] = part.astype(BF16)
        at = pl.ds(g * span, span)
        stores.append(pltpu.make_async_copy(out_ref.at[at], out_hbm.at[at], out_sem.at[g]))
        stores[-1].start()
    for copy in stores:
        copy.wait()


def encode_kernel(len_ref, hist_ref, gain_ref, wv_ref, wk_ref, out_ref, key_ref, value_ref):
    users, rows, dim = hist_ref.shape
    width = wk_ref.shape[1]
    first = pl.program_id(0) * users
    x = hist_ref[...].reshape(users * rows, dim).astype(F32)
    normed = (norm_rows(x) * gain_ref[...]).astype(BF16)
    keys = silu(mm(normed, wk_ref[...]))
    values = silu(mm(normed, wv_ref[...]))
    row_ids = iota((rows, width), 0)
    for u in range(users):
        live = row_ids < len_ref[first + u] * PIECE
        part = slice(u * rows, (u + 1) * rows)
        side = slice((u % 2) * rows, (u % 2 + 1) * rows)
        pair = slice((u // 2) * HDIM, (u // 2 + 1) * HDIM)
        key = jnp.where(live, keys[part], 0.0)
        value = jnp.where(live, values[part], 0.0).astype(BF16)
        out_ref[u, :, :width] = key.astype(BF16)
        out_ref[u, :, width:] = value
        for h in range(width // HDIM):
            cols = slice(h * HDIM, (h + 1) * HDIM)
            key_ref[h, pair, side] = key[:, cols].T.astype(BF16)
            value_ref[h, pair, side] = value[:, cols]


def own_kernel(cap, cand_ref, gain_ref, w_ref, owner_ref, u_ref, self_ref, pick_ref, slot_ref):
    step, width = u_ref.shape
    total = pick_ref.shape[1]
    i = pl.program_id(0)

    @pl.when(i == 0)
    def _():
        place = owner_ref[...]
        _, rank = ranks(place, total // cap)
        slot = (place * cap + rank).astype(F32)
        slot_ref[...] = jnp.broadcast_to(slot, (128, slot.shape[1])).T

    normed = (norm_rows(cand_ref[...].astype(F32)) * gain_ref[...]).astype(BF16)

    def projected(part):
        return silu(mm(normed, w_ref[:, part * width : (part + 1) * width])).astype(BF16)

    u_ref[...] = projected(0)
    own_v = projected(1).astype(F32)
    prod = projected(2).astype(F32) * projected(3).astype(F32)
    for h in range(width // HDIM):
        cols = slice(h * HDIM, (h + 1) * HDIM)
        score = jnp.sum(prod[:, cols], axis=-1, keepdims=True) * HDIM ** (-0.5)
        self_ref[:, cols] = (silu(score).astype(BF16).astype(F32) * own_v[:, cols]).astype(BF16)
    slot = slot_ref[pl.ds(pl.multiple_of(i * step, step), step), 0:1].astype(jnp.int32)
    pick_ref[...] = one_hot(iota((step, total), 1) == slot)


def attend_kernel(
    cap, arrived_ref, k_ref, v_hbm, out_hbm, v_ref, out_ref, mask_ref, odd_ref, v_sem, out_sem
):
    n_dev = arrived_ref.shape[0]
    heads, depth = k_ref.shape[0], k_ref.shape[1]
    total = n_dev * cap
    pairs = depth // HDIM
    groups = v_sem.shape[0]
    each = heads // groups

    def load(g):
        at = pl.ds(g * each, each)
        return pltpu.make_async_copy(v_hbm.at[at], v_ref.at[at], v_sem.at[g])

    for g in range(groups):
        load(g).start()

    full = (n_dev, cap, 128)
    table = arrived_ref[:, heads * cap : heads * cap + 8, :].astype(F32)[:, 0:1, :]
    own = jnp.where(iota(full, 1) == iota(full, 2), jnp.broadcast_to(table, full), 0.0)
    uid = mm(own.reshape(total, 128).astype(BF16), jnp.ones((128, 128), BF16))
    pair = jnp.floor(uid * 0.5)
    odd_ref[...] = uid - 2.0 * pair
    pair = pair.astype(BF16)
    for p in range(pairs):
        hit = pair == jnp.asarray(1.0 * p, BF16)
        mask_ref[:, p * 128 : (p + 1) * 128] = jnp.where(hit, jnp.ones((), BF16), jnp.zeros((), BF16))

    def spread(x):
        return jnp.concatenate([x * mask_ref[:, p * 128 : (p + 1) * 128] for p in range(pairs)], axis=1)

    def chosen(x):
        return jnp.where(odd_ref[...] > 0.5, x[:, 128:], x[:, :128])

    @pl.loop(0, groups)
    def _(g):
        members = [g * each + t for t in range(each)]
        scores = []
        for h in members:
            rows = pl.ds(pl.multiple_of(h * cap, cap), cap)
            query = arrived_ref[:, rows, :].astype(F32).reshape(total, HDIM).astype(BF16)
            scores.append(mm(spread(query), k_ref[h]))
        weights = [silu(chosen(score) * HDIM ** (-0.5)).astype(BF16) for score in scores]
        load(g).wait()
        for h, weight in zip(members, weights):
            cols = pl.ds(pl.multiple_of(h * HDIM, HDIM), HDIM)
            out_ref[:, cols] = chosen(mm(spread(weight), v_ref[h])).astype(BF16)

    copy = pltpu.make_async_copy(out_ref, out_hbm, out_sem.at[0])
    copy.start()
    copy.wait()


def answer_kernel(back_ref, u_ref, self_ref, pick_ref, out_ref):
    normed = norm_rows(mm(pick_ref[...], back_ref[...]) + self_ref[...].astype(F32))
    out_ref[...] = normed.astype(BF16) * u_ref[...]


def params():
    return pltpu.CompilerParams(vmem_limit_bytes=36 * 1024 * 1024)


def whole(shape):
    return pl.BlockSpec(shape, lambda *_: (0,) * len(shape))


def column(shape, index):
    return pl.BlockSpec(shape, lambda *_: (0, index))


def cost(flops, size):
    return pl.CostEstimate(flops=flops, bytes_accessed=size, transcendentals=0)


def in_hbm(x):
    return pltpu.with_memory_space_constraint(x, pltpu.HBM)


def in_vmem(x):
    return pltpu.with_memory_space_constraint(x, pltpu.VMEM)


def exchange(slots):
    return lax.all_to_all(slots, AXES, split_axis=0, concat_axis=0, tiled=True)


def body(history, hist_len, cand, cand_owner, cand_user, norm_gain, w_proj):
    users, rows, dim = history.shape
    width = w_proj.shape[1] // 4
    heads = width // HDIM
    count = cand.shape[0]
    n_dev = lax.axis_size("grp") * lax.axis_size("enc")
    cap = -(-max(2, 3 * count // (2 * n_dev)) // 8) * 8
    total = n_dev * cap
    parts = 4
    shape = jax.ShapeDtypeStruct
    anywhere = pl.BlockSpec(memory_space=pl.ANY)
    dma = pltpu.SemaphoreType.DMA

    history, cand, w_proj = in_hbm(history), in_hbm(cand), in_hbm(w_proj)
    gain = in_hbm(norm_gain.reshape(1, dim))
    owner = in_hbm(cand_owner.reshape(1, count))
    user = in_hbm(cand_user.reshape(1, count))

    outgoing = pl.pallas_call(
        functools.partial(dispatch_kernel, cap),
        in_specs=[anywhere] * 5,
        out_specs=anywhere,
        out_shape=pltpu.HBM((n_dev, heads * cap + 8, HDIM), BF16),
        scratch_shapes=[
            pltpu.VMEM((count, dim), BF16),
            pltpu.VMEM((1, dim), F32),
            pltpu.VMEM((dim, width), BF16),
            pltpu.VMEM((1, count), jnp.int32),
            pltpu.VMEM((1, count), jnp.int32),
            pltpu.VMEM((n_dev, heads * cap + 8, HDIM), BF16),
            pltpu.VMEM((count, width), BF16),
            pltpu.VMEM((total, count), BF16),
            dma((3,)),
            dma((parts,)),
            dma((1,)),
            dma((1,)),
        ],
        compiler_params=params(),
        cost_estimate=cost(2 * count * width * (dim + total), 4 << 20),
        name="dispatch",
    )(cand, gain, w_proj, owner, user)

    arrived = exchange(outgoing)

    span = 4
    kv_cache, keys, values = pl.pallas_call(
        encode_kernel,
        grid=(users // span,),
        in_specs=[
            pl.BlockSpec(memory_space=pltpu.SMEM),
            pl.BlockSpec((span, rows, dim), lambda i: (i, 0, 0)),
            whole((1, dim)),
            column((dim, width), 1),
            column((dim, width), 3),
        ],
        out_specs=[
            pl.BlockSpec((span, rows, 2 * width), lambda i: (i, 0, 0)),
            pl.BlockSpec((heads, span * HDIM // 2, 2 * rows), lambda i: (0, i, 0)),
            pl.BlockSpec((heads, span * rows // 2, 2 * HDIM), lambda i: (0, i, 0)),
        ],
        out_shape=[
            shape((users, rows, 2 * width), BF16),
            pltpu.VMEM((heads, users * HDIM // 2, 2 * rows), BF16),
            pltpu.HBM((heads, users * rows // 2, 2 * HDIM), BF16),
        ],
        compiler_params=params(),
        cost_estimate=cost(2 * users * rows * dim * 2 * width, 12 << 20),
        name="encode",
    )(in_hbm(hist_len), history, gain, w_proj, w_proj)

    step = count // 2
    gate, own, pick = pl.pallas_call(
        functools.partial(own_kernel, cap),
        grid=(count // step,),
        in_specs=[
            pl.BlockSpec((step, dim), lambda i: (i, 0)),
            whole((1, dim)),
            whole((dim, 4 * width)),
            whole((1, count)),
        ],
        out_specs=[
            pl.BlockSpec((step, width), lambda i: (i, 0)),
            pl.BlockSpec((step, width), lambda i: (i, 0)),
            pl.BlockSpec((step, total), lambda i: (i, 0)),
        ],
        out_shape=[shape((count, width), BF16), shape((count, width), BF16), shape((count, total), BF16)],
        scratch_shapes=[pltpu.VMEM((count, 128), F32)],
        compiler_params=params(),
        cost_estimate=cost(8 * count * dim * width, 6 << 20),
        name="own",
    )(cand, gain, w_proj, owner)

    attended = pl.pallas_call(
        functools.partial(attend_kernel, cap),
        in_specs=[pl.BlockSpec(memory_space=pltpu.VMEM), pl.BlockSpec(memory_space=pltpu.VMEM), anywhere],
        out_specs=anywhere,
        out_shape=pltpu.HBM((total, width), BF16),
        scratch_shapes=[
            pltpu.VMEM((heads, users * rows // 2, 2 * HDIM), BF16),
            pltpu.VMEM((total, width), BF16),
            pltpu.VMEM((total, users * 64), BF16),
            pltpu.VMEM((total, 128), F32),
            dma((heads // 2,)),
            dma((1,)),
        ],
        compiler_params=params(),
        cost_estimate=cost(2 * total * rows * users * width * 2, 6 << 20),
        name="attend",
    )(in_vmem(arrived), in_vmem(keys), in_hbm(values))

    back = exchange(attended.reshape(n_dev, cap, width)).reshape(total, width)

    cand_out = pl.pallas_call(
        answer_kernel,
        in_specs=[pl.BlockSpec(memory_space=pltpu.VMEM)] * 4,
        out_specs=pl.BlockSpec(memory_space=pltpu.VMEM),
        out_shape=shape((count, width), BF16),
        compiler_params=params(),
        cost_estimate=cost(2 * count * total * width, 4 << 20),
        name="answer",
    )(in_vmem(back), gate, own, pick)
    return (kv_cache, cand_out)


def solution(mesh):
    placed = (
        P(AXES, None, None),
        P(AXES),
        P(AXES, None),
        P(AXES, None),
        P(AXES),
        P(),
        P(),
    )
    return jax.shard_map(
        body,
        mesh=mesh,
        in_specs=placed,
        out_specs=(P(AXES, None, None), P(AXES, None)),
        check_vma=False,
    )
```

```python
import functools

import jax
import jax.numpy as jnp
from jax import lax
from jax.experimental import pallas as pl
from jax.experimental.pallas import tpu as pltpu
from jax.sharding import PartitionSpec as P

HDIM = 128
PIECE = 64
F32 = jnp.float32
BF16 = jnp.bfloat16
AXES = ("grp", "enc")
NT = (((1,), (1,)), ((), ()))


def silu(x):
    half = 0.5 * x
    return half + half * jnp.tanh(half)


def norm_rows(values):
    center = values - jnp.mean(values, axis=-1, keepdims=True)
    spread = jnp.mean(center * center, axis=-1, keepdims=True)
    return center * lax.rsqrt(spread + 1e-05)


def mm(a, b):
    return jnp.dot(a, b, preferred_element_type=F32)


def one_hot(hit):
    return jnp.where(hit, 1.0, 0.0).astype(BF16)


def iota(shape, dim):
    return lax.broadcasted_iota(jnp.int32, shape, dim)


def ranks(place, n_dev):
    count = place.shape[1]
    named = iota((n_dev, count), 0) == place
    hot = jnp.where(named, 1.0, 0.0)
    upper = one_hot(iota((128, 128), 0) < iota((128, 128), 1))
    carry, before = jnp.zeros((n_dev, 1), F32), []
    for c in range(0, count, 128):
        block = hot[:, c : c + 128]
        before.append(mm(block.astype(BF16), upper) + carry)
        carry = carry + jnp.sum(block, axis=1, keepdims=True)
    rank = jnp.where(named, jnp.concatenate(before, axis=1), 0.0)
    return named, jnp.sum(rank, axis=0, keepdims=True).astype(jnp.int32)


def dispatch_kernel(
    cap, cand_hbm, gain_hbm, w_hbm, owner_hbm, user_hbm, out_ref,
    cand_ref, gain_ref, wq_ref, owner_ref, user_ref, q_ref, pick_ref, small_sem, cand_sem, w_sem,
):
    n_dev = out_ref.shape[0]
    count, width = q_ref.shape
    heads = width // HDIM
    parts = cand_sem.shape[0]
    step = count // parts

    def block(ref, i):
        return ref.at[pl.ds(i * step, step), :]

    small = [
        pltpu.make_async_copy(owner_hbm, owner_ref, small_sem.at[0]),
        pltpu.make_async_copy(user_hbm, user_ref, small_sem.at[1]),
        pltpu.make_async_copy(gain_hbm, gain_ref, small_sem.at[2]),
    ]
    loads = [pltpu.make_async_copy(block(cand_hbm, i), block(cand_ref, i), cand_sem.at[i]) for i in range(parts)]
    weights = pltpu.make_async_copy(w_hbm.at[:, pl.ds(2 * width, width)], wq_ref, w_sem.at[0])
    for copy in small:
        copy.start()
    loads[0].start()
    weights.start()
    for copy in loads[1:]:
        copy.start()
    for copy in small:
        copy.wait()
    place = owner_ref[...]
    named, rank = ranks(place, n_dev)
    pick_ref[...] = one_hot(iota((n_dev * cap, count), 0) == place * cap + rank)
    users = jnp.where(named, user_ref[...].astype(F32), 0.0).astype(BF16)
    table = lax.dot_general(users, one_hot(iota((128, count), 0) == rank), NT, preferred_element_type=F32)
    out_ref[:, heads * cap :, :] = jnp.broadcast_to(table[:, None, :], (n_dev, 8, 128)).astype(BF16)
    for copy in loads:
        copy.wait()
    weights.wait()
    gain = gain_ref[...]
    for r in range(0, count, 256):
        rows = slice(r, r + 256)
        x = cand_ref[rows, :].astype(F32)
        center = x - jnp.mean(x, axis=-1, keepdims=True)
        scale = lax.rsqrt(jnp.mean(center * center, axis=-1, keepdims=True) + 1e-05)
        q_ref[rows, :] = silu(mm((center * gain).astype(BF16), wq_ref[...]) * scale).astype(BF16)
    sent = mm(pick_ref[...], q_ref[...])
    for h in range(heads):
        part = sent[:, h * HDIM : (h + 1) * HDIM].reshape(n_dev, cap, HDIM)
        out_ref[:, h * cap : (h + 1) * cap, :] = part.astype(BF16)


def encode_kernel(len_ref, hist_ref, gain_ref, wv_ref, wk_ref, out_ref, key_ref, value_ref):
    users, rows, dim = hist_ref.shape
    width = wk_ref.shape[1]
    first = pl.program_id(0) * users
    x = hist_ref[...].reshape(users * rows, dim).astype(F32)
    normed = (norm_rows(x) * gain_ref[...]).astype(BF16)
    keys = silu(mm(normed, wk_ref[...]))
    values = silu(mm(normed, wv_ref[...]))
    row_ids = iota((rows, width), 0)
    for u in range(users):
        live = row_ids < len_ref[first + u] * PIECE
        part = slice(u * rows, (u + 1) * rows)
        side = slice((u % 2) * rows, (u % 2 + 1) * rows)
        pair = slice((u // 2) * HDIM, (u // 2 + 1) * HDIM)
        key = jnp.where(live, keys[part], 0.0)
        value = jnp.where(live, values[part], 0.0).astype(BF16)
        out_ref[u, :, :width] = key.astype(BF16)
        out_ref[u, :, width:] = value
        for h in range(width // HDIM):
            cols = slice(h * HDIM, (h + 1) * HDIM)
            key_ref[h, pair, side] = key[:, cols].T.astype(BF16)
            value_ref[h, pair, side] = value[:, cols]


def own_kernel(cap, cand_ref, gain_ref, w_ref, owner_ref, u_ref, self_ref, pick_ref, slot_ref):
    step, width = u_ref.shape
    total = pick_ref.shape[1]
    i = pl.program_id(0)

    @pl.when(i == 0)
    def _():
        place = owner_ref[...]
        _, rank = ranks(place, total // cap)
        slot = (place * cap + rank).astype(F32)
        slot_ref[...] = jnp.broadcast_to(slot, (128, slot.shape[1])).T

    normed = (norm_rows(cand_ref[...].astype(F32)) * gain_ref[...]).astype(BF16)

    def projected(part):
        return silu(mm(normed, w_ref[:, part * width : (part + 1) * width])).astype(BF16)

    u_ref[...] = projected(0)
    own_v = projected(1).astype(F32)
    prod = projected(2).astype(F32) * projected(3).astype(F32)
    for h in range(width // HDIM):
        cols = slice(h * HDIM, (h + 1) * HDIM)
        score = jnp.sum(prod[:, cols], axis=-1, keepdims=True) * HDIM ** (-0.5)
        self_ref[:, cols] = (silu(score).astype(BF16).astype(F32) * own_v[:, cols]).astype(BF16)
    slot = slot_ref[pl.ds(pl.multiple_of(i * step, step), step), 0:1].astype(jnp.int32)
    pick_ref[...] = one_hot(iota((step, total), 1) == slot)


def attend_kernel(
    cap, arrived_ref, k_ref, v_hbm, out_ref, v_ref, mask_ref, odd_ref, v_sem
):
    n_dev = arrived_ref.shape[0]
    heads, depth = k_ref.shape[0], k_ref.shape[1]
    total = n_dev * cap
    pairs = depth // HDIM
    groups = v_sem.shape[0]
    each = heads // groups

    def load(g):
        at = pl.ds(g * each, each)
        return pltpu.make_async_copy(v_hbm.at[at], v_ref.at[at], v_sem.at[g])

    for g in range(groups):
        load(g).start()

    full = (n_dev, cap, 128)
    table = arrived_ref[:, heads * cap : heads * cap + 8, :].astype(F32)[:, 0:1, :]
    own = jnp.where(iota(full, 1) == iota(full, 2), jnp.broadcast_to(table, full), 0.0)
    uid = mm(own.reshape(total, 128).astype(BF16), jnp.ones((128, 128), BF16))
    pair = jnp.floor(uid * 0.5)
    odd_ref[...] = uid - 2.0 * pair
    pair = pair.astype(BF16)
    for p in range(pairs):
        hit = pair == jnp.asarray(1.0 * p, BF16)
        mask_ref[:, p * 128 : (p + 1) * 128] = jnp.where(hit, jnp.ones((), BF16), jnp.zeros((), BF16))

    def spread(x):
        return jnp.concatenate([x * mask_ref[:, p * 128 : (p + 1) * 128] for p in range(pairs)], axis=1)

    def chosen(x):
        return jnp.where(odd_ref[...] > 0.5, x[:, 128:], x[:, :128])

    @pl.loop(0, groups)
    def _(g):
        members = [g * each + t for t in range(each)]
        scores = []
        for h in members:
            rows = pl.ds(pl.multiple_of(h * cap, cap), cap)
            query = arrived_ref[:, rows, :].astype(F32).reshape(total, HDIM).astype(BF16)
            scores.append(mm(spread(query), k_ref[h]))
        weights = [silu(chosen(score) * HDIM ** (-0.5)).astype(BF16) for score in scores]
        load(g).wait()
        for h, weight in zip(members, weights):
            cols = pl.ds(pl.multiple_of(h * HDIM, HDIM), HDIM)
            out_ref[:, cols] = chosen(mm(spread(weight), v_ref[h])).astype(BF16)


def answer_kernel(back_ref, u_ref, self_ref, pick_ref, out_ref):
    normed = norm_rows(mm(pick_ref[...], back_ref[...]) + self_ref[...].astype(F32))
    out_ref[...] = normed.astype(BF16) * u_ref[...]


def params():
    return pltpu.CompilerParams(vmem_limit_bytes=36 * 1024 * 1024)


def whole(shape):
    return pl.BlockSpec(shape, lambda *_: (0,) * len(shape))


def column(shape, index):
    return pl.BlockSpec(shape, lambda *_: (0, index))


def cost(flops, size):
    return pl.CostEstimate(flops=flops, bytes_accessed=size, transcendentals=0)


def in_hbm(x):
    return pltpu.with_memory_space_constraint(x, pltpu.HBM)


def in_vmem(x):
    return pltpu.with_memory_space_constraint(x, pltpu.VMEM)


def exchange(slots):
    return lax.all_to_all(slots, AXES, split_axis=0, concat_axis=0, tiled=True)


def body(history, hist_len, cand, cand_owner, cand_user, norm_gain, w_proj):
    users, rows, dim = history.shape
    width = w_proj.shape[1] // 4
    heads = width // HDIM
    count = cand.shape[0]
    n_dev = lax.axis_size("grp") * lax.axis_size("enc")
    cap = -(-max(2, 3 * count // (2 * n_dev)) // 8) * 8
    total = n_dev * cap
    parts = 4
    shape = jax.ShapeDtypeStruct
    anywhere = pl.BlockSpec(memory_space=pl.ANY)
    dma = pltpu.SemaphoreType.DMA

    history, cand, w_proj = in_hbm(history), in_hbm(cand), in_hbm(w_proj)
    gain = in_hbm(norm_gain.reshape(1, dim))
    owner = in_hbm(cand_owner.reshape(1, count))
    user = in_hbm(cand_user.reshape(1, count))

    outgoing = pl.pallas_call(
        functools.partial(dispatch_kernel, cap),
        in_specs=[anywhere] * 5,
        out_specs=pl.BlockSpec(memory_space=pltpu.VMEM),
        out_shape=pltpu.VMEM((n_dev, heads * cap + 8, HDIM), BF16),
        scratch_shapes=[
            pltpu.VMEM((count, dim), BF16),
            pltpu.VMEM((1, dim), F32),
            pltpu.VMEM((dim, width), BF16),
            pltpu.VMEM((1, count), jnp.int32),
            pltpu.VMEM((1, count), jnp.int32),
            pltpu.VMEM((count, width), BF16),
            pltpu.VMEM((total, count), BF16),
            dma((3,)),
            dma((parts,)),
            dma((1,)),
        ],
        compiler_params=params(),
        cost_estimate=cost(2 * count * width * (dim + total), 4 << 20),
        name="dispatch",
    )(cand, gain, w_proj, owner, user)

    arrived = exchange(outgoing)

    span = 4
    kv_cache, keys, values = pl.pallas_call(
        encode_kernel,
        grid=(users // span,),
        in_specs=[
            pl.BlockSpec(memory_space=pltpu.SMEM),
            pl.BlockSpec((span, rows, dim), lambda i: (i, 0, 0)),
            whole((1, dim)),
            column((dim, width), 1),
            column((dim, width), 3),
        ],
        out_specs=[
            pl.BlockSpec((span, rows, 2 * width), lambda i: (i, 0, 0)),
            pl.BlockSpec((heads, span * HDIM // 2, 2 * rows), lambda i: (0, i, 0)),
            pl.BlockSpec((heads, span * rows // 2, 2 * HDIM), lambda i: (0, i, 0)),
        ],
        out_shape=[
            shape((users, rows, 2 * width), BF16),
            pltpu.VMEM((heads, users * HDIM // 2, 2 * rows), BF16),
            pltpu.HBM((heads, users * rows // 2, 2 * HDIM), BF16),
        ],
        compiler_params=params(),
        cost_estimate=cost(2 * users * rows * dim * 2 * width, 12 << 20),
        name="encode",
    )(in_hbm(hist_len), history, gain, w_proj, w_proj)

    step = count // 2
    gate, own, pick = pl.pallas_call(
        functools.partial(own_kernel, cap),
        grid=(count // step,),
        in_specs=[
            pl.BlockSpec((step, dim), lambda i: (i, 0)),
            whole((1, dim)),
            whole((dim, 4 * width)),
            whole((1, count)),
        ],
        out_specs=[
            pl.BlockSpec((step, width), lambda i: (i, 0)),
            pl.BlockSpec((step, width), lambda i: (i, 0)),
            pl.BlockSpec((step, total), lambda i: (i, 0)),
        ],
        out_shape=[shape((count, width), BF16), shape((count, width), BF16), shape((count, total), BF16)],
        scratch_shapes=[pltpu.VMEM((count, 128), F32)],
        compiler_params=params(),
        cost_estimate=cost(8 * count * dim * width, 6 << 20),
        name="own",
    )(cand, gain, w_proj, owner)

    attended = pl.pallas_call(
        functools.partial(attend_kernel, cap),
        in_specs=[pl.BlockSpec(memory_space=pltpu.VMEM), pl.BlockSpec(memory_space=pltpu.VMEM), anywhere],
        out_specs=pl.BlockSpec(memory_space=pltpu.VMEM),
        out_shape=pltpu.VMEM((total, width), BF16),
        scratch_shapes=[
            pltpu.VMEM((heads, users * rows // 2, 2 * HDIM), BF16),
            pltpu.VMEM((total, users * 64), BF16),
            pltpu.VMEM((total, 128), F32),
            dma((heads // 2,)),
        ],
        compiler_params=params(),
        cost_estimate=cost(2 * total * rows * users * width * 2, 6 << 20),
        name="attend",
    )(in_vmem(arrived), in_vmem(keys), in_hbm(values))

    back = exchange(attended.reshape(n_dev, cap, width)).reshape(total, width)

    cand_out = pl.pallas_call(
        answer_kernel,
        in_specs=[pl.BlockSpec(memory_space=pltpu.VMEM)] * 4,
        out_specs=pl.BlockSpec(memory_space=pltpu.VMEM),
        out_shape=shape((count, width), BF16),
        compiler_params=params(),
        cost_estimate=cost(2 * count * total * width, 4 << 20),
        name="answer",
    )(in_vmem(back), gate, own, pick)
    return (kv_cache, cand_out)


def solution(mesh):
    placed = (
        P(AXES, None, None),
        P(AXES),
        P(AXES, None),
        P(AXES, None),
        P(AXES),
        P(),
        P(),
    )
    return jax.shard_map(
        body,
        mesh=mesh,
        in_specs=placed,
        out_specs=(P(AXES, None, None), P(AXES, None)),
        check_vma=False,
    )
```

```python
import functools

import jax
import jax.numpy as jnp
from jax import lax
from jax.experimental import pallas as pl
from jax.experimental.pallas import tpu as pltpu
from jax.sharding import PartitionSpec as P

HDIM = 128
PIECE = 64
F32 = jnp.float32
BF16 = jnp.bfloat16
AXES = ("grp", "enc")
NT = (((1,), (1,)), ((), ()))


def silu(x):
    half = 0.5 * x
    return half + half * jnp.tanh(half)


def norm_rows(values):
    center = values - jnp.mean(values, axis=-1, keepdims=True)
    spread = jnp.mean(center * center, axis=-1, keepdims=True)
    return center * lax.rsqrt(spread + 1e-05)


def mm(a, b):
    return jnp.dot(a, b, preferred_element_type=F32)


def one_hot(hit):
    return jnp.where(hit, 1.0, 0.0).astype(BF16)


def iota(shape, dim):
    return lax.broadcasted_iota(jnp.int32, shape, dim)


def ranks(place, n_dev):
    count = place.shape[1]
    named = iota((n_dev, count), 0) == place
    hot = jnp.where(named, 1.0, 0.0)
    upper = one_hot(iota((128, 128), 0) < iota((128, 128), 1))
    carry, before = jnp.zeros((n_dev, 1), F32), []
    for c in range(0, count, 128):
        block = hot[:, c : c + 128]
        before.append(mm(block.astype(BF16), upper) + carry)
        carry = carry + jnp.sum(block, axis=1, keepdims=True)
    rank = jnp.where(named, jnp.concatenate(before, axis=1), 0.0)
    return named, jnp.sum(rank, axis=0, keepdims=True).astype(jnp.int32)


def dispatch_kernel(
    cap, cand_hbm, gain_hbm, w_hbm, owner_hbm, user_hbm, out_hbm,
    cand_ref, gain_ref, wq_ref, owner_ref, user_ref, out_ref, q_ref, pick_ref, small_sem, cand_sem, w_sem, out_sem,
):
    n_dev = out_ref.shape[0]
    count, width = q_ref.shape
    heads = width // HDIM
    parts = cand_sem.shape[0]
    step = count // parts

    def block(ref, i):
        return ref.at[pl.ds(i * step, step), :]

    small = [
        pltpu.make_async_copy(owner_hbm, owner_ref, small_sem.at[0]),
        pltpu.make_async_copy(user_hbm, user_ref, small_sem.at[1]),
        pltpu.make_async_copy(gain_hbm, gain_ref, small_sem.at[2]),
    ]
    loads = [pltpu.make_async_copy(block(cand_hbm, i), block(cand_ref, i), cand_sem.at[i]) for i in range(parts)]
    weights = pltpu.make_async_copy(w_hbm.at[:, pl.ds(2 * width, width)], wq_ref, w_sem.at[0])
    for copy in small:
        copy.start()
    loads[0].start()
    weights.start()
    for copy in loads[1:]:
        copy.start()
    for copy in small:
        copy.wait()
    place = owner_ref[...]
    named, rank = ranks(place, n_dev)
    pick_ref[...] = one_hot(iota((n_dev * cap, count), 0) == place * cap + rank)
    users = jnp.where(named, user_ref[...].astype(F32), 0.0).astype(BF16)
    table = lax.dot_general(users, one_hot(iota((128, count), 0) == rank), NT, preferred_element_type=F32)
    out_ref[:, heads * cap :, :] = jnp.broadcast_to(table[:, None, :], (n_dev, 8, 128)).astype(BF16)
    for copy in loads:
        copy.wait()
    weights.wait()
    gain = gain_ref[...]
    for r in range(0, count, 256):
        rows = slice(r, r + 256)
        x = cand_ref[rows, :].astype(F32)
        center = x - jnp.mean(x, axis=-1, keepdims=True)
        scale = lax.rsqrt(jnp.mean(center * center, axis=-1, keepdims=True) + 1e-05)
        q_ref[rows, :] = silu(mm((center * gain).astype(BF16), wq_ref[...]) * scale).astype(BF16)
    stores = []
    groups = out_sem.shape[0]
    span = n_dev // groups
    for g in range(groups):
        devs = slice(g * span, (g + 1) * span)
        sent = mm(pick_ref[g * span * cap : (g + 1) * span * cap, :], q_ref[...])
        for h in range(heads):
            part = sent[:, h * HDIM : (h + 1) * HDIM].reshape(span, cap, HDIM)
            out_ref[devs, h * cap : (h + 1) * cap, :] = part.astype(BF16)
        at = pl.ds(g * span, span)
        stores.append(pltpu.make_async_copy(out_ref.at[at], out_hbm.at[at], out_sem.at[g]))
        stores[-1].start()
    for copy in stores:
        copy.wait()


def encode_kernel(len_ref, hist_ref, gain_ref, wv_ref, wk_ref, out_ref, near_ref, far_ref, value_ref):
    users, rows, dim = hist_ref.shape
    width = wk_ref.shape[1]
    first = pl.program_id(0) * users
    x = hist_ref[...].reshape(users * rows, dim).astype(F32)
    normed = (norm_rows(x) * gain_ref[...]).astype(BF16)
    keys = silu(mm(normed, wk_ref[...]))
    values = silu(mm(normed, wv_ref[...]))
    row_ids = iota((rows, width), 0)
    for u in range(users):
        live = row_ids < len_ref[first + u] * PIECE
        part = slice(u * rows, (u + 1) * rows)
        side = slice((u % 2) * rows, (u % 2 + 1) * rows)
        pair = slice((u // 2) * HDIM, (u // 2 + 1) * HDIM)
        key = jnp.where(live, keys[part], 0.0)
        value = jnp.where(live, values[part], 0.0).astype(BF16)
        out_ref[u, :, :width] = key.astype(BF16)
        out_ref[u, :, width:] = value
        for h in range(width // HDIM):
            cols = slice(h * HDIM, (h + 1) * HDIM)
            key_ref, at = (near_ref, h) if h < near_ref.shape[0] else (far_ref, h - near_ref.shape[0])
            key_ref[at, pair, side] = key[:, cols].T.astype(BF16)
            value_ref[h, pair, side] = value[:, cols]


def own_kernel(cap, cand_ref, gain_ref, w_ref, owner_ref, u_ref, self_ref, pick_ref, slot_ref):
    step, width = u_ref.shape
    total = pick_ref.shape[1]
    i = pl.program_id(0)

    @pl.when(i == 0)
    def _():
        place = owner_ref[...]
        _, rank = ranks(place, total // cap)
        slot = (place * cap + rank).astype(F32)
        slot_ref[...] = jnp.broadcast_to(slot, (128, slot.shape[1])).T

    normed = (norm_rows(cand_ref[...].astype(F32)) * gain_ref[...]).astype(BF16)

    def projected(part):
        return silu(mm(normed, w_ref[:, part * width : (part + 1) * width])).astype(BF16)

    u_ref[...] = projected(0)
    own_v = projected(1).astype(F32)
    prod = projected(2).astype(F32) * projected(3).astype(F32)
    for h in range(width // HDIM):
        cols = slice(h * HDIM, (h + 1) * HDIM)
        score = jnp.sum(prod[:, cols], axis=-1, keepdims=True) * HDIM ** (-0.5)
        self_ref[:, cols] = (silu(score).astype(BF16).astype(F32) * own_v[:, cols]).astype(BF16)
    slot = slot_ref[pl.ds(pl.multiple_of(i * step, step), step), 0:1].astype(jnp.int32)
    pick_ref[...] = one_hot(iota((step, total), 1) == slot)


def attend_kernel(
    cap, arrived_ref, near_ref, far_hbm, v_hbm, _, out_ref, far_ref, v_ref, mask_ref, odd_ref, far_sem, v_sem
):
    n_dev = arrived_ref.shape[0]
    heads, depth = v_ref.shape[0], v_ref.shape[1]
    total = n_dev * cap
    pairs = depth // HDIM
    groups = v_sem.shape[0]
    each = heads // groups

    def load(g):
        at = pl.ds(g * each, each)
        return pltpu.make_async_copy(v_hbm.at[at], v_ref.at[at], v_sem.at[g])

    far = pltpu.make_async_copy(far_hbm, far_ref, far_sem.at[0])
    load(0).start()
    far.start()
    for g in range(1, groups):
        load(g).start()

    full = (n_dev, cap, 128)
    table = arrived_ref[:, heads * cap : heads * cap + 8, :].astype(F32)[:, 0:1, :]
    own = jnp.where(iota(full, 1) == iota(full, 2), jnp.broadcast_to(table, full), 0.0)
    uid = mm(own.reshape(total, 128).astype(BF16), jnp.ones((128, 128), BF16))
    pair = jnp.floor(uid * 0.5)
    odd_ref[...] = uid - 2.0 * pair
    pair = pair.astype(BF16)
    for p in range(pairs):
        hit = pair == jnp.asarray(1.0 * p, BF16)
        mask_ref[:, p * 128 : (p + 1) * 128] = jnp.where(hit, jnp.ones((), BF16), jnp.zeros((), BF16))

    def spread(x):
        return jnp.concatenate([x * mask_ref[:, p * 128 : (p + 1) * 128] for p in range(pairs)], axis=1)

    def chosen(x):
        return jnp.where(odd_ref[...] > 0.5, x[:, 128:], x[:, :128])

    for g in range(groups):
        members = [g * each + t for t in range(each)]
        if g == groups // 2:
            far.wait()
        scores = []
        for h in members:
            query = arrived_ref[:, h * cap : (h + 1) * cap, :].astype(F32).reshape(total, HDIM).astype(BF16)
            key = near_ref[h] if h < near_ref.shape[0] else far_ref[h - near_ref.shape[0]]
            scores.append(mm(spread(query), key))
        weights = [silu(chosen(score) * HDIM ** (-0.5)).astype(BF16) for score in scores]
        load(g).wait()
        for h, weight in zip(members, weights):
            out_ref[:, h * HDIM : (h + 1) * HDIM] = chosen(mm(spread(weight), v_ref[h])).astype(BF16)


def answer_kernel(back_ref, u_ref, self_ref, pick_ref, out_ref):
    normed = norm_rows(mm(pick_ref[...], back_ref[...]) + self_ref[...].astype(F32))
    out_ref[...] = normed.astype(BF16) * u_ref[...]


def params():
    return pltpu.CompilerParams(vmem_limit_bytes=36 * 1024 * 1024)


def whole(shape):
    return pl.BlockSpec(shape, lambda *_: (0,) * len(shape))


def column(shape, index):
    return pl.BlockSpec(shape, lambda *_: (0, index))


def cost(flops, size):
    return pl.CostEstimate(flops=flops, bytes_accessed=size, transcendentals=0)


def in_hbm(x):
    return pltpu.with_memory_space_constraint(x, pltpu.HBM)


def in_vmem(x):
    return pltpu.with_memory_space_constraint(x, pltpu.VMEM)


def exchange(slots):
    return lax.all_to_all(slots, AXES, split_axis=0, concat_axis=0, tiled=True)


def body(history, hist_len, cand, cand_owner, cand_user, norm_gain, w_proj):
    users, rows, dim = history.shape
    width = w_proj.shape[1] // 4
    heads = width // HDIM
    count = cand.shape[0]
    n_dev = lax.axis_size("grp") * lax.axis_size("enc")
    cap = -(-max(2, 3 * count // (2 * n_dev)) // 8) * 8
    total = n_dev * cap
    parts = 4
    shape = jax.ShapeDtypeStruct
    anywhere = pl.BlockSpec(memory_space=pl.ANY)
    dma = pltpu.SemaphoreType.DMA

    history, cand, w_proj = in_hbm(history), in_hbm(cand), in_hbm(w_proj)
    gain = in_hbm(norm_gain.reshape(1, dim))
    owner = in_hbm(cand_owner.reshape(1, count))
    user = in_hbm(cand_user.reshape(1, count))

    outgoing = pl.pallas_call(
        functools.partial(dispatch_kernel, cap),
        in_specs=[anywhere] * 5,
        out_specs=anywhere,
        out_shape=pltpu.HBM((n_dev, heads * cap + 8, HDIM), BF16),
        scratch_shapes=[
            pltpu.VMEM((count, dim), BF16),
            pltpu.VMEM((1, dim), F32),
            pltpu.VMEM((dim, width), BF16),
            pltpu.VMEM((1, count), jnp.int32),
            pltpu.VMEM((1, count), jnp.int32),
            pltpu.VMEM((n_dev, heads * cap + 8, HDIM), BF16),
            pltpu.VMEM((count, width), BF16),
            pltpu.VMEM((total, count), BF16),
            dma((3,)),
            dma((parts,)),
            dma((1,)),
            dma((2,)),
        ],
        compiler_params=params(),
        cost_estimate=cost(2 * count * width * (dim + total), 4 << 20),
        name="dispatch",
    )(cand, gain, w_proj, owner, user)

    arrived = exchange(outgoing)

    span = 4
    half = heads // 2
    kv_cache, near_keys, far_keys, values = pl.pallas_call(
        encode_kernel,
        grid=(users // span,),
        in_specs=[
            pl.BlockSpec(memory_space=pltpu.SMEM),
            pl.BlockSpec((span, rows, dim), lambda i: (i, 0, 0)),
            whole((1, dim)),
            column((dim, width), 1),
            column((dim, width), 3),
        ],
        out_specs=[
            pl.BlockSpec((span, rows, 2 * width), lambda i: (i, 0, 0)),
            pl.BlockSpec((half, span * HDIM // 2, 2 * rows), lambda i: (0, i, 0)),
            pl.BlockSpec((half, span * HDIM // 2, 2 * rows), lambda i: (0, i, 0)),
            pl.BlockSpec((heads, span * rows // 2, 2 * HDIM), lambda i: (0, i, 0)),
        ],
        out_shape=[
            shape((users, rows, 2 * width), BF16),
            pltpu.VMEM((half, users * HDIM // 2, 2 * rows), BF16),
            pltpu.HBM((half, users * HDIM // 2, 2 * rows), BF16),
            pltpu.HBM((heads, users * rows // 2, 2 * HDIM), BF16),
        ],
        compiler_params=params(),
        cost_estimate=cost(2 * users * rows * dim * 2 * width, 12 << 20),
        name="encode",
    )(in_hbm(hist_len), history, gain, w_proj, w_proj)

    step = count // 2
    gate, own, pick = pl.pallas_call(
        functools.partial(own_kernel, cap),
        grid=(count // step,),
        in_specs=[
            pl.BlockSpec((step, dim), lambda i: (i, 0)),
            whole((1, dim)),
            whole((dim, 4 * width)),
            whole((1, count)),
        ],
        out_specs=[
            pl.BlockSpec((step, width), lambda i: (i, 0)),
            pl.BlockSpec((step, width), lambda i: (i, 0)),
            pl.BlockSpec((step, total), lambda i: (i, 0)),
        ],
        out_shape=[shape((count, width), BF16), shape((count, width), BF16), shape((count, total), BF16)],
        scratch_shapes=[pltpu.VMEM((count, 128), F32)],
        compiler_params=params(),
        cost_estimate=cost(8 * count * dim * width, 6 << 20),
        name="own",
    )(cand, gain, w_proj, owner)

    attended = pl.pallas_call(
        functools.partial(attend_kernel, cap),
        in_specs=[pl.BlockSpec(memory_space=pltpu.VMEM)] * 2 + [anywhere] * 3,
        out_specs=pl.BlockSpec(memory_space=pltpu.VMEM),
        out_shape=pltpu.VMEM((total, width), BF16),
        scratch_shapes=[
            pltpu.VMEM((half, users * HDIM // 2, 2 * rows), BF16),
            pltpu.VMEM((heads, users * rows // 2, 2 * HDIM), BF16),
            pltpu.VMEM((total, users * 64), BF16),
            pltpu.VMEM((total, 128), F32),
            dma((1,)),
            dma((heads // 2,)),
        ],
        compiler_params=params(),
        cost_estimate=cost(2 * total * rows * users * width * 2, 6 << 20),
        name="attend",
    )(in_vmem(arrived), in_vmem(near_keys), in_hbm(far_keys), in_hbm(values), own)

    back = exchange(attended.reshape(n_dev, cap, width)).reshape(total, width)

    cand_out = pl.pallas_call(
        answer_kernel,
        in_specs=[pl.BlockSpec(memory_space=pltpu.VMEM)] * 4,
        out_specs=pl.BlockSpec(memory_space=pltpu.VMEM),
        out_shape=shape((count, width), BF16),
        compiler_params=params(),
        cost_estimate=cost(2 * count * total * width, 4 << 20),
        name="answer",
    )(in_vmem(back), gate, own, pick)
    return (kv_cache, cand_out)


def solution(mesh):
    placed = (
        P(AXES, None, None),
        P(AXES),
        P(AXES, None),
        P(AXES, None),
        P(AXES),
        P(),
        P(),
    )
    return jax.shard_map(
        body,
        mesh=mesh,
        in_specs=placed,
        out_specs=(P(AXES, None, None), P(AXES, None)),
        check_vma=False,
    )
```

```python
import functools

import jax
import jax.numpy as jnp
from jax import lax
from jax.experimental import pallas as pl
from jax.experimental.pallas import tpu as pltpu
from jax.sharding import PartitionSpec as P

HDIM = 128
PIECE = 64
F32 = jnp.float32
BF16 = jnp.bfloat16
AXES = ("grp", "enc")
NT = (((1,), (1,)), ((), ()))


def silu(x):
    half = 0.5 * x
    return half + half * jnp.tanh(half)


def norm_rows(values):
    center = values - jnp.mean(values, axis=-1, keepdims=True)
    spread = jnp.mean(center * center, axis=-1, keepdims=True)
    return center * lax.rsqrt(spread + 1e-05)


def mm(a, b):
    return jnp.dot(a, b, preferred_element_type=F32)


def one_hot(hit):
    return jnp.where(hit, 1.0, 0.0).astype(BF16)


def iota(shape, dim):
    return lax.broadcasted_iota(jnp.int32, shape, dim)


def ranks(place, n_dev):
    count = place.shape[1]
    named = iota((n_dev, count), 0) == place
    hot = jnp.where(named, 1.0, 0.0)
    upper = one_hot(iota((128, 128), 0) < iota((128, 128), 1))
    carry, before = jnp.zeros((n_dev, 1), F32), []
    for c in range(0, count, 128):
        block = hot[:, c : c + 128]
        before.append(mm(block.astype(BF16), upper) + carry)
        carry = carry + jnp.sum(block, axis=1, keepdims=True)
    rank = jnp.where(named, jnp.concatenate(before, axis=1), 0.0)
    return named, jnp.sum(rank, axis=0, keepdims=True).astype(jnp.int32)


def place_of(owner, n_grp, n_enc):
    if n_enc & (n_enc - 1):
        return lax.rem(owner, n_enc) * n_grp + lax.div(owner, n_enc)
    return (owner & (n_enc - 1)) * n_grp + (owner >> (n_enc.bit_length() - 1))


def dispatch_kernel(
    n_grp, n_enc, cap, cand_hbm, gain_hbm, w_hbm, owner_hbm, user_hbm, out_hbm,
    cand_ref, gain_ref, wq_ref, owner_ref, user_ref, out_ref, q_ref, pick_ref, small_sem, cand_sem, w_sem, out_sem,
):
    n_dev = out_ref.shape[0]
    count, width = q_ref.shape
    heads = width // HDIM
    parts = cand_sem.shape[0]
    step = count // parts

    def block(ref, i):
        return ref.at[pl.ds(i * step, step), :]

    small = [
        pltpu.make_async_copy(owner_hbm, owner_ref, small_sem.at[0]),
        pltpu.make_async_copy(user_hbm, user_ref, small_sem.at[1]),
        pltpu.make_async_copy(gain_hbm, gain_ref, small_sem.at[2]),
    ]
    loads = [pltpu.make_async_copy(block(cand_hbm, i), block(cand_ref, i), cand_sem.at[i]) for i in range(parts)]
    weights = pltpu.make_async_copy(w_hbm.at[:, pl.ds(2 * width, width)], wq_ref, w_sem.at[0])
    for copy in small:
        copy.start()
    loads[0].start()
    weights.start()
    for copy in loads[1:]:
        copy.start()
    for copy in small:
        copy.wait()
    place = place_of(owner_ref[...], n_grp, n_enc)
    named, rank = ranks(place, n_dev)
    pick_ref[...] = one_hot(iota((n_dev * cap, count), 0) == place * cap + rank)
    users = jnp.where(named, user_ref[...].astype(F32), 0.0).astype(BF16)
    table = lax.dot_general(users, one_hot(iota((128, count), 0) == rank), NT, preferred_element_type=F32)
    out_ref[:, heads * cap :, :] = jnp.broadcast_to(table[:, None, :], (n_dev, 8, 128)).astype(BF16)
    for copy in loads:
        copy.wait()
    weights.wait()
    gain = gain_ref[...]
    for r in range(0, count, 256):
        rows = slice(r, r + 256)
        x = cand_ref[rows, :].astype(F32)
        center = x - jnp.mean(x, axis=-1, keepdims=True)
        scale = lax.rsqrt(jnp.mean(center * center, axis=-1, keepdims=True) + 1e-05)
        q_ref[rows, :] = silu(mm((center * gain).astype(BF16), wq_ref[...]) * scale).astype(BF16)
    stores = []
    groups = out_sem.shape[0]
    span = n_dev // groups
    for g in range(groups):
        devs = slice(g * span, (g + 1) * span)
        sent = mm(pick_ref[g * span * cap : (g + 1) * span * cap, :], q_ref[...])
        for h in range(heads):
            part = sent[:, h * HDIM : (h + 1) * HDIM].reshape(span, cap, HDIM)
            out_ref[devs, h * cap : (h + 1) * cap, :] = part.astype(BF16)
        at = pl.ds(g * span, span)
        stores.append(pltpu.make_async_copy(out_ref.at[at], out_hbm.at[at], out_sem.at[g]))
        stores[-1].start()
    for copy in stores:
        copy.wait()


def encode_kernel(len_ref, hist_ref, gain_ref, wv_ref, wk_ref, out_ref, near_ref, far_ref, value_ref):
    users, rows, dim = hist_ref.shape
    width = wk_ref.shape[1]
    first = pl.program_id(0) * users
    x = hist_ref[...].reshape(users * rows, dim).astype(F32)
    normed = (norm_rows(x) * gain_ref[...]).astype(BF16)
    keys = silu(mm(normed, wk_ref[...]))
    values = silu(mm(normed, wv_ref[...]))
    row_ids = iota((rows, width), 0)
    for u in range(users):
        live = row_ids < len_ref[first + u] * PIECE
        part = slice(u * rows, (u + 1) * rows)
        side = slice((u % 2) * rows, (u % 2 + 1) * rows)
        pair = slice((u // 2) * HDIM, (u // 2 + 1) * HDIM)
        key = jnp.where(live, keys[part], 0.0)
        value = jnp.where(live, values[part], 0.0).astype(BF16)
        out_ref[u, :, :width] = key.astype(BF16)
        out_ref[u, :, width:] = value
        for h in range(width // HDIM):
            cols = slice(h * HDIM, (h + 1) * HDIM)
            key_ref, at = (near_ref, h) if h < near_ref.shape[0] else (far_ref, h - near_ref.shape[0])
            key_ref[at, pair, side] = key[:, cols].T.astype(BF16)
            value_ref[h, pair, side] = value[:, cols]


def own_kernel(n_grp, n_enc, cap, cand_ref, gain_ref, w_ref, owner_ref, u_ref, self_ref, pick_ref, slot_ref):
    step, width = u_ref.shape
    total = pick_ref.shape[1]
    i = pl.program_id(0)

    @pl.when(i == 0)
    def _():
        place = place_of(owner_ref[...], n_grp, n_enc)
        _, rank = ranks(place, total // cap)
        slot = (place * cap + rank).astype(F32)
        slot_ref[...] = jnp.broadcast_to(slot, (128, slot.shape[1])).T

    normed = (norm_rows(cand_ref[...].astype(F32)) * gain_ref[...]).astype(BF16)

    def projected(part):
        return silu(mm(normed, w_ref[:, part * width : (part + 1) * width])).astype(BF16)

    u_ref[...] = projected(0)
    own_v = projected(1).astype(F32)
    prod = projected(2).astype(F32) * projected(3).astype(F32)
    for h in range(width // HDIM):
        cols = slice(h * HDIM, (h + 1) * HDIM)
        score = jnp.sum(prod[:, cols], axis=-1, keepdims=True) * HDIM ** (-0.5)
        self_ref[:, cols] = (silu(score).astype(BF16).astype(F32) * own_v[:, cols]).astype(BF16)
    slot = slot_ref[pl.ds(pl.multiple_of(i * step, step), step), 0:1].astype(jnp.int32)
    pick_ref[...] = one_hot(iota((step, total), 1) == slot)


def attend_kernel(
    cap, arrived_ref, near_ref, far_hbm, v_hbm, _, out_ref, far_ref, v_ref, mask_ref, odd_ref, far_sem, v_sem
):
    n_dev = arrived_ref.shape[0]
    heads, depth = v_ref.shape[0], v_ref.shape[1]
    total = n_dev * cap
    pairs = depth // HDIM
    groups = v_sem.shape[0]
    each = heads // groups

    def load(g):
        at = pl.ds(g * each, each)
        return pltpu.make_async_copy(v_hbm.at[at], v_ref.at[at], v_sem.at[g])

    far = pltpu.make_async_copy(far_hbm, far_ref, far_sem.at[0])
    load(0).start()
    far.start()
    for g in range(1, groups):
        load(g).start()

    full = (n_dev, cap, 128)
    table = arrived_ref[:, heads * cap : heads * cap + 8, :].astype(F32)[:, 0:1, :]
    own = jnp.where(iota(full, 1) == iota(full, 2), jnp.broadcast_to(table, full), 0.0)
    uid = mm(own.reshape(total, 128).astype(BF16), jnp.ones((128, 128), BF16))
    pair = jnp.floor(uid * 0.5)
    odd_ref[...] = uid - 2.0 * pair
    pair = pair.astype(BF16)
    for p in range(pairs):
        hit = pair == jnp.asarray(1.0 * p, BF16)
        mask_ref[:, p * 128 : (p + 1) * 128] = jnp.where(hit, jnp.ones((), BF16), jnp.zeros((), BF16))

    def spread(x):
        return jnp.concatenate([x * mask_ref[:, p * 128 : (p + 1) * 128] for p in range(pairs)], axis=1)

    def chosen(x):
        return jnp.where(odd_ref[...] > 0.5, x[:, 128:], x[:, :128])

    for g in range(groups):
        members = [g * each + t for t in range(each)]
        scores = []
        for h in members:
            query = arrived_ref[:, h * cap : (h + 1) * cap, :].astype(F32).reshape(total, HDIM).astype(BF16)
            key = near_ref[h] if h < near_ref.shape[0] else far_ref[h - near_ref.shape[0]]
            scores.append(mm(spread(query), key))
        weights = [silu(chosen(score) * HDIM ** (-0.5)).astype(BF16) for score in scores]
        if g == 0:
            load(0).wait()
            far.wait()
            load(1).wait()
        for h, weight in zip(members, weights):
            out_ref[:, h * HDIM : (h + 1) * HDIM] = chosen(mm(spread(weight), v_ref[h])).astype(BF16)


def answer_kernel(back_ref, u_ref, self_ref, pick_ref, out_ref):
    normed = norm_rows(mm(pick_ref[...], back_ref[...]) + self_ref[...].astype(F32))
    out_ref[...] = normed.astype(BF16) * u_ref[...]


def params():
    return pltpu.CompilerParams(vmem_limit_bytes=36 * 1024 * 1024)


def whole(shape):
    return pl.BlockSpec(shape, lambda *_: (0,) * len(shape))


def column(shape, index):
    return pl.BlockSpec(shape, lambda *_: (0, index))


def cost(flops, size):
    return pl.CostEstimate(flops=flops, bytes_accessed=size, transcendentals=0)


def in_hbm(x):
    return pltpu.with_memory_space_constraint(x, pltpu.HBM)


def in_vmem(x):
    return pltpu.with_memory_space_constraint(x, pltpu.VMEM)


def exchange(slots):
    return lax.all_to_all(slots, ("enc", "grp"), split_axis=0, concat_axis=0, tiled=True)


def body(history, hist_len, cand, cand_owner, cand_user, norm_gain, w_proj):
    users, rows, dim = history.shape
    width = w_proj.shape[1] // 4
    heads = width // HDIM
    count = cand.shape[0]
    n_grp, n_enc = lax.axis_size("grp"), lax.axis_size("enc")
    n_dev = n_grp * n_enc
    cap = -(-max(2, 3 * count // (2 * n_dev)) // 8) * 8
    total = n_dev * cap
    parts = 4
    shape = jax.ShapeDtypeStruct
    anywhere = pl.BlockSpec(memory_space=pl.ANY)
    dma = pltpu.SemaphoreType.DMA

    history, cand, w_proj = in_hbm(history), in_hbm(cand), in_hbm(w_proj)
    gain = in_hbm(norm_gain.reshape(1, dim))
    owner = in_hbm(cand_owner.reshape(1, count))
    user = in_hbm(cand_user.reshape(1, count))

    outgoing = pl.pallas_call(
        functools.partial(dispatch_kernel, n_grp, n_enc, cap),
        in_specs=[anywhere] * 5,
        out_specs=anywhere,
        out_shape=pltpu.HBM((n_dev, heads * cap + 8, HDIM), BF16),
        scratch_shapes=[
            pltpu.VMEM((count, dim), BF16),
            pltpu.VMEM((1, dim), F32),
            pltpu.VMEM((dim, width), BF16),
            pltpu.VMEM((1, count), jnp.int32),
            pltpu.VMEM((1, count), jnp.int32),
            pltpu.VMEM((n_dev, heads * cap + 8, HDIM), BF16),
            pltpu.VMEM((count, width), BF16),
            pltpu.VMEM((total, count), BF16),
            dma((3,)),
            dma((parts,)),
            dma((1,)),
            dma((2,)),
        ],
        compiler_params=params(),
        cost_estimate=cost(2 * count * width * (dim + total), 4 << 20),
        name="dispatch",
    )(cand, gain, w_proj, owner, user)

    arrived = exchange(outgoing)

    span = 4
    half = heads // 2
    kv_cache, near_keys, far_keys, values = pl.pallas_call(
        encode_kernel,
        grid=(users // span,),
        in_specs=[
            pl.BlockSpec(memory_space=pltpu.SMEM),
            pl.BlockSpec((span, rows, dim), lambda i: (i, 0, 0)),
            whole((1, dim)),
            column((dim, width), 1),
            column((dim, width), 3),
        ],
        out_specs=[
            pl.BlockSpec((span, rows, 2 * width), lambda i: (i, 0, 0)),
            pl.BlockSpec((half, span * HDIM // 2, 2 * rows), lambda i: (0, i, 0)),
            pl.BlockSpec((half, span * HDIM // 2, 2 * rows), lambda i: (0, i, 0)),
            pl.BlockSpec((heads, span * rows // 2, 2 * HDIM), lambda i: (0, i, 0)),
        ],
        out_shape=[
            shape((users, rows, 2 * width), BF16),
            pltpu.VMEM((half, users * HDIM // 2, 2 * rows), BF16),
            pltpu.HBM((half, users * HDIM // 2, 2 * rows), BF16),
            pltpu.HBM((heads, users * rows // 2, 2 * HDIM), BF16),
        ],
        compiler_params=params(),
        cost_estimate=cost(2 * users * rows * dim * 2 * width, 12 << 20),
        name="encode",
    )(in_hbm(hist_len), history, gain, w_proj, w_proj)

    step = count // 2
    gate, own, pick = pl.pallas_call(
        functools.partial(own_kernel, n_grp, n_enc, cap),
        grid=(count // step,),
        in_specs=[
            pl.BlockSpec((step, dim), lambda i: (i, 0)),
            whole((1, dim)),
            whole((dim, 4 * width)),
            whole((1, count)),
        ],
        out_specs=[
            pl.BlockSpec((step, width), lambda i: (i, 0)),
            pl.BlockSpec((step, width), lambda i: (i, 0)),
            pl.BlockSpec((step, total), lambda i: (i, 0)),
        ],
        out_shape=[shape((count, width), BF16), shape((count, width), BF16), shape((count, total), BF16)],
        scratch_shapes=[pltpu.VMEM((count, 128), F32)],
        compiler_params=params(),
        cost_estimate=cost(8 * count * dim * width, 6 << 20),
        name="own",
    )(cand, gain, w_proj, owner)

    attended = pl.pallas_call(
        functools.partial(attend_kernel, cap),
        in_specs=[pl.BlockSpec(memory_space=pltpu.VMEM)] * 2 + [anywhere] * 3,
        out_specs=pl.BlockSpec(memory_space=pltpu.VMEM),
        out_shape=pltpu.VMEM((total, width), BF16),
        scratch_shapes=[
            pltpu.VMEM((half, users * HDIM // 2, 2 * rows), BF16),
            pltpu.VMEM((heads, users * rows // 2, 2 * HDIM), BF16),
            pltpu.VMEM((total, users * 64), BF16),
            pltpu.VMEM((total, 128), F32),
            dma((1,)),
            dma((heads // 2,)),
        ],
        compiler_params=params(),
        cost_estimate=cost(2 * total * rows * users * width * 2, 6 << 20),
        name="attend",
    )(in_vmem(arrived), in_vmem(near_keys), in_hbm(far_keys), in_hbm(values), own)

    back = exchange(attended.reshape(n_dev, cap, width)).reshape(total, width)

    cand_out = pl.pallas_call(
        answer_kernel,
        in_specs=[pl.BlockSpec(memory_space=pltpu.VMEM)] * 4,
        out_specs=pl.BlockSpec(memory_space=pltpu.VMEM),
        out_shape=shape((count, width), BF16),
        compiler_params=params(),
        cost_estimate=cost(2 * count * total * width, 4 << 20),
        name="answer",
    )(in_vmem(back), gate, own, pick)
    return (kv_cache, cand_out)


def solution(mesh):
    placed = (
        P(AXES, None, None),
        P(AXES),
        P(AXES, None),
        P(AXES, None),
        P(AXES),
        P(),
        P(),
    )
    return jax.shard_map(
        body,
        mesh=mesh,
        in_specs=placed,
        out_specs=(P(AXES, None, None), P(AXES, None)),
        check_vma=False,
    )
```

```python
import functools

import jax
import jax.numpy as jnp
from jax import lax
from jax.experimental import pallas as pl
from jax.experimental.pallas import tpu as pltpu
from jax.sharding import PartitionSpec as P

HDIM = 128
PIECE = 64
F32 = jnp.float32
BF16 = jnp.bfloat16
AXES = ("grp", "enc")
NT = (((1,), (1,)), ((), ()))


def silu(x):
    half = 0.5 * x
    return half + half * jnp.tanh(half)


def norm_rows(values):
    center = values - jnp.mean(values, axis=-1, keepdims=True)
    spread = jnp.mean(center * center, axis=-1, keepdims=True)
    return center * lax.rsqrt(spread + 1e-05)


def mm(a, b):
    return jnp.dot(a, b, preferred_element_type=F32)


def one_hot(hit):
    return jnp.where(hit, 1.0, 0.0).astype(BF16)


def iota(shape, dim):
    return lax.broadcasted_iota(jnp.int32, shape, dim)


def ranks(place, n_dev):
    count = place.shape[1]
    named = iota((n_dev, count), 0) == place
    hot = jnp.where(named, 1.0, 0.0)
    upper = one_hot(iota((128, 128), 0) < iota((128, 128), 1))
    carry, before = jnp.zeros((n_dev, 1), F32), []
    for c in range(0, count, 128):
        block = hot[:, c : c + 128]
        before.append(mm(block.astype(BF16), upper) + carry)
        carry = carry + jnp.sum(block, axis=1, keepdims=True)
    rank = jnp.where(named, jnp.concatenate(before, axis=1), 0.0)
    return named, jnp.sum(rank, axis=0, keepdims=True).astype(jnp.int32)


def place_of(owner, n_grp, n_enc):
    if n_enc & (n_enc - 1):
        return lax.rem(owner, n_enc) * n_grp + lax.div(owner, n_enc)
    return (owner & (n_enc - 1)) * n_grp + (owner >> (n_enc.bit_length() - 1))


def dispatch_kernel(
    n_grp, n_enc, cap, cand_hbm, gain_hbm, w_hbm, owner_hbm, user_hbm, out_hbm,
    cand_ref, gain_ref, wq_ref, owner_ref, user_ref, out_ref, q_ref, pick_ref, small_sem, cand_sem, w_sem, out_sem,
):
    n_dev = out_ref.shape[0]
    count, width = q_ref.shape
    heads = width // HDIM
    parts = cand_sem.shape[0]
    step = count // parts

    def block(ref, i):
        return ref.at[pl.ds(i * step, step), :]

    small = [
        pltpu.make_async_copy(owner_hbm, owner_ref, small_sem.at[0]),
        pltpu.make_async_copy(user_hbm, user_ref, small_sem.at[1]),
        pltpu.make_async_copy(gain_hbm, gain_ref, small_sem.at[2]),
    ]
    loads = [pltpu.make_async_copy(block(cand_hbm, i), block(cand_ref, i), cand_sem.at[i]) for i in range(parts)]
    weights = pltpu.make_async_copy(w_hbm.at[:, pl.ds(2 * width, width)], wq_ref, w_sem.at[0])
    for copy in small:
        copy.start()
    loads[0].start()
    weights.start()
    for copy in loads[1:]:
        copy.start()
    for copy in small:
        copy.wait()
    place = place_of(owner_ref[...], n_grp, n_enc)
    named, rank = ranks(place, n_dev)
    pick_ref[...] = one_hot(iota((n_dev * cap, count), 0) == place * cap + rank)
    users = jnp.where(named, user_ref[...].astype(F32), 0.0).astype(BF16)
    table = lax.dot_general(users, one_hot(iota((128, count), 0) == rank), NT, preferred_element_type=F32)
    out_ref[:, heads * cap // 8, :, :] = jnp.broadcast_to(table[:, None, :], (n_dev, 8, 128)).astype(BF16)
    for copy in loads:
        copy.wait()
    weights.wait()
    gain = gain_ref[...]
    for r in range(0, count, 256):
        rows = slice(r, r + 256)
        x = cand_ref[rows, :].astype(F32)
        center = x - jnp.mean(x, axis=-1, keepdims=True)
        scale = lax.rsqrt(jnp.mean(center * center, axis=-1, keepdims=True) + 1e-05)
        q_ref[rows, :] = silu(mm((center * gain).astype(BF16), wq_ref[...]) * scale).astype(BF16)
    stores = []
    groups = out_sem.shape[0]
    span = n_dev // groups
    for g in range(groups):
        devs = slice(g * span, (g + 1) * span)
        sent = mm(pick_ref[g * span * cap : (g + 1) * span * cap, :], q_ref[...])
        for h in range(heads):
            part = sent[:, h * HDIM : (h + 1) * HDIM].reshape(span, cap // 8, 8, HDIM)
            out_ref[devs, h * cap // 8 : (h + 1) * cap // 8, :, :] = part.astype(BF16)
        at = pl.ds(g * span, span)
        stores.append(pltpu.make_async_copy(out_ref.at[at], out_hbm.at[at], out_sem.at[g]))
        stores[-1].start()
    for copy in stores:
        copy.wait()


def encode_kernel(len_ref, hist_ref, gain_ref, wv_ref, wk_ref, out_ref, near_ref, far_ref, value_ref):
    users, rows, dim = hist_ref.shape
    width = wk_ref.shape[1]
    first = pl.program_id(0) * users
    x = hist_ref[...].reshape(users * rows, dim).astype(F32)
    normed = (norm_rows(x) * gain_ref[...]).astype(BF16)
    keys = silu(mm(normed, wk_ref[...]))
    values = silu(mm(normed, wv_ref[...]))
    row_ids = iota((rows, width), 0)
    for u in range(users):
        live = row_ids < len_ref[first + u] * PIECE
        part = slice(u * rows, (u + 1) * rows)
        side = slice((u % 2) * rows, (u % 2 + 1) * rows)
        pair = slice((u // 2) * HDIM, (u // 2 + 1) * HDIM)
        key = jnp.where(live, keys[part], 0.0)
        value = jnp.where(live, values[part], 0.0).astype(BF16)
        out_ref[u, :, :width] = key.astype(BF16)
        out_ref[u, :, width:] = value
        for h in range(width // HDIM):
            cols = slice(h * HDIM, (h + 1) * HDIM)
            key_ref, at = (near_ref, h) if h < near_ref.shape[0] else (far_ref, h - near_ref.shape[0])
            key_ref[at, pair, side] = key[:, cols].T.astype(BF16)
            value_ref[h, pair, side] = value[:, cols]


def own_kernel(n_grp, n_enc, cap, cand_ref, gain_ref, w_ref, owner_ref, u_ref, self_ref, pick_ref, slot_ref):
    step, width = u_ref.shape
    total = pick_ref.shape[1]
    i = pl.program_id(0)

    @pl.when(i == 0)
    def _():
        place = place_of(owner_ref[...], n_grp, n_enc)
        _, rank = ranks(place, total // cap)
        slot = (place * cap + rank).astype(F32)
        slot_ref[...] = jnp.broadcast_to(slot, (128, slot.shape[1])).T

    normed = (norm_rows(cand_ref[...].astype(F32)) * gain_ref[...]).astype(BF16)

    def projected(part):
        return silu(mm(normed, w_ref[:, part * width : (part + 1) * width])).astype(BF16)

    u_ref[...] = projected(0)
    own_v = projected(1).astype(F32)
    prod = projected(2).astype(F32) * projected(3).astype(F32)
    for h in range(width // HDIM):
        cols = slice(h * HDIM, (h + 1) * HDIM)
        score = jnp.sum(prod[:, cols], axis=-1, keepdims=True) * HDIM ** (-0.5)
        self_ref[:, cols] = (silu(score).astype(BF16).astype(F32) * own_v[:, cols]).astype(BF16)
    slot = slot_ref[pl.ds(pl.multiple_of(i * step, step), step), 0:1].astype(jnp.int32)
    pick_ref[...] = one_hot(iota((step, total), 1) == slot)


def attend_kernel(
    cap, arrived_ref, near_ref, far_hbm, v_hbm, _, out_ref, far_ref, v_ref, mask_ref, odd_ref, far_sem, v_sem
):
    n_dev = arrived_ref.shape[0]
    heads, depth = v_ref.shape[0], v_ref.shape[1]
    total = n_dev * cap
    pairs = depth // HDIM
    groups = v_sem.shape[0]
    each = heads // groups

    def load(g):
        at = pl.ds(g * each, each)
        return pltpu.make_async_copy(v_hbm.at[at], v_ref.at[at], v_sem.at[g])

    far = pltpu.make_async_copy(far_hbm, far_ref, far_sem.at[0])
    load(0).start()
    far.start()
    for g in range(1, groups):
        load(g).start()

    full = (n_dev, cap, 128)
    table = arrived_ref[:, heads * cap // 8, :, :].astype(F32)[:, 0:1, :]
    own = jnp.where(iota(full, 1) == iota(full, 2), jnp.broadcast_to(table, full), 0.0)
    uid = mm(own.reshape(total, 128).astype(BF16), jnp.ones((128, 128), BF16))
    pair = jnp.floor(uid * 0.5)
    odd_ref[...] = uid - 2.0 * pair
    pair = pair.astype(BF16)
    for p in range(pairs):
        hit = pair == jnp.asarray(1.0 * p, BF16)
        mask_ref[:, p * 128 : (p + 1) * 128] = jnp.where(hit, jnp.ones((), BF16), jnp.zeros((), BF16))

    def spread(x):
        return jnp.concatenate([x * mask_ref[:, p * 128 : (p + 1) * 128] for p in range(pairs)], axis=1)

    def chosen(x):
        return jnp.where(odd_ref[...] > 0.5, x[:, 128:], x[:, :128])

    for g in range(groups):
        members = [g * each + t for t in range(each)]
        if g == groups // 2:
            far.wait()
        scores = []
        for h in members:
            query = arrived_ref[:, h * cap // 8 : (h + 1) * cap // 8, :, :].astype(F32)
            query = query.reshape(total, HDIM).astype(BF16)
            key = near_ref[h] if h < near_ref.shape[0] else far_ref[h - near_ref.shape[0]]
            scores.append(mm(spread(query), key))
        weights = [silu(chosen(score) * HDIM ** (-0.5)).astype(BF16) for score in scores]
        load(g).wait()
        for h, weight in zip(members, weights):
            out_ref[:, h * HDIM : (h + 1) * HDIM] = chosen(mm(spread(weight), v_ref[h])).astype(BF16)


def answer_kernel(back_ref, u_ref, self_ref, pick_ref, out_ref):
    normed = norm_rows(mm(pick_ref[...], back_ref[...]) + self_ref[...].astype(F32))
    out_ref[...] = normed.astype(BF16) * u_ref[...]


def params():
    return pltpu.CompilerParams(vmem_limit_bytes=36 * 1024 * 1024)


def whole(shape):
    return pl.BlockSpec(shape, lambda *_: (0,) * len(shape))


def column(shape, index):
    return pl.BlockSpec(shape, lambda *_: (0, index))


def cost(flops, size):
    return pl.CostEstimate(flops=flops, bytes_accessed=size, transcendentals=0)


def in_hbm(x):
    return pltpu.with_memory_space_constraint(x, pltpu.HBM)


def in_vmem(x):
    return pltpu.with_memory_space_constraint(x, pltpu.VMEM)


def exchange(slots):
    return lax.all_to_all(slots, ("enc", "grp"), split_axis=0, concat_axis=0, tiled=True)


def body(history, hist_len, cand, cand_owner, cand_user, norm_gain, w_proj):
    users, rows, dim = history.shape
    width = w_proj.shape[1] // 4
    heads = width // HDIM
    count = cand.shape[0]
    n_grp, n_enc = lax.axis_size("grp"), lax.axis_size("enc")
    n_dev = n_grp * n_enc
    cap = -(-max(2, 3 * count // (2 * n_dev)) // 8) * 8
    total = n_dev * cap
    parts = 4
    shape = jax.ShapeDtypeStruct
    anywhere = pl.BlockSpec(memory_space=pl.ANY)
    dma = pltpu.SemaphoreType.DMA

    history, cand, w_proj = in_hbm(history), in_hbm(cand), in_hbm(w_proj)
    gain = in_hbm(norm_gain.reshape(1, dim))
    owner = in_hbm(cand_owner.reshape(1, count))
    user = in_hbm(cand_user.reshape(1, count))

    outgoing = pl.pallas_call(
        functools.partial(dispatch_kernel, n_grp, n_enc, cap),
        in_specs=[anywhere] * 5,
        out_specs=anywhere,
        out_shape=pltpu.HBM((n_dev, heads * cap // 8 + 1, 8, HDIM), BF16),
        scratch_shapes=[
            pltpu.VMEM((count, dim), BF16),
            pltpu.VMEM((1, dim), F32),
            pltpu.VMEM((dim, width), BF16),
            pltpu.VMEM((1, count), jnp.int32),
            pltpu.VMEM((1, count), jnp.int32),
            pltpu.VMEM((n_dev, heads * cap // 8 + 1, 8, HDIM), BF16),
            pltpu.VMEM((count, width), BF16),
            pltpu.VMEM((total, count), BF16),
            dma((3,)),
            dma((parts,)),
            dma((1,)),
            dma((2,)),
        ],
        compiler_params=params(),
        cost_estimate=cost(2 * count * width * (dim + total), 4 << 20),
        name="dispatch",
    )(cand, gain, w_proj, owner, user)

    arrived = exchange(outgoing)

    span = 4
    half = heads // 2
    kv_cache, near_keys, far_keys, values = pl.pallas_call(
        encode_kernel,
        grid=(users // span,),
        in_specs=[
            pl.BlockSpec(memory_space=pltpu.SMEM),
            pl.BlockSpec((span, rows, dim), lambda i: (i, 0, 0)),
            whole((1, dim)),
            column((dim, width), 1),
            column((dim, width), 3),
        ],
        out_specs=[
            pl.BlockSpec((span, rows, 2 * width), lambda i: (i, 0, 0)),
            pl.BlockSpec((half, span * HDIM // 2, 2 * rows), lambda i: (0, i, 0)),
            pl.BlockSpec((half, span * HDIM // 2, 2 * rows), lambda i: (0, i, 0)),
            pl.BlockSpec((heads, span * rows // 2, 2 * HDIM), lambda i: (0, i, 0)),
        ],
        out_shape=[
            shape((users, rows, 2 * width), BF16),
            pltpu.VMEM((half, users * HDIM // 2, 2 * rows), BF16),
            pltpu.HBM((half, users * HDIM // 2, 2 * rows), BF16),
            pltpu.HBM((heads, users * rows // 2, 2 * HDIM), BF16),
        ],
        compiler_params=params(),
        cost_estimate=cost(2 * users * rows * dim * 2 * width, 12 << 20),
        name="encode",
    )(in_hbm(hist_len), history, gain, w_proj, w_proj)

    step = count // 2
    gate, own, pick = pl.pallas_call(
        functools.partial(own_kernel, n_grp, n_enc, cap),
        grid=(count // step,),
        in_specs=[
            pl.BlockSpec((step, dim), lambda i: (i, 0)),
            whole((1, dim)),
            whole((dim, 4 * width)),
            whole((1, count)),
        ],
        out_specs=[
            pl.BlockSpec((step, width), lambda i: (i, 0)),
            pl.BlockSpec((step, width), lambda i: (i, 0)),
            pl.BlockSpec((step, total), lambda i: (i, 0)),
        ],
        out_shape=[shape((count, width), BF16), shape((count, width), BF16), shape((count, total), BF16)],
        scratch_shapes=[pltpu.VMEM((count, 128), F32)],
        compiler_params=params(),
        cost_estimate=cost(8 * count * dim * width, 6 << 20),
        name="own",
    )(cand, gain, w_proj, owner)

    attended = pl.pallas_call(
        functools.partial(attend_kernel, cap),
        in_specs=[pl.BlockSpec(memory_space=pltpu.VMEM)] * 2 + [anywhere] * 3,
        out_specs=pl.BlockSpec(memory_space=pltpu.VMEM),
        out_shape=pltpu.VMEM((total, width), BF16),
        scratch_shapes=[
            pltpu.VMEM((half, users * HDIM // 2, 2 * rows), BF16),
            pltpu.VMEM((heads, users * rows // 2, 2 * HDIM), BF16),
            pltpu.VMEM((total, users * 64), BF16),
            pltpu.VMEM((total, 128), F32),
            dma((1,)),
            dma((heads // 2,)),
        ],
        compiler_params=params(),
        cost_estimate=cost(2 * total * rows * users * width * 2, 6 << 20),
        name="attend",
    )(in_vmem(arrived), in_vmem(near_keys), in_hbm(far_keys), in_hbm(values), own)

    back = exchange(attended.reshape(n_dev, cap, width)).reshape(total, width)

    cand_out = pl.pallas_call(
        answer_kernel,
        in_specs=[pl.BlockSpec(memory_space=pltpu.VMEM)] * 4,
        out_specs=pl.BlockSpec(memory_space=pltpu.VMEM),
        out_shape=shape((count, width), BF16),
        compiler_params=params(),
        cost_estimate=cost(2 * count * total * width, 4 << 20),
        name="answer",
    )(in_vmem(back), gate, own, pick)
    return (kv_cache, cand_out)


def solution(mesh):
    placed = (
        P(AXES, None, None),
        P(AXES),
        P(AXES, None),
        P(AXES, None),
        P(AXES),
        P(),
        P(),
    )
    return jax.shard_map(
        body,
        mesh=mesh,
        in_specs=placed,
        out_specs=(P(AXES, None, None), P(AXES, None)),
        check_vma=False,
    )
```

```python
import functools

import jax
import jax.numpy as jnp
from jax import lax
from jax.experimental import pallas as pl
from jax.experimental.pallas import tpu as pltpu
from jax.sharding import PartitionSpec as P

HDIM = 128
PIECE = 64
F32 = jnp.float32
BF16 = jnp.bfloat16
AXES = ("grp", "enc")
NT = (((1,), (1,)), ((), ()))


def silu(x):
    half = 0.5 * x
    return half + half * jnp.tanh(half)


def norm_rows(values):
    center = values - jnp.mean(values, axis=-1, keepdims=True)
    spread = jnp.mean(center * center, axis=-1, keepdims=True)
    return center * lax.rsqrt(spread + 1e-05)


def mm(a, b):
    return jnp.dot(a, b, preferred_element_type=F32)


def one_hot(hit):
    return jnp.where(hit, 1.0, 0.0).astype(BF16)


def iota(shape, dim):
    return lax.broadcasted_iota(jnp.int32, shape, dim)


def ranks(place, n_dev):
    count = place.shape[1]
    named = iota((n_dev, count), 0) == place
    hot = jnp.where(named, 1.0, 0.0)
    upper = one_hot(iota((128, 128), 0) < iota((128, 128), 1))
    carry, before = jnp.zeros((n_dev, 1), F32), []
    for c in range(0, count, 128):
        block = hot[:, c : c + 128]
        before.append(mm(block.astype(BF16), upper) + carry)
        carry = carry + jnp.sum(block, axis=1, keepdims=True)
    rank = jnp.where(named, jnp.concatenate(before, axis=1), 0.0)
    return named, jnp.sum(rank, axis=0, keepdims=True).astype(jnp.int32)


def place_of(owner, n_grp, n_enc):
    if n_enc & (n_enc - 1):
        return lax.rem(owner, n_enc) * n_grp + lax.div(owner, n_enc)
    return (owner & (n_enc - 1)) * n_grp + (owner >> (n_enc.bit_length() - 1))


def dispatch_kernel(
    n_grp, n_enc, cap, cand_hbm, gain_hbm, w_hbm, owner_hbm, user_hbm, out_hbm,
    cand_ref, gain_ref, wq_ref, owner_ref, user_ref, out_ref, q_ref, pick_ref, small_sem, cand_sem, w_sem, out_sem,
):
    n_dev = out_ref.shape[0]
    count, width = q_ref.shape
    heads = width // HDIM
    parts = cand_sem.shape[0]
    step = count // parts

    def block(ref, i):
        return ref.at[pl.ds(i * step, step), :]

    small = [
        pltpu.make_async_copy(owner_hbm, owner_ref, small_sem.at[0]),
        pltpu.make_async_copy(user_hbm, user_ref, small_sem.at[1]),
        pltpu.make_async_copy(gain_hbm, gain_ref, small_sem.at[2]),
    ]
    loads = [pltpu.make_async_copy(block(cand_hbm, i), block(cand_ref, i), cand_sem.at[i]) for i in range(parts)]
    weights = pltpu.make_async_copy(w_hbm.at[:, pl.ds(2 * width, width)], wq_ref, w_sem.at[0])
    for copy in small:
        copy.start()
    loads[0].start()
    weights.start()
    for copy in loads[1:]:
        copy.start()
    for copy in small:
        copy.wait()
    place = place_of(owner_ref[...], n_grp, n_enc)
    named, rank = ranks(place, n_dev)
    pick_ref[...] = one_hot(iota((n_dev * cap, count), 0) == place * cap + rank)
    users = jnp.where(named, user_ref[...].astype(F32), 0.0).astype(BF16)
    table = lax.dot_general(users, one_hot(iota((128, count), 0) == rank), NT, preferred_element_type=F32)
    out_ref[:, heads * cap // 8, :, :] = jnp.broadcast_to(table[:, None, :], (n_dev, 8, 128)).astype(BF16)
    for copy in loads:
        copy.wait()
    weights.wait()
    gain = gain_ref[...]
    for r in range(0, count, 256):
        rows = slice(r, r + 256)
        x = cand_ref[rows, :].astype(F32)
        center = x - jnp.mean(x, axis=-1, keepdims=True)
        scale = lax.rsqrt(jnp.mean(center * center, axis=-1, keepdims=True) + 1e-05)
        q_ref[rows, :] = silu(mm((center * gain).astype(BF16), wq_ref[...]) * scale).astype(BF16)
    stores = []
    groups = out_sem.shape[0]
    span = n_dev // groups
    for g in range(groups):
        devs = slice(g * span, (g + 1) * span)
        sent = mm(pick_ref[g * span * cap : (g + 1) * span * cap, :], q_ref[...])
        for h in range(heads):
            part = sent[:, h * HDIM : (h + 1) * HDIM].reshape(span, cap // 8, 8, HDIM)
            out_ref[devs, h * cap // 8 : (h + 1) * cap // 8, :, :] = part.astype(BF16)
        at = pl.ds(g * span, span)
        stores.append(pltpu.make_async_copy(out_ref.at[at], out_hbm.at[at], out_sem.at[g]))
        stores[-1].start()
    for copy in stores:
        copy.wait()


def encode_kernel(len_ref, hist_ref, gain_ref, wv_ref, wk_ref, out_ref, near_ref, far_ref, value_ref):
    users, rows, dim = hist_ref.shape
    width = wk_ref.shape[1]
    first = pl.program_id(0) * users
    x = hist_ref[...].reshape(users * rows, dim).astype(F32)
    normed = (norm_rows(x) * gain_ref[...]).astype(BF16)
    keys = silu(mm(normed, wk_ref[...]))
    values = silu(mm(normed, wv_ref[...]))
    row_ids = iota((rows, width), 0)
    for u in range(users):
        live = row_ids < len_ref[first + u] * PIECE
        part = slice(u * rows, (u + 1) * rows)
        side = slice((u % 2) * rows, (u % 2 + 1) * rows)
        pair = slice((u // 2) * HDIM, (u // 2 + 1) * HDIM)
        key = jnp.where(live, keys[part], 0.0)
        value = jnp.where(live, values[part], 0.0).astype(BF16)
        out_ref[u, :, :width] = key.astype(BF16)
        out_ref[u, :, width:] = value
        for h in range(width // HDIM):
            cols = slice(h * HDIM, (h + 1) * HDIM)
            key_ref, at = (near_ref, h) if h < near_ref.shape[0] else (far_ref, h - near_ref.shape[0])
            key_ref[at, pair, side] = key[:, cols].T.astype(BF16)
            value_ref[h, pair, side] = value[:, cols]


def own_kernel(n_grp, n_enc, cap, cand_ref, gain_ref, w_ref, owner_ref, u_ref, self_ref, pick_ref, slot_ref):
    step, width = u_ref.shape
    total = pick_ref.shape[1]
    i = pl.program_id(0)

    @pl.when(i == 0)
    def _():
        place = place_of(owner_ref[...], n_grp, n_enc)
        _, rank = ranks(place, total // cap)
        slot = (place * cap + rank).astype(F32)
        slot_ref[...] = jnp.broadcast_to(slot, (128, slot.shape[1])).T

    normed = (norm_rows(cand_ref[...].astype(F32)) * gain_ref[...]).astype(BF16)

    def projected(part):
        return silu(mm(normed, w_ref[:, part * width : (part + 1) * width])).astype(BF16)

    u_ref[...] = projected(0)
    own_v = projected(1).astype(F32)
    prod = projected(2).astype(F32) * projected(3).astype(F32)
    for h in range(width // HDIM):
        cols = slice(h * HDIM, (h + 1) * HDIM)
        score = jnp.sum(prod[:, cols], axis=-1, keepdims=True) * HDIM ** (-0.5)
        self_ref[:, cols] = (silu(score).astype(BF16).astype(F32) * own_v[:, cols]).astype(BF16)
    slot = slot_ref[pl.ds(pl.multiple_of(i * step, step), step), 0:1].astype(jnp.int32)
    pick_ref[...] = one_hot(iota((step, total), 1) == slot)


def attend_kernel(
    cap, arrived_ref, near_ref, far_hbm, v_hbm, _, out_ref, far_ref, v_ref, mask_ref, odd_ref, far_sem, v_sem
):
    n_dev = arrived_ref.shape[0]
    heads, depth = v_ref.shape[0], v_ref.shape[1]
    total = n_dev * cap
    pairs = depth // HDIM
    groups = v_sem.shape[0]
    each = heads // groups

    def load(g):
        at = pl.ds(g * each, each)
        return pltpu.make_async_copy(v_hbm.at[at], v_ref.at[at], v_sem.at[g])

    far = pltpu.make_async_copy(far_hbm, far_ref, far_sem.at[0])
    far.start()
    for g in range(groups):
        load(g).start()

    full = (n_dev, cap, 128)
    table = arrived_ref[:, heads * cap // 8, :, :].astype(F32)[:, 0:1, :]
    own = jnp.where(iota(full, 1) == iota(full, 2), jnp.broadcast_to(table, full), 0.0)
    uid = mm(own.reshape(total, 128).astype(BF16), jnp.ones((128, 128), BF16))
    pair = jnp.floor(uid * 0.5)
    odd_ref[...] = uid - 2.0 * pair
    pair = pair.astype(BF16)
    for p in range(pairs):
        hit = pair == jnp.asarray(1.0 * p, BF16)
        mask_ref[:, p * 128 : (p + 1) * 128] = jnp.where(hit, jnp.ones((), BF16), jnp.zeros((), BF16))

    def spread(x):
        return jnp.concatenate([x * mask_ref[:, p * 128 : (p + 1) * 128] for p in range(pairs)], axis=1)

    def chosen(x):
        return jnp.where(odd_ref[...] > 0.5, x[:, 128:], x[:, :128])

    weights = []
    for h in range(heads):
        if h == near_ref.shape[0]:
            far.wait()
        query = arrived_ref[:, h * cap // 8 : (h + 1) * cap // 8, :, :].astype(F32)
        query = query.reshape(total, HDIM).astype(BF16)
        key = near_ref[h] if h < near_ref.shape[0] else far_ref[h - near_ref.shape[0]]
        weights.append(silu(chosen(mm(spread(query), key)) * HDIM ** (-0.5)).astype(BF16))
    for g in range(groups):
        load(g).wait()
    for h, weight in enumerate(weights):
        out_ref[:, h * HDIM : (h + 1) * HDIM] = chosen(mm(spread(weight), v_ref[h])).astype(BF16)


def answer_kernel(back_ref, u_ref, self_ref, pick_ref, out_ref):
    normed = norm_rows(mm(pick_ref[...], back_ref[...]) + self_ref[...].astype(F32))
    out_ref[...] = normed.astype(BF16) * u_ref[...]


def params():
    return pltpu.CompilerParams(vmem_limit_bytes=36 * 1024 * 1024)


def whole(shape):
    return pl.BlockSpec(shape, lambda *_: (0,) * len(shape))


def column(shape, index):
    return pl.BlockSpec(shape, lambda *_: (0, index))


def cost(flops, size):
    return pl.CostEstimate(flops=flops, bytes_accessed=size, transcendentals=0)


def in_hbm(x):
    return pltpu.with_memory_space_constraint(x, pltpu.HBM)


def in_vmem(x):
    return pltpu.with_memory_space_constraint(x, pltpu.VMEM)


def exchange(slots):
    return lax.all_to_all(slots, ("enc", "grp"), split_axis=0, concat_axis=0, tiled=True)


def body(history, hist_len, cand, cand_owner, cand_user, norm_gain, w_proj):
    users, rows, dim = history.shape
    width = w_proj.shape[1] // 4
    heads = width // HDIM
    count = cand.shape[0]
    n_grp, n_enc = lax.axis_size("grp"), lax.axis_size("enc")
    n_dev = n_grp * n_enc
    cap = -(-max(2, 3 * count // (2 * n_dev)) // 8) * 8
    total = n_dev * cap
    parts = 4
    shape = jax.ShapeDtypeStruct
    anywhere = pl.BlockSpec(memory_space=pl.ANY)
    dma = pltpu.SemaphoreType.DMA

    history, cand, w_proj = in_hbm(history), in_hbm(cand), in_hbm(w_proj)
    gain = in_hbm(norm_gain.reshape(1, dim))
    owner = in_hbm(cand_owner.reshape(1, count))
    user = in_hbm(cand_user.reshape(1, count))

    outgoing = pl.pallas_call(
        functools.partial(dispatch_kernel, n_grp, n_enc, cap),
        in_specs=[anywhere] * 5,
        out_specs=anywhere,
        out_shape=pltpu.HBM((n_dev, heads * cap // 8 + 1, 8, HDIM), BF16),
        scratch_shapes=[
            pltpu.VMEM((count, dim), BF16),
            pltpu.VMEM((1, dim), F32),
            pltpu.VMEM((dim, width), BF16),
            pltpu.VMEM((1, count), jnp.int32),
            pltpu.VMEM((1, count), jnp.int32),
            pltpu.VMEM((n_dev, heads * cap // 8 + 1, 8, HDIM), BF16),
            pltpu.VMEM((count, width), BF16),
            pltpu.VMEM((total, count), BF16),
            dma((3,)),
            dma((parts,)),
            dma((1,)),
            dma((2,)),
        ],
        compiler_params=params(),
        cost_estimate=cost(2 * count * width * (dim + total), 4 << 20),
        name="dispatch",
    )(cand, gain, w_proj, owner, user)

    arrived = exchange(outgoing)

    span = 4
    half = heads // 2
    kv_cache, near_keys, far_keys, values = pl.pallas_call(
        encode_kernel,
        grid=(users // span,),
        in_specs=[
            pl.BlockSpec(memory_space=pltpu.SMEM),
            pl.BlockSpec((span, rows, dim), lambda i: (i, 0, 0)),
            whole((1, dim)),
            column((dim, width), 1),
            column((dim, width), 3),
        ],
        out_specs=[
            pl.BlockSpec((span, rows, 2 * width), lambda i: (i, 0, 0)),
            pl.BlockSpec((half, span * HDIM // 2, 2 * rows), lambda i: (0, i, 0)),
            pl.BlockSpec((half, span * HDIM // 2, 2 * rows), lambda i: (0, i, 0)),
            pl.BlockSpec((heads, span * rows // 2, 2 * HDIM), lambda i: (0, i, 0)),
        ],
        out_shape=[
            shape((users, rows, 2 * width), BF16),
            pltpu.VMEM((half, users * HDIM // 2, 2 * rows), BF16),
            pltpu.HBM((half, users * HDIM // 2, 2 * rows), BF16),
            pltpu.HBM((heads, users * rows // 2, 2 * HDIM), BF16),
        ],
        compiler_params=params(),
        cost_estimate=cost(2 * users * rows * dim * 2 * width, 12 << 20),
        name="encode",
    )(in_hbm(hist_len), history, gain, w_proj, w_proj)

    step = count // 2
    gate, own, pick = pl.pallas_call(
        functools.partial(own_kernel, n_grp, n_enc, cap),
        grid=(count // step,),
        in_specs=[
            pl.BlockSpec((step, dim), lambda i: (i, 0)),
            whole((1, dim)),
            whole((dim, 4 * width)),
            whole((1, count)),
        ],
        out_specs=[
            pl.BlockSpec((step, width), lambda i: (i, 0)),
            pl.BlockSpec((step, width), lambda i: (i, 0)),
            pl.BlockSpec((step, total), lambda i: (i, 0)),
        ],
        out_shape=[shape((count, width), BF16), shape((count, width), BF16), shape((count, total), BF16)],
        scratch_shapes=[pltpu.VMEM((count, 128), F32)],
        compiler_params=params(),
        cost_estimate=cost(8 * count * dim * width, 6 << 20),
        name="own",
    )(cand, gain, w_proj, owner)

    attended = pl.pallas_call(
        functools.partial(attend_kernel, cap),
        in_specs=[pl.BlockSpec(memory_space=pltpu.VMEM)] * 2 + [anywhere] * 3,
        out_specs=pl.BlockSpec(memory_space=pltpu.VMEM),
        out_shape=pltpu.VMEM((total, width), BF16),
        scratch_shapes=[
            pltpu.VMEM((half, users * HDIM // 2, 2 * rows), BF16),
            pltpu.VMEM((heads, users * rows // 2, 2 * HDIM), BF16),
            pltpu.VMEM((total, users * 64), BF16),
            pltpu.VMEM((total, 128), F32),
            dma((1,)),
            dma((heads // 2,)),
        ],
        compiler_params=params(),
        cost_estimate=cost(2 * total * rows * users * width * 2, 6 << 20),
        name="attend",
    )(in_vmem(arrived), in_vmem(near_keys), in_hbm(far_keys), in_hbm(values), own)

    back = exchange(attended.reshape(n_dev, cap, width)).reshape(total, width)

    cand_out = pl.pallas_call(
        answer_kernel,
        in_specs=[pl.BlockSpec(memory_space=pltpu.VMEM)] * 4,
        out_specs=pl.BlockSpec(memory_space=pltpu.VMEM),
        out_shape=shape((count, width), BF16),
        compiler_params=params(),
        cost_estimate=cost(2 * count * total * width, 4 << 20),
        name="answer",
    )(in_vmem(back), gate, own, pick)
    return (kv_cache, cand_out)


def solution(mesh):
    placed = (
        P(AXES, None, None),
        P(AXES),
        P(AXES, None),
        P(AXES, None),
        P(AXES),
        P(),
        P(),
    )
    return jax.shard_map(
        body,
        mesh=mesh,
        in_specs=placed,
        out_specs=(P(AXES, None, None), P(AXES, None)),
        check_vma=False,
    )
```
